256 devices in a mesh: neg: 32 (over x_hi, z, core), dp: 8 (over y, x_lo).
Axes of the slice: x: 4 (x_hi: 2, x_lo: 2; x = x_hi * 2 + x_lo), y: 4, z: 8, core: 2. Of those that a mesh axis runs over, the one named last changes fastest.
Arguments:
- observations: bfloat16 [8, 10240, 256], P('dp', 'neg'), may hold values from -6 to 6
- actions: bfloat16 [8, 10240, 16], P('dp', 'neg'), may hold values from -12 to 12
- replay_index: int32 [8, 8192], P('dp', 'neg'), may hold values from 0 to 255
- future_offset: int32 [8, 8192], P('dp', 'neg'), may hold values from 1 to 64
- sa_obs: bfloat16 [256, 1024], replicated, may hold values from -0.375 to 0.375
- sa_act: bfloat16 [16, 1024], replicated, may hold values from -1.5 to 1.5
- sa_mid: bfloat16 [1024, 1024], replicated, may hold values from -0.1875 to 0.1875
- sa_out: bfloat16 [1024, 256], replicated, may hold values from -0.1875 to 0.1875
- goal_obs: bfloat16 [256, 1024], replicated, may hold values from -0.375 to 0.375
- goal_mid: bfloat16 [1024, 1024], replicated, may hold values from -0.1875 to 0.1875
- goal_out: bfloat16 [1024, 256], replicated, may hold values from -0.1875 to 0.1875
Outputs:
- row_loss: float32 [8, 8192], P('dp', 'neg')
- sa_obs_grad: float32 [256, 1024], P(None, ('neg', 'dp'))
- sa_act_grad: float32 [16, 1024], P(None, ('neg', 'dp'))
- sa_mid_grad: float32 [1024, 1024], P(('neg', 'dp'))
- sa_out_grad: float32 [1024, 256], P(('neg', 'dp'))
- goal_obs_grad: float32 [256, 1024], P(None, ('neg', 'dp'))
- goal_mid_grad: float32 [1024, 1024], P(('neg', 'dp'))
- goal_out_grad: float32 [1024, 256], P(('neg', 'dp'))
The draws below stay inside these ranges and needn't reach their ends.
Inputs may be any that keep to these rules, and one draw needn't show every extreme that they name: `replay_index`: a row of the device's own slab, so that the future row stays inside it.
All inputs are finite; a program needn't handle non-finite values.
Results may differ from the reference program's by a relative error of at most 0.012.
Values may be sent and summed in bfloat16 or wider, within the bound.
No kernel may reach another device: no remote copies, remote signals or barrier semaphores. Data moves between devices by JAX's collectives and lax.ppermute only.
A program may use at most 128 MiB of HBM per device.

```python
import math
import jax
import jax.numpy as jnp
from jax import lax

OBS = 256
ACT = 16
HIDDEN_SIZE = 1024
EMBED = 256
ROWS = 256
HORIZON = 64
SLAB = 320
GROUP_ROWS = 8192
N_NEG = 32
N_DP = 8


def touch_ends(array, own_key, smallest, high):
    spot = [jax.random.randint(jax.random.fold_in(own_key, axis), (), 0, length) for axis, length in enumerate(array.shape)]
    longest = array.shape.index(max(array.shape))
    next_to = spot[:longest] + [(spot[longest] + 1) % array.shape[longest]] + spot[longest + 1:]
    return array.at[tuple(spot)].set(smallest).at[tuple(next_to)].set(high)


def block_levels(key, dims, split, least, top_value):
    level, own = 1.0, jax.random.fold_in(key, 6)
    for position, parts in split:
        heights = jnp.exp(jax.random.uniform(jax.random.fold_in(own, position), (parts,), jnp.float32, least / len(split), top_value / len(split)))
        level = level * jnp.repeat(heights, dims[position] // parts).reshape([-1 if axis == position else 1 for axis in range(len(dims))])
    return level


def normal_values(own_key, shape, scale, reach, shards=(), held_as=jnp.bfloat16):
    entries = scale * jax.random.normal(own_key, shape, jnp.float32)
    if shards:
        entries = entries * block_levels(own_key, shape, shards, -0.22, 0.18)
    return jnp.clip(entries, -reach, reach).astype(held_as)


def setup_inputs(seed: int = 0) -> dict:
    splits = jax.random.split(jax.random.key(seed), 12)
    observations = normal_values(splits[0], (N_DP, N_NEG * SLAB, OBS), 1.0, 6.0, ((0, 8), (1, 32)))
    actions = normal_values(splits[1], (N_DP, N_NEG * SLAB, ACT), 2.0, 12.0, ((0, 8), (1, 32)))
    replay_index = touch_ends(jax.random.randint(splits[2], (N_DP, GROUP_ROWS), 0, ROWS), jax.random.fold_in(splits[2], 1), 0, ROWS - 1).astype(jnp.int32)
    future_offset = touch_ends(jax.random.randint(splits[3], (N_DP, GROUP_ROWS), 1, HORIZON + 1), jax.random.fold_in(splits[3], 1), 1, HORIZON).astype(jnp.int32)
    sa_obs = normal_values(splits[4], (OBS, HIDDEN_SIZE), OBS ** -0.5, 0.375)
    sa_act = normal_values(splits[5], (ACT, HIDDEN_SIZE), ACT ** -0.5, 1.5)
    sa_mid = normal_values(splits[6], (HIDDEN_SIZE, HIDDEN_SIZE), HIDDEN_SIZE ** -0.5, 0.1875)
    sa_out = normal_values(splits[7], (HIDDEN_SIZE, EMBED), HIDDEN_SIZE ** -0.5, 0.1875)
    goal_obs = normal_values(splits[8], (OBS, HIDDEN_SIZE), OBS ** -0.5, 0.375)
    goal_mid = normal_values(splits[9], (HIDDEN_SIZE, HIDDEN_SIZE), HIDDEN_SIZE ** -0.5, 0.1875)
    goal_out = normal_values(splits[10], (HIDDEN_SIZE, EMBED), HIDDEN_SIZE ** -0.5, 0.1875)
    return {"observations": observations, "actions": actions, "replay_index": replay_index, "future_offset": future_offset, "sa_obs": sa_obs, "sa_act": sa_act, "sa_mid": sa_mid, "sa_out": sa_out, "goal_obs": goal_obs, "goal_mid": goal_mid, "goal_out": goal_out}


NORM_EPS = 1e-05
UNIT_EPS = 1e-06

def swish_grad(normed):
    sigma = jax.nn.sigmoid(normed)
    return sigma * (1.0 + normed * (1.0 - sigma))

def normalize(values):
    center = values - lax.optimization_barrier(jnp.mean(values, axis=-1, keepdims=True))
    factor = lax.rsqrt(lax.optimization_barrier(jnp.mean(center * center, axis=-1, keepdims=True)) + NORM_EPS)
    return (center * factor, factor)

def norm_back(grad, normed, factor):
    return factor * (grad - lax.optimization_barrier(jnp.mean(grad, axis=-1, keepdims=True)) - normed * lax.optimization_barrier(jnp.mean(grad * normed, axis=-1, keepdims=True)))

def encode(inputs, extra, w_first, w_extra, w_mid, w_last):
    first = jnp.dot(inputs, w_first, preferred_element_type=jnp.float32)
    if extra is not None:
        first = first + jnp.dot(extra, w_extra, preferred_element_type=jnp.float32)
    normed_one, factor_one = normalize(first)
    hidden_one = jax.nn.silu(normed_one).astype(jnp.bfloat16)
    second = jnp.dot(hidden_one, w_mid, preferred_element_type=jnp.float32)
    normed_two, factor_two = normalize(second)
    hidden_two = jax.nn.silu(normed_two).astype(jnp.bfloat16)
    embed = jnp.dot(hidden_two, w_last, preferred_element_type=jnp.float32)
    width = embed.shape[-1]
    inverse = lax.rsqrt(lax.optimization_barrier(jnp.mean(embed * embed, axis=-1, keepdims=True)) + UNIT_EPS)
    unit = embed * inverse * width ** (-0.5)
    saved = (normed_one, factor_one, hidden_one, normed_two, factor_two, hidden_two, embed, inverse)
    return (unit, saved)

def backward(grad_unit, inputs, extra, saved, w_mid, w_last):
    normed_one, factor_one, hidden_one, normed_two, factor_two, hidden_two, embed, inverse = saved
    width = embed.shape[-1]
    along = lax.optimization_barrier(jnp.mean(grad_unit * embed, axis=-1, keepdims=True))
    grad_embed = (width ** (-0.5) * inverse * (grad_unit - embed * inverse * inverse * along)).astype(jnp.bfloat16)
    grad_last = jnp.dot(hidden_two.T, grad_embed, preferred_element_type=jnp.float32)
    back_two = jnp.dot(grad_embed, w_last.T, preferred_element_type=jnp.float32) * swish_grad(normed_two)
    pre_two = norm_back(back_two, normed_two, factor_two).astype(jnp.bfloat16)
    grad_mid = jnp.dot(hidden_one.T, pre_two, preferred_element_type=jnp.float32)
    back_one = jnp.dot(pre_two, w_mid.T, preferred_element_type=jnp.float32) * swish_grad(normed_one)
    pre_one = norm_back(back_one, normed_one, factor_one).astype(jnp.bfloat16)
    grad_first = jnp.dot(inputs.T, pre_one, preferred_element_type=jnp.float32)
    if extra is None:
        return (grad_first, grad_mid, grad_last)
    grad_extra = jnp.dot(extra.T, pre_one, preferred_element_type=jnp.float32)
    return (grad_first, grad_extra, grad_mid, grad_last)

def pick_rows(blocks, rows):
    picked = jnp.take_along_axis(blocks, rows[:, :, None], axis=1)
    return picked.reshape(N_NEG * ROWS, blocks.shape[-1])

def reference(observations, actions, replay_index, future_offset, sa_obs, sa_act, sa_mid, sa_out, goal_obs, goal_mid, goal_out):
    logit_scale = 3.0 * math.sqrt(EMBED)
    grad_coef = logit_scale / (2.0 * N_DP)
    losses = []
    totals = None
    for group in range(N_DP):
        obs_blocks = observations[group].reshape(N_NEG, SLAB, OBS)
        act_blocks = actions[group].reshape(N_NEG, SLAB, ACT)
        replay = replay_index[group].reshape(N_NEG, ROWS).astype(jnp.int32)
        future = (replay + future_offset[group].reshape(N_NEG, ROWS)).astype(jnp.int32)
        state_rows = pick_rows(obs_blocks, replay)
        action_rows = pick_rows(act_blocks, replay)
        goal_rows = pick_rows(obs_blocks, future)
        unit_q, saved_q = encode(state_rows, action_rows, sa_obs, sa_act, sa_mid, sa_out)
        unit_t, saved_t = encode(goal_rows, None, goal_obs, None, goal_mid, goal_out)
        queries = unit_q.astype(jnp.bfloat16)
        targets = unit_t.astype(jnp.bfloat16)
        scores = logit_scale * jnp.dot(queries, targets.T, preferred_element_type=jnp.float32)
        expo = jnp.exp(scores)
        rowsum = lax.optimization_barrier(jnp.sum(expo, axis=1))
        colsum = lax.optimization_barrier(jnp.sum(expo, axis=0))
        positive = logit_scale * lax.optimization_barrier(jnp.sum(queries.astype(jnp.float32) * targets.astype(jnp.float32), axis=-1))
        losses.append(0.5 * (jnp.log(rowsum) - positive + jnp.log(colsum) - positive))
        mixing = (expo / rowsum[:, None] + expo / colsum[None, :]).astype(jnp.bfloat16)
        query_grad = grad_coef * (jnp.dot(mixing, targets, preferred_element_type=jnp.float32) - 2.0 * targets.astype(jnp.float32))
        target_grad = grad_coef * (jnp.dot(mixing.T, queries, preferred_element_type=jnp.float32) - 2.0 * queries.astype(jnp.float32))
        grads = backward(query_grad, state_rows, action_rows, saved_q, sa_mid, sa_out) + backward(target_grad, goal_rows, None, saved_t, goal_mid, goal_out)
        if totals is None:
            totals = grads
        else:
            totals = tuple((left + right for left, right in zip(totals, grads)))
    row_loss = jnp.stack(losses, axis=0)
    return (row_loss, totals[0], totals[1], totals[2], totals[3], totals[4], totals[5], totals[6])
```

```python
import functools
import math

import jax
import jax.numpy as jnp
import numpy as np
from jax import lax
from jax.experimental import pallas as pl
from jax.experimental.pallas import tpu as pltpu
from jax.sharding import Mesh
from jax.sharding import PartitionSpec as P

NORM_EPS = 1e-05
UNIT_EPS = 1e-06
ROWS = 256
CHIP = 512
HID = 1024
EMB = 256
WIDE = 384
COLS = HID + EMB + WIDE
LANES = 128
BF = jnp.bfloat16
F32 = jnp.float32
VMEM = pl.BlockSpec(memory_space=pltpu.VMEM)
SMEM = pl.BlockSpec(memory_space=pltpu.SMEM)
ANY = pl.BlockSpec(memory_space=pl.ANY)
PARAMS = pltpu.CompilerParams(vmem_limit_bytes=50 * 1024 * 1024)


def shape(dims, dtype):
    return jax.ShapeDtypeStruct(dims, dtype)


def dot_nn(a, b):
    return lax.dot_general(a, b, (((1,), (0,)), ((), ())), preferred_element_type=F32)


def dot_nt(a, b):
    return lax.dot_general(a, b, (((1,), (1,)), ((), ())), preferred_element_type=F32)


def dot_tn(a, b):
    return lax.dot_general(a, b, (((0,), (0,)), ((), ())), preferred_element_type=F32)


def sigmoid(v):
    return 0.5 + 0.5 * jnp.tanh(0.5 * v)


def call(kernel, outs, in_specs, scratch=(), cost=None):
    specs = [VMEM] * len(outs)
    return pl.pallas_call(
        kernel,
        out_shape=outs,
        in_specs=in_specs,
        out_specs=specs,
        scratch_shapes=list(scratch),
        compiler_params=PARAMS,
        cost_estimate=cost,
    )


def pick_kernel(place, replay, offset, obs, act, keep, send):
    role = place[2]
    index = replay[...]
    ahead = index + offset[...]
    count = obs.shape[0]
    spot = lax.broadcasted_iota(jnp.int32, (count, ROWS), 0)
    for out, rows in (
        (keep, jnp.where(role == 0, index, ahead)),
        (send, jnp.where(role == 0, ahead, index)),
    ):
        hot = jnp.where(spot == rows, 1.0, 0.0).astype(BF)
        out[:, :EMB] = dot_tn(hot, obs[...]).astype(BF)
        extra = dot_tn(hot, act[...])
        pad = jnp.zeros((ROWS, LANES - extra.shape[1]), F32)
        out[:, EMB:] = jnp.concatenate([extra, pad], axis=1).astype(BF)


def by_role(role, pairs, sems):
    for k in range(2):

        @pl.when(role == k)
        def _():
            for n, (sources, target) in enumerate(pairs):
                if sources[k] is not None:
                    pltpu.make_async_copy(sources[k], target, sems.at[n]).start()


def wait_role(role, pairs, sems):
    for k in range(2):

        @pl.when(role == k)
        def _():
            for n, (sources, target) in enumerate(pairs):
                if sources[k] is not None:
                    pltpu.make_async_copy(sources[k], target, sems.at[n]).wait()


def forward_kernel(
    place, keep, recv, sa_obs, sa_act, sa_mid, sa_out, goal_obs, goal_mid, goal_out,
    x, n1, f1, n2, f2, embed, inv, unit,
    w_first, w_mid, w_out, sems,
):
    role = place[2]
    acts = sa_act.shape[0]
    w_first[EMB:, :] = jnp.zeros((WIDE - EMB, HID), BF)
    pairs = [
        ((sa_obs, goal_obs), w_first.at[pl.ds(0, EMB)]),
        ((sa_act, None), w_first.at[pl.ds(EMB, acts)]),
        ((sa_mid, goal_mid), w_mid),
        ((sa_out, goal_out), w_out),
    ]
    by_role(role, pairs, sems)
    own = pl.multiple_of(role * ROWS, ROWS)
    other = pl.multiple_of((1 - role) * ROWS, ROWS)
    x[pl.ds(own, ROWS), :] = keep[...]
    x[pl.ds(other, ROWS), :] = recv[...]
    wait_role(role, pairs, sems)
    for start in range(0, CHIP, LANES):
        rows = pl.ds(start, LANES)

        def norm(values, normed, factor):
            center = values - jnp.mean(values, axis=-1, keepdims=True)
            scale = lax.rsqrt(jnp.mean(center * center, axis=-1, keepdims=True) + NORM_EPS)
            v = center * scale
            normed[rows, :] = v
            factor[rows, :] = scale
            return (v * sigmoid(v)).astype(BF)

        h1 = norm(dot_nn(x[rows, :], w_first[...]), n1, f1)
        h2 = norm(dot_nn(h1, w_mid[...]), n2, f2)
        e = dot_nn(h2, w_out[...])
        scale = lax.rsqrt(jnp.mean(e * e, axis=-1, keepdims=True) + UNIT_EPS)
        embed[rows, :] = e
        inv[rows, :] = scale
        unit[rows, :] = (e * scale * EMB ** (-0.5)).astype(BF)


def to_lanes(values):
    return jnp.sum(values.T, axis=0, keepdims=True)


def score_kernel(n_blocks, first, last, factor, *refs):
    refs = list(refs)
    ours, theirs = refs[:2]
    blocks = refs[2 : 2 + n_blocks]
    refs = refs[2 + n_blocks :]
    if not first:
        old_sum, old_total = refs[:2]
        refs = refs[2:]
    expo, part, total = refs[:3]
    for start in range(0, 2 * CHIP, ROWS):
        source = ours if start < CHIP else theirs
        q = source[pl.ds(start % CHIP, ROWS), :]
        rows = pl.ds(start, ROWS)
        acc = None if first else old_total[rows, :]
        sums = None if first else old_sum[rows, :]
        at = 0
        for block in blocks:
            t = block[...]
            width = t.shape[0]
            e = jnp.exp2(dot_nt(q, t) * factor)
            for lane in range(0, width, LANES):
                piece = e[:, lane : lane + LANES]
                sums = piece if sums is None else sums + piece
            e16 = e.astype(BF)
            expo[rows, at : at + width] = e16
            add = dot_nn(e16, t)
            acc = add if acc is None else acc + add
            at += width
        total[rows, :] = acc
        if last:
            for k in range(ROWS // LANES):
                line = start // LANES + k
                part[line : line + 1, :] = to_lanes(sums[k * LANES : (k + 1) * LANES, :])
        else:
            part[rows, :] = sums


def scores(ours, theirs, blocks, prev, last, factor):
    width = sum(b.shape[0] for b in blocks)
    outs = [
        shape((2 * CHIP, width), BF),
        shape((8, LANES) if last else (2 * CHIP, LANES), F32),
        shape((2 * CHIP, EMB), F32),
    ]
    args = [ours, theirs, *blocks] + list(prev or ())
    kernel = functools.partial(score_kernel, len(blocks), prev is None, last, factor)
    cost = pl.CostEstimate(
        flops=4 * 2 * CHIP * width * EMB,
        bytes_accessed=2 * 2 * CHIP * width + 4 * 2 * CHIP * EMB,
        transcendentals=2 * CHIP * width,
    )
    return call(kernel, outs, [VMEM] * len(args), cost=cost)(*args)


def mix_kernel(n_z, logit, place, sums, total, ours, *refs):
    n_exp = n_z // 2 + 1
    expos = refs[:n_exp]
    blocks = refs[n_exp : n_exp + n_z + 1]
    own, send, loss = refs[n_exp + n_z + 1 : n_exp + n_z + 4]
    lines, scaled = refs[n_exp + n_z + 4 :]
    xh, z, role = place[0], place[1], place[2]

    def full(x_at, z_at, side):
        mine = sums[(x_at * n_z + z_at) * 2 + side]
        partner = sums[((1 - x_at) * n_z + z_at) * 2 + side]
        return mine[:4] + partner[4:]

    order = [0]
    for k in range(1, n_z // 2):
        order += [n_z - k, k]
    order.append(n_z // 2)
    lines[...] = jnp.ones((LANES, LANES), F32)
    for k, shift in enumerate(order):
        lines[4 * k : 4 * k + 4, :] = 1.0 / full(xh, lax.rem(z + shift, n_z), 1 - role)
    mine = full(xh, z, role)
    lines[4 * n_z : 4 * n_z + 4, :] = 1.0 / mine
    lines[4 * n_z + 4 : 4 * n_z + 8, :] = 1.0 / full(1 - xh, z, role)
    columns = lines[...].T

    logs = jnp.log(mine) + jnp.log(full(xh, z, 1 - role))
    logs = jnp.where(role == 0, logs[:2], logs[2:])
    at = pl.multiple_of(role * ROWS, ROWS)
    both = ours[pl.ds(at, ROWS), :].astype(F32) * blocks[0][pl.ds(at, ROWS), :].astype(F32)
    both = both[:, :LANES] + both[:, LANES:]
    for k in range(2):
        positive = logit * to_lanes(both[k * LANES : (k + 1) * LANES, :])
        loss[:, k * LANES : (k + 1) * LANES] = 0.5 * logs[k : k + 1, :] - positive

    at = 0
    for block in blocks:
        for start in range(0, block.shape[0], LANES):
            line = at // LANES
            t = block[pl.ds(start, LANES), :].astype(F32)
            scaled[pl.ds(at, LANES), :] = (t * columns[:, line : line + 1]).astype(BF)
            at += LANES
    for start in range(0, 2 * CHIP, ROWS):
        rows = pl.ds(start, ROWS)
        acc = None
        at = 0
        for expo in expos:
            width = expo.shape[1]
            add = dot_nn(expo[rows, :], scaled[pl.ds(at, width), :])
            acc = add if acc is None else acc + add
            at += width
        for k in range(ROWS // LANES):
            line = 4 * n_z + start // LANES + k
            half = pl.ds(start + k * LANES, LANES)
            value = total[half, :] * columns[:, line : line + 1]
            value = value + acc[k * LANES : (k + 1) * LANES, :]
            if start < CHIP:
                own[half, :] = value
            else:
                send[pl.ds(start - CHIP + k * LANES, LANES), :] = value.astype(BF)


def backward_kernel(
    coef, n_y, place, own, recv, other, embed, inv, n1, f1, n2, f2, x,
    sa_mid, sa_out, goal_mid, goal_out,
    grads,
    w_mid, w_out, ge_s, h1_s, h2_s, p1_s, p2_s, sems,
):
    role = place[2]
    pairs = [((sa_out, goal_out), w_out), ((sa_mid, goal_mid), w_mid)]
    by_role(role, pairs, sems)
    wait_role(role, pairs, sems)
    for start in range(0, CHIP, LANES):
        rows = pl.ds(start, LANES)
        grad = coef * (
            own[rows, :] + recv[rows, :].astype(F32) - 2.0 * other[rows, :].astype(F32)
        )
        e = embed[rows, :]
        scale = inv[rows, :]
        along = jnp.mean(grad * e, axis=-1, keepdims=True)
        ge = (EMB ** (-0.5) * scale * (grad - e * (scale * scale * along))).astype(BF)
        ge_s[rows, :] = ge

        def step(back, normed, factor, hidden, out):
            v = normed[rows, :]
            gate = sigmoid(v)
            h = v * gate
            hidden[rows, :] = h.astype(BF)
            back = back * (gate * (1.0 + v - h))
            mean = jnp.mean(back, axis=-1, keepdims=True)
            tilt = jnp.mean(back * v, axis=-1, keepdims=True)
            pre = (factor[rows, :] * (back - mean - v * tilt)).astype(BF)
            out[rows, :] = pre
            return pre

        p2 = step(dot_nt(ge, w_out[...]), n2, f2, h2_s, p2_s)
        step(dot_nt(p2, w_mid[...]), n1, f1, h1_s, p1_s)
    tall = 256
    for start in range(0, HID, tall):
        span = slice(start, start + tall)
        for left, right, at in ((h1_s, p2_s, 0), (h2_s, ge_s, HID), (p1_s, x, HID + EMB)):
            width = right.shape[1]
            value = dot_tn(left[:, span], right[...])
            value = value.reshape(tall // (8 * n_y), n_y, 8, width)
            for y in range(n_y):
                piece = value[:, y].reshape(tall // n_y, width).astype(BF)
                first = start // n_y
                grads[y, first : first + tall // n_y, at : at + width] = piece


def sum_kernel(parts, order, out):
    value = parts[0].astype(F32)
    for k in range(1, parts.shape[0]):
        value = value + parts[k].astype(F32)
    out[...] = dot_nn(order[...], value.astype(BF)).astype(BF)


def add_kernel(parts, out):
    value = parts[0].astype(F32)
    for k in range(1, parts.shape[0]):
        value = value + parts[k].astype(F32)
    out[...] = value.astype(BF)


def shifted(value, axis, shift):
    count = lax.axis_size(axis)
    return lax.ppermute(value, axis, [(k, (k + shift) % count) for k in range(count)])


def body(
    observations,
    actions,
    replay_index,
    future_offset,
    sa_obs,
    sa_act,
    sa_mid,
    sa_out,
    goal_obs,
    goal_mid,
    goal_out,
):
    n_z, n_y, n_xl = lax.axis_size("z"), lax.axis_size("y"), lax.axis_size("xl")
    logit = 3.0 * math.sqrt(EMB)
    coef = logit / (2.0 * n_y * n_xl)
    role = lax.axis_index("c")
    place = jnp.stack([lax.axis_index("xh"), lax.axis_index("z"), role]).astype(jnp.int32)

    keep, send = call(
        pick_kernel, [shape((ROWS, WIDE), BF)] * 2, [SMEM] + [VMEM] * 4
    )(place, replay_index, future_offset, observations[0], actions[0])
    recv = shifted(send, "c", 1)
    x, n1, f1, n2, f2, embed, inv, unit = call(
        forward_kernel,
        [
            shape((CHIP, WIDE), BF),
            shape((CHIP, HID), F32),
            shape((CHIP, 1), F32),
            shape((CHIP, HID), F32),
            shape((CHIP, 1), F32),
            shape((CHIP, EMB), F32),
            shape((CHIP, 1), F32),
            shape((CHIP, EMB), BF),
        ],
        [SMEM, VMEM, VMEM] + [ANY] * 7,
        scratch=[
            pltpu.VMEM((WIDE, HID), BF),
            pltpu.VMEM((HID, HID), BF),
            pltpu.VMEM((HID, EMB), BF),
            pltpu.SemaphoreType.DMA((4,)),
        ],
    )(place, keep, recv, sa_obs, sa_act, sa_mid, sa_out, goal_obs, goal_mid, goal_out)

    other = shifted(unit, "c", 1)
    ahead = back = other
    theirs = shifted(unit, "xh", 1)
    blocks = [other]
    steps = [[other]]
    for k in range(1, n_z // 2):
        ahead, back = shifted(ahead, "z", 1), shifted(back, "z", -1)
        steps.append([ahead, back])
        blocks += [ahead, back]
    last = [shifted(ahead[:ROWS], "z", 1), shifted(back[ROWS:], "z", -1)]
    steps.append(last)
    blocks += last
    factor = logit * math.log2(math.e)
    expos = []
    prev = None
    for k, step in enumerate(steps):
        expo, part, total = scores(unit, theirs, step, prev, k == len(steps) - 1, factor)
        expos.append(expo)
        prev = (part, total)
    everyone = jnp.broadcast_to(part[None], (4 * n_z, 8, LANES))
    sums = lax.all_to_all(everyone, ("xh", "z", "c"), 0, 0)
    own, partial, loss = call(
        functools.partial(mix_kernel, n_z, logit),
        [shape((CHIP, EMB), F32), shape((CHIP, EMB), BF), shape((1, ROWS), F32)],
        [SMEM] + [VMEM] * (3 + len(expos) + len(blocks)),
        scratch=[pltpu.VMEM((LANES, LANES), F32), pltpu.VMEM((n_z * CHIP, EMB), BF)],
    )(place, sums, total, unit, *expos, *blocks)
    added = shifted(partial, "xh", 1)
    grads = call(
        functools.partial(backward_kernel, coef, n_y),
        [shape((n_y, HID // n_y, COLS), BF)],
        [SMEM] + [VMEM] * 10 + [ANY] * 4,
        scratch=[
            pltpu.VMEM((HID, HID), BF),
            pltpu.VMEM((HID, EMB), BF),
            pltpu.VMEM((CHIP, EMB), BF),
            pltpu.VMEM((CHIP, HID), BF),
            pltpu.VMEM((CHIP, HID), BF),
            pltpu.VMEM((CHIP, HID), BF),
            pltpu.VMEM((CHIP, HID), BF),
            pltpu.SemaphoreType.DMA((2,)),
        ],
    )(place, own, added, other, embed, inv, n1, f1, n2, f2, x, sa_mid, sa_out, goal_mid, goal_out)[0]

    tall = HID // n_y
    r = 8 // n_xl
    source = np.arange(tall).reshape(2, 2 * n_z, n_xl, r).transpose(0, 2, 1, 3).reshape(-1)
    order = jnp.asarray(np.eye(tall, dtype=np.float32)[source], BF)
    grads = lax.all_to_all(grads, "y", 0, 0)
    grads = call(sum_kernel, [shape((tall, COLS), BF)], [VMEM] * 2)(grads, order)[0]
    tall = tall // (2 * n_xl)
    grads = lax.all_to_all(grads.reshape(2 * n_xl, tall, COLS), ("xh", "xl"), 0, 0)
    grads = call(add_kernel, [shape((tall, COLS), BF)], [VMEM])(grads)[0]
    grads = lax.all_to_all(grads.reshape(n_z, 2 * r, COLS), "z", 0, 0)
    grads = jnp.sum(grads.astype(F32), axis=0)
    low, high = grads[:r], grads[r:]
    keep = jnp.where(role == 0, low, high)
    swap = shifted(jnp.where(role == 0, high, low), "c", 1)
    sa = jnp.where(role == 0, keep, swap)
    goal = jnp.where(role == 0, swap, keep)
    acts = sa_act.shape[0]
    low = HID + EMB
    return (
        loss,
        sa[:, low : low + EMB].T,
        sa[:, low + EMB : low + EMB + acts].T,
        sa[:, :HID],
        sa[:, HID:low],
        goal[:, low : low + EMB].T,
        goal[:, :HID],
        goal[:, HID:low],
    )


def solution(mesh):
    fine = Mesh(mesh.devices.reshape(2, -1, 2, mesh.shape["dp"] // 2, 2), ("xh", "z", "c", "y", "xl"))
    neg = ("xh", "z", "c")
    dp = ("y", "xl")
    return jax.shard_map(
        body,
        mesh=fine,
        in_specs=(
            P(dp, neg, None),
            P(dp, neg, None),
            P(dp, neg),
            P(dp, neg),
            P(),
            P(),
            P(),
            P(),
            P(),
            P(),
            P(),
        ),
        out_specs=(
            P(dp, neg),
            P(None, neg + dp),
            P(None, neg + dp),
            P(neg + dp, None),
            P(neg + dp, None),
            P(None, neg + dp),
            P(neg + dp, None),
            P(neg + dp, None),
        ),
        check_vma=False,
    )
```

```python
import functools
import math

import jax
import jax.numpy as jnp
from jax import lax
from jax.experimental import pallas as pl
from jax.experimental.pallas import tpu as pltpu
from jax.sharding import Mesh
from jax.sharding import PartitionSpec as P

NORM_EPS = 1e-05
UNIT_EPS = 1e-06
ROWS = 256
CHIP = 512
HID = 1024
EMB = 256
WIDE = 384
TILES = (HID + 2 * EMB) // 128
LANES = 128
BF = jnp.bfloat16
F32 = jnp.float32
VMEM = pl.BlockSpec(memory_space=pltpu.VMEM)
SMEM = pl.BlockSpec(memory_space=pltpu.SMEM)
HBM = pl.BlockSpec(memory_space=pltpu.HBM)
PARAMS = pltpu.CompilerParams(vmem_limit_bytes=20 * 1024 * 1024)


def shape(dims, dtype):
    return jax.ShapeDtypeStruct(dims, dtype)


def dot_nn(a, b):
    return lax.dot_general(a, b, (((1,), (0,)), ((), ())), preferred_element_type=F32)


def dot_nt(a, b):
    return lax.dot_general(a, b, (((1,), (1,)), ((), ())), preferred_element_type=F32)


def dot_tn(a, b):
    return lax.dot_general(a, b, (((0,), (0,)), ((), ())), preferred_element_type=F32)


def sigmoid(v):
    return 0.5 + 0.5 * jnp.tanh(0.5 * v)


def call(kernel, outs, in_specs, scratch=(), cost=None):
    specs = [VMEM] * len(outs)
    return pl.pallas_call(
        kernel,
        out_shape=outs,
        in_specs=in_specs,
        out_specs=specs,
        scratch_shapes=list(scratch),
        compiler_params=PARAMS,
        cost_estimate=cost,
    )


def pick_kernel(place, replay, offset, obs, act, keep, send, replay_s, offset_s, obs_s, act_s, sems):
    copies = [
        pltpu.make_async_copy(source, target, sems.at[n])
        for n, (source, target) in enumerate(
            ((replay, replay_s), (offset, offset_s), (obs, obs_s), (act, act_s))
        )
    ]
    for copy in copies:
        copy.start()
    for copy in copies:
        copy.wait()
    role = place[2]
    index = replay_s[...]
    ahead = index + offset_s[...]
    spot = lax.broadcasted_iota(jnp.int32, (obs_s.shape[0], ROWS), 0)
    for out, rows in (
        (keep, jnp.where(role == 0, index, ahead)),
        (send, jnp.where(role == 0, ahead, index)),
    ):
        hot = jnp.where(spot == rows, 1.0, 0.0).astype(BF)
        out[:, :EMB] = dot_tn(hot, obs_s[...]).astype(BF)
        extra = dot_nn(act_s[...], hot)
        copies = LANES // extra.shape[0]
        out[:, EMB:] = jnp.concatenate([extra] * copies, axis=0).T.astype(BF)


def by_role(role, pairs, sems):
    for k in range(2):

        @pl.when(role == k)
        def _():
            for n, (sources, target) in enumerate(pairs):
                if sources[k] is not None:
                    pltpu.make_async_copy(sources[k], target, sems.at[n]).start()


def wait_role(role, pairs, sems, first):
    for k in range(2):

        @pl.when(role == k)
        def _():
            for n, (sources, target) in enumerate(pairs):
                if sources[k] is not None:
                    pltpu.make_async_copy(sources[k], target, sems.at[first + n]).wait()


def forward_kernel(
    place, keep, recv, sa_obs, sa_act, sa_mid, sa_out, goal_obs, goal_mid, goal_out,
    x, n1, f1, n2, f2, embed, inv, unit,
    w_first, w_mid, w_out, sems,
):
    role = place[2]
    acts = sa_act.shape[0]
    w_first[EMB:, :] = jnp.zeros((WIDE - EMB, HID), BF)
    pairs = [
        ((sa_obs, goal_obs), w_first.at[pl.ds(0, EMB)]),
        ((sa_act, None), w_first.at[pl.ds(EMB, acts)]),
        ((sa_mid, goal_mid), w_mid),
        ((sa_out, goal_out), w_out),
    ]
    by_role(role, pairs, sems)
    own = pl.multiple_of(role * ROWS, ROWS)
    other = pl.multiple_of((1 - role) * ROWS, ROWS)
    x[pl.ds(own, ROWS), :] = keep[...]
    x[pl.ds(other, ROWS), :] = recv[...]
    for start in range(0, CHIP, LANES):
        rows = pl.ds(start, LANES)

        def norm(values, normed, factor):
            center = values - jnp.mean(values, axis=-1, keepdims=True)
            scale = lax.rsqrt(jnp.mean(center * center, axis=-1, keepdims=True) + NORM_EPS)
            v = center * scale
            normed[rows, :] = v
            factor[rows, :] = scale
            return (v * sigmoid(v)).astype(BF)

        if start == 0:
            wait_role(role, pairs[:2], sems, 0)
        h1 = norm(dot_nn(x[rows, :], w_first[...]), n1, f1)
        if start == 0:
            wait_role(role, pairs[2:], sems, 2)
        h2 = norm(dot_nn(h1, w_mid[...]), n2, f2)
        e = dot_nn(h2, w_out[...])
        scale = lax.rsqrt(jnp.mean(e * e, axis=-1, keepdims=True) + UNIT_EPS)
        embed[rows, :] = e
        inv[rows, :] = scale
        unit[rows, :] = (e * scale * EMB ** (-0.5)).astype(BF)


def to_lanes(values):
    return jnp.sum(values.T, axis=0, keepdims=True)


def score_kernel(n_blocks, first, last, factor, *refs):
    refs = list(refs)
    ours, theirs = refs[:2]
    blocks = refs[2 : 2 + n_blocks]
    refs = refs[2 + n_blocks :]
    if not first:
        old_sum, old_total = refs[:2]
        refs = refs[2:]
    expo, part, total = refs[:3]
    for start in range(0, 2 * CHIP, ROWS):
        source = ours if start < CHIP else theirs
        q = source[pl.ds(start % CHIP, ROWS), :]
        rows = pl.ds(start, ROWS)
        acc = None if first else old_total[rows, :]
        sums = None if first else old_sum[rows, :]
        at = 0
        for block in blocks:
            t = block[...]
            width = t.shape[0]
            e = jnp.exp2(dot_nt(q, t) * factor)
            for lane in range(0, width, LANES):
                piece = e[:, lane : lane + LANES]
                sums = piece if sums is None else sums + piece
            e16 = e.astype(BF)
            expo[rows, at : at + width] = e16
            add = dot_nn(e16, t)
            acc = add if acc is None else acc + add
            at += width
        total[rows, :] = acc
        if last:
            for k in range(ROWS // LANES):
                line = start // LANES + k
                part[line : line + 1, :] = to_lanes(sums[k * LANES : (k + 1) * LANES, :])
        else:
            part[rows, :] = sums


def scores(ours, theirs, blocks, prev, last, factor):
    width = sum(b.shape[0] for b in blocks)
    outs = [
        shape((2 * CHIP, width), BF),
        shape((8, LANES) if last else (2 * CHIP, LANES), F32),
        shape((2 * CHIP, EMB), F32),
    ]
    args = [ours, theirs, *blocks] + list(prev or ())
    kernel = functools.partial(score_kernel, len(blocks), prev is None, last, factor)
    cost = pl.CostEstimate(
        flops=4 * 2 * CHIP * width * EMB,
        bytes_accessed=2 * 2 * CHIP * width + 4 * 2 * CHIP * EMB,
        transcendentals=2 * CHIP * width,
    )
    return call(kernel, outs, [VMEM] * len(args), cost=cost)(*args)


def mix_rows(expos, scaled, total, columns, line, start, write):
    acc = None
    at = 0
    for expo in expos:
        width = expo.shape[1]
        add = dot_nn(expo[pl.ds(start, ROWS), :], scaled[pl.ds(at, width), :])
        acc = add if acc is None else acc + add
        at += width
    for k in range(ROWS // LANES):
        here = line + start // LANES + k
        value = total[pl.ds(start + k * LANES, LANES), :] * columns[:, here : here + 1]
        write(start + k * LANES, value + acc[k * LANES : (k + 1) * LANES, :])


def send_kernel(n_z, logit, place, sums, total, ours, *refs):
    n_exp = n_z // 2 + 1
    expos = refs[:n_exp]
    blocks = refs[n_exp : n_exp + n_z + 1]
    send, scaled, across, loss = refs[n_exp + n_z + 1 : n_exp + n_z + 5]
    lines = refs[n_exp + n_z + 5]
    xh, z, role = place[0], place[1], place[2]

    def full(x_at, z_at, side):
        mine = sums[(x_at * n_z + z_at) * 2 + side]
        partner = sums[((1 - x_at) * n_z + z_at) * 2 + side]
        return mine[:4] + partner[4:]

    order = [0]
    for k in range(1, n_z // 2):
        order += [n_z - k, k]
    order.append(n_z // 2)
    lines[...] = jnp.ones((LANES, LANES), F32)
    for k, shift in enumerate(order):
        lines[4 * k : 4 * k + 4, :] = 1.0 / full(xh, lax.rem(z + shift, n_z), 1 - role)
    mine = full(xh, z, role)
    lines[4 * n_z : 4 * n_z + 4, :] = 1.0 / mine
    lines[4 * n_z + 4 : 4 * n_z + 8, :] = 1.0 / full(1 - xh, z, role)
    columns = lines[...].T
    across[...] = columns

    at = 0
    for block in blocks:
        for start in range(0, block.shape[0], LANES):
            line = at // LANES
            t = block[pl.ds(start, LANES), :].astype(F32)
            scaled[pl.ds(at, LANES), :] = (t * columns[:, line : line + 1]).astype(BF)
            at += LANES

    def write(start, value):
        send[pl.ds(start - CHIP, LANES), :] = value.astype(BF)

    for start in range(CHIP, 2 * CHIP, ROWS):
        mix_rows(expos, scaled, total, columns, 4 * n_z, start, write)

    logs = jnp.log(mine) + jnp.log(full(xh, z, 1 - role))
    logs = jnp.where(role == 0, logs[:2], logs[2:])
    at = pl.multiple_of(role * ROWS, ROWS)
    both = ours[pl.ds(at, ROWS), :].astype(F32) * blocks[0][pl.ds(at, ROWS), :].astype(F32)
    both = both[:, :LANES] + both[:, LANES:]
    for k in range(2):
        positive = logit * to_lanes(both[k * LANES : (k + 1) * LANES, :])
        loss[:, k * LANES : (k + 1) * LANES] = 0.5 * logs[k : k + 1, :] - positive


def own_kernel(n_z, total, scaled, across, *refs):
    expos, own = refs[:-1], refs[-1]
    columns = across[...]

    def write(start, value):
        own[pl.ds(start, LANES), :] = value

    for start in range(0, CHIP, ROWS):
        mix_rows(expos, scaled, total, columns, 4 * n_z, start, write)


def backward_kernel(
    coef, place, own, recv, other, embed, inv, n1, f1, n2, f2, x,
    sa_mid, sa_out, goal_mid, goal_out,
    grads,
    w_mid, w_out, ge_s, h1_s, h2_s, p1_s, p2_s, sems,
):
    role = place[2]
    pairs = [((sa_out, goal_out), w_out), ((sa_mid, goal_mid), w_mid)]
    by_role(role, pairs, sems)
    for start in range(0, CHIP, LANES):
        rows = pl.ds(start, LANES)
        grad = coef * (
            own[rows, :] + recv[rows, :].astype(F32) - 2.0 * other[rows, :].astype(F32)
        )
        e = embed[rows, :]
        scale = inv[rows, :]
        along = jnp.mean(grad * e, axis=-1, keepdims=True)
        ge = (EMB ** (-0.5) * scale * (grad - e * (scale * scale * along))).astype(BF)
        ge_s[rows, :] = ge

        def step(back, normed, factor, hidden, out):
            v = normed[rows, :]
            gate = sigmoid(v)
            h = v * gate
            hidden[rows, :] = h.astype(BF)
            back = back * (gate * (1.0 + v - h))
            mean = jnp.mean(back, axis=-1, keepdims=True)
            tilt = jnp.mean(back * v, axis=-1, keepdims=True)
            pre = (factor[rows, :] * (back - mean - v * tilt)).astype(BF)
            out[rows, :] = pre
            return pre

        if start == 0:
            wait_role(role, pairs[:1], sems, 0)
        p2 = step(dot_nt(ge, w_out[...]), n2, f2, h2_s, p2_s)
        if start == 0:
            wait_role(role, pairs[1:], sems, 1)
        step(dot_nt(p2, w_mid[...]), n1, f1, h1_s, p1_s)
    tall = 256
    unit = lax.broadcasted_iota(jnp.int32, (tall, tall), 1)
    origin = (unit // 4 % 8) * 32 + unit // 64 * 8 + (unit // 32 % 2) * 4 + unit % 4
    order = jnp.where(lax.broadcasted_iota(jnp.int32, (tall, tall), 0) == origin, 1.0, 0.0).astype(BF)
    line = lax.broadcasted_iota(jnp.int32, (tall, LANES), 0)
    lane = lax.broadcasted_iota(jnp.int32, (tall, LANES), 1)
    wanted = lane // 16 == (line // 32 % 2) * 4 + line % 4
    pack_row = lax.broadcasted_iota(jnp.int32, (32, tall), 0)
    pack_col = lax.broadcasted_iota(jnp.int32, (32, tall), 1)
    pack = (pack_col // 64 == pack_row // 8) & (pack_col // 4 % 8 == pack_row % 8)
    pack = jnp.where(pack, 1.0, 0.0).astype(BF)
    packed = []
    for start in range(0, HID, tall):
        span = slice(start, start + tall)
        xh, half = start // tall // 2, start // tall % 2
        for left, right, tile in ((h1_s, p2_s, 0), (h2_s, ge_s, 8), (p1_s, x, 10)):
            units = dot_nn(left[:, span], order).astype(BF)
            value = dot_tn(units, right[:, : right.shape[1] // EMB * EMB])
            for k in range(value.shape[1] // LANES):
                for part in range(8):
                    piece = value[part * 32 : part * 32 + 32, k * LANES : (k + 1) * LANES]
                    at = (tile + k) * 64 + half * 32
                    dest = part // 2 * 4 + xh * 2 + part % 2
                    grads[dest, at : at + 32, :] = piece.astype(BF)
            if tile == 10:
                value = jnp.where(wanted, dot_tn(units, x[:, EMB:]), 0.0).astype(BF)
                packed.append(dot_nn(pack, value))
    for dest in range(16):
        y, xh = dest // 4, dest // 2 % 2
        two = [packed[2 * xh + half][y * 8 : y * 8 + 8] for half in range(2)]
        grads[dest, TILES * 64 : TILES * 64 + 16, :] = jnp.concatenate(two, axis=0).astype(BF)


def plus(parts, rows):
    value = parts[0, rows, :].astype(F32)
    for k in range(1, parts.shape[0]):
        value = value + parts[k, rows, :].astype(F32)
    return value


def sum_kernel(parts, out):
    tiles = [plus(parts, pl.ds(k * 64, 64)) for k in range(TILES)]
    extra = plus(parts, pl.ds(TILES * 64, 16))
    for z in range(out.shape[0]):
        rows = [tile[z * 8 : z * 8 + 8] for tile in tiles] + [extra]
        out[z] = jnp.concatenate(rows, axis=0).astype(BF)


def split_kernel(place, parts, keep, send, extra):
    role = place[2]
    value = plus(parts, slice(None))
    extra[...] = value[TILES * 8 :]
    for k in range(TILES):
        low, high = value[k * 8 : k * 8 + 4], value[k * 8 + 4 : k * 8 + 8]
        keep[k * 4 : k * 4 + 4, :] = jnp.where(role == 0, low, high)
        send[k * 4 : k * 4 + 4, :] = jnp.where(role == 0, high, low)
    blank = jnp.zeros((8, LANES), F32)
    for out, side in ((keep, role), (send, 1 - role)):
        out[TILES * 4 :, :] = blank + extra[pl.ds(place[1] * 2 + side, 1), :]


def last_kernel(place, keep, recv, obs_a, act_a, mid_a, out_a, obs_b, mid_b, out_b):
    role, xl = place[2], place[3]
    sa = jnp.where(role == 0, keep[...], recv[...])
    goal = jnp.where(role == 0, recv[...], keep[...])
    for value, mid, out, obs in ((sa, mid_a, out_a, obs_a), (goal, mid_b, out_b, obs_b)):
        for k in range(TILES):
            target, at = (mid, k) if k < 8 else (out, k - 8) if k < 10 else (obs, k - 10)
            target[:, at * LANES : (at + 1) * LANES] = value[k * 4 : k * 4 + 4]
    line = sa[TILES * 4 : TILES * 4 + 1]
    line = jnp.where(xl == 0, line[:, :64], line[:, 64:])
    for r in range(4):
        act_a[r : r + 1, :] = line[:, r * 16 : r * 16 + 16]


def shifted(value, axis, shift):
    count = lax.axis_size(axis)
    return lax.ppermute(value, axis, [(k, (k + shift) % count) for k in range(count)])


def body(
    observations,
    actions,
    replay_index,
    future_offset,
    sa_obs,
    sa_act,
    sa_mid,
    sa_out,
    goal_obs,
    goal_mid,
    goal_out,
):
    n_z = lax.axis_size("z")
    weights = (sa_obs, sa_act, sa_mid, sa_out, goal_obs, goal_mid, goal_out)
    sa_obs, sa_act, sa_mid, sa_out, goal_obs, goal_mid, goal_out = (
        pltpu.with_memory_space_constraint(weight, pltpu.HBM) for weight in weights
    )
    slabs = (replay_index, future_offset, observations[0], actions[0].T)
    slabs = [pltpu.with_memory_space_constraint(slab, pltpu.HBM) for slab in slabs]
    logit = 3.0 * math.sqrt(EMB)
    coef = logit / (2.0 * lax.axis_size("y") * lax.axis_size("xl"))
    place = jnp.stack([lax.axis_index(axis) for axis in ("xh", "z", "c", "xl")]).astype(jnp.int32)

    acts = actions.shape[2]
    tall = observations.shape[1]
    keep, send = call(
        pick_kernel,
        [shape((ROWS, WIDE), BF)] * 2,
        [SMEM] + [HBM] * 4,
        scratch=[
            pltpu.VMEM((1, ROWS), jnp.int32),
            pltpu.VMEM((1, ROWS), jnp.int32),
            pltpu.VMEM((tall, EMB), BF),
            pltpu.VMEM((acts, tall), BF),
            pltpu.SemaphoreType.DMA((4,)),
        ],
    )(place, *slabs)
    recv = shifted(send, "c", 1)
    x, n1, f1, n2, f2, embed, inv, unit = call(
        forward_kernel,
        [
            shape((CHIP, WIDE), BF),
            shape((CHIP, HID), F32),
            shape((CHIP, 1), F32),
            shape((CHIP, HID), F32),
            shape((CHIP, 1), F32),
            shape((CHIP, EMB), F32),
            shape((CHIP, 1), F32),
            shape((CHIP, EMB), BF),
        ],
        [SMEM, VMEM, VMEM] + [HBM] * 7,
        scratch=[
            pltpu.VMEM((WIDE, HID), BF),
            pltpu.VMEM((HID, HID), BF),
            pltpu.VMEM((HID, EMB), BF),
            pltpu.SemaphoreType.DMA((4,)),
        ],
    )(place, keep, recv, sa_obs, sa_act, sa_mid, sa_out, goal_obs, goal_mid, goal_out)

    other = shifted(unit, "c", 1)
    ahead = back = other
    theirs = shifted(unit, "xh", 1)
    steps = [[other]]
    factor = logit * math.log2(math.e)
    expos = []
    prev = None
    for k in range(n_z // 2 + 1):
        if k < n_z // 2 - 1:
            ahead, back = shifted(ahead, "z", 1), shifted(back, "z", -1)
            steps.append([ahead, back])
        elif k == n_z // 2 - 1:
            steps.append([shifted(ahead[:ROWS], "z", 1), shifted(back[ROWS:], "z", -1)])
        expo, part, total = scores(unit, theirs, steps[k], prev, k == n_z // 2, factor)
        expos.append(expo)
        prev = (part, total)
        if k < n_z // 2 - 1:
            ahead, back, part, total = lax.optimization_barrier((ahead, back, part, total))
            steps[-1] = [ahead, back]
            prev = (part, total)
    blocks = [block for step in steps for block in step]
    everyone = jnp.broadcast_to(part[None], (4 * n_z, 8, LANES))
    sums = lax.all_to_all(everyone, ("xh", "z", "c"), 0, 0)
    partial, scaled, across, loss = call(
        functools.partial(send_kernel, n_z, logit),
        [
            shape((CHIP, EMB), BF),
            shape((n_z * CHIP, EMB), BF),
            shape((LANES, LANES), F32),
            shape((1, ROWS), F32),
        ],
        [SMEM] + [VMEM] * (3 + len(expos) + len(blocks)),
        scratch=[pltpu.VMEM((LANES, LANES), F32)],
    )(place, sums, total, unit, *expos, *blocks)
    added = shifted(partial, "xh", 1)
    own = call(
        functools.partial(own_kernel, n_z),
        [shape((CHIP, EMB), F32)],
        [VMEM] * (3 + len(expos)),
        cost=pl.CostEstimate(
            flops=2 * CHIP * n_z * CHIP * EMB,
            bytes_accessed=2 * n_z * CHIP * (CHIP + EMB),
            transcendentals=0,
        ),
    )(total, scaled, across, *expos)[0]
    grads = call(
        functools.partial(backward_kernel, coef),
        [shape((16, TILES * 64 + 16, LANES), BF)],
        [SMEM] + [VMEM] * 10 + [HBM] * 4,
        scratch=[
            pltpu.VMEM((HID, HID), BF),
            pltpu.VMEM((HID, EMB), BF),
            pltpu.VMEM((CHIP, EMB), BF),
            pltpu.VMEM((CHIP, HID), BF),
            pltpu.VMEM((CHIP, HID), BF),
            pltpu.VMEM((CHIP, HID), BF),
            pltpu.VMEM((CHIP, HID), BF),
            pltpu.SemaphoreType.DMA((2,)),
        ],
    )(place, own, added, other, embed, inv, n1, f1, n2, f2, x, sa_mid, sa_out, goal_mid, goal_out)[0]

    grads = lax.all_to_all(grads, ("y", "xh", "xl"), 0, 0)
    grads = call(sum_kernel, [shape((n_z, TILES * 8 + 16, LANES), BF)], [VMEM])(grads)[0]
    grads = lax.all_to_all(grads, "z", 0, 0)
    keep, send = call(
        split_kernel,
        [shape((TILES * 4 + 8, LANES), F32)] * 2,
        [SMEM, VMEM],
        scratch=[pltpu.VMEM((16, LANES), F32)],
    )(place, grads)
    recv = shifted(send, "c", 1)
    obs_a, act_a, mid_a, out_a, obs_b, mid_b, out_b = call(
        last_kernel,
        [
            shape((4, EMB), F32),
            shape((4, acts), F32),
            shape((4, HID), F32),
            shape((4, EMB), F32),
            shape((4, EMB), F32),
            shape((4, HID), F32),
            shape((4, EMB), F32),
        ],
        [SMEM] + [VMEM] * 2,
    )(place, keep, recv)
    return (loss, obs_a.T, act_a.T, mid_a, out_a, obs_b.T, mid_b, out_b)


def solution(mesh):
    fine = Mesh(mesh.devices.reshape(2, -1, 2, mesh.shape["dp"] // 2, 2), ("xh", "z", "c", "y", "xl"))
    neg = ("xh", "z", "c")
    dp = ("y", "xl")
    return jax.shard_map(
        body,
        mesh=fine,
        in_specs=(
            P(dp, neg, None),
            P(dp, neg, None),
            P(dp, neg),
            P(dp, neg),
            P(),
            P(),
            P(),
            P(),
            P(),
            P(),
            P(),
        ),
        out_specs=(
            P(dp, neg),
            P(None, neg + dp),
            P(None, neg + dp),
            P(neg + dp, None),
            P(neg + dp, None),
            P(None, neg + dp),
            P(neg + dp, None),
            P(neg + dp, None),
        ),
        check_vma=False,
    )
```

```python
import functools
import math

import jax
import jax.numpy as jnp
from jax import lax
from jax.experimental import pallas as pl
from jax.experimental.pallas import tpu as pltpu
from jax.sharding import Mesh
from jax.sharding import PartitionSpec as P

NORM_EPS = 1e-05
UNIT_EPS = 1e-06
ROWS = 256
CHIP = 512
HID = 1024
EMB = 256
WIDE = 384
TALL = 256
TILES = (HID + 2 * EMB) // 128
LANES = 128
BF = jnp.bfloat16
F32 = jnp.float32
VMEM = pl.BlockSpec(memory_space=pltpu.VMEM)
SMEM = pl.BlockSpec(memory_space=pltpu.SMEM)
HBM = pl.BlockSpec(memory_space=pltpu.HBM)
PARAMS = pltpu.CompilerParams(vmem_limit_bytes=20 * 1024 * 1024)


def shape(dims, dtype):
    return jax.ShapeDtypeStruct(dims, dtype)


def dot_nn(a, b):
    return lax.dot_general(a, b, (((1,), (0,)), ((), ())), preferred_element_type=F32)


def dot_nt(a, b):
    return lax.dot_general(a, b, (((1,), (1,)), ((), ())), preferred_element_type=F32)


def dot_tn(a, b):
    return lax.dot_general(a, b, (((0,), (0,)), ((), ())), preferred_element_type=F32)


def sigmoid(v):
    return 0.5 + 0.5 * jnp.tanh(0.5 * v)


def call(kernel, outs, in_specs, scratch=(), cost=None):
    specs = [VMEM] * len(outs)
    return pl.pallas_call(
        kernel,
        out_shape=outs,
        in_specs=in_specs,
        out_specs=specs,
        scratch_shapes=list(scratch),
        compiler_params=PARAMS,
        cost_estimate=cost,
    )


def pick_kernel(place, replay, offset, obs, act, keep, send, replay_s, offset_s, obs_s, act_s, sems):
    copies = [
        pltpu.make_async_copy(source, target, sems.at[n])
        for n, (source, target) in enumerate(
            ((replay, replay_s), (offset, offset_s), (obs, obs_s), (act, act_s))
        )
    ]
    for copy in copies:
        copy.start()
    for copy in copies:
        copy.wait()
    role = place[2]
    index = replay_s[...]
    ahead = index + offset_s[...]
    spot = lax.broadcasted_iota(jnp.int32, (obs_s.shape[0], ROWS), 0)
    for out, rows in (
        (keep, jnp.where(role == 0, index, ahead)),
        (send, jnp.where(role == 0, ahead, index)),
    ):
        hot = jnp.where(spot == rows, 1.0, 0.0).astype(BF)
        out[:, :EMB] = dot_tn(hot, obs_s[...]).astype(BF)
        extra = dot_nn(act_s[...], hot)
        copies = LANES // extra.shape[0]
        out[:, EMB:] = jnp.concatenate([extra] * copies, axis=0).T.astype(BF)


def by_role(role, pairs, sems):
    for k in range(2):

        @pl.when(role == k)
        def _():
            for n, (sources, target) in enumerate(pairs):
                if sources[k] is not None:
                    pltpu.make_async_copy(sources[k], target, sems.at[n]).start()


def wait_role(role, pairs, sems, first):
    for k in range(2):

        @pl.when(role == k)
        def _():
            for n, (sources, target) in enumerate(pairs):
                if sources[k] is not None:
                    pltpu.make_async_copy(sources[k], target, sems.at[first + n]).wait()


def forward_kernel(
    place, keep, recv, sa_obs, sa_act, sa_mid, sa_out, goal_obs, goal_mid, goal_out,
    x, n1, f1, n2, f2, embed, inv, unit,
    w_first, w_mid, w_out, sems,
):
    role = place[2]
    acts = sa_act.shape[0]
    w_first[EMB:, :] = jnp.zeros((WIDE - EMB, HID), BF)
    pairs = [
        ((sa_obs, goal_obs), w_first.at[pl.ds(0, EMB)]),
        ((sa_act, None), w_first.at[pl.ds(EMB, acts)]),
        ((sa_mid, goal_mid), w_mid),
        ((sa_out, goal_out), w_out),
    ]
    by_role(role, pairs, sems)
    own = pl.multiple_of(role * ROWS, ROWS)
    other = pl.multiple_of((1 - role) * ROWS, ROWS)
    x[pl.ds(own, ROWS), :] = keep[...]
    x[pl.ds(other, ROWS), :] = recv[...]
    for start in range(0, CHIP, LANES):
        rows = pl.ds(start, LANES)

        def norm(values, normed, factor):
            center = values - jnp.mean(values, axis=-1, keepdims=True)
            scale = lax.rsqrt(jnp.mean(center * center, axis=-1, keepdims=True) + NORM_EPS)
            v = center * scale
            normed[rows, :] = v
            factor[rows, :] = scale
            return (v * sigmoid(v)).astype(BF)

        if start == 0:
            wait_role(role, pairs[:2], sems, 0)
        h1 = norm(dot_nn(x[rows, :], w_first[...]), n1, f1)
        if start == 0:
            wait_role(role, pairs[2:], sems, 2)
        h2 = norm(dot_nn(h1, w_mid[...]), n2, f2)
        e = dot_nn(h2, w_out[...])
        scale = lax.rsqrt(jnp.mean(e * e, axis=-1, keepdims=True) + UNIT_EPS)
        embed[rows, :] = e
        inv[rows, :] = scale
        unit[rows, :] = (e * scale * EMB ** (-0.5)).astype(BF)


def to_lanes(values):
    return jnp.sum(values.T, axis=0, keepdims=True)


def score_kernel(n_blocks, first, last, factor, *refs):
    refs = list(refs)
    ours, theirs = refs[:2]
    blocks = refs[2 : 2 + n_blocks]
    refs = refs[2 + n_blocks :]
    if not first:
        old_sum, old_total = refs[:2]
        refs = refs[2:]
    expo, part, total = refs[:3]
    for start in range(0, 2 * CHIP, ROWS):
        source = ours if start < CHIP else theirs
        q = source[pl.ds(start % CHIP, ROWS), :]
        rows = pl.ds(start, ROWS)
        acc = None if first else old_total[rows, :]
        sums = None if first else old_sum[rows, :]
        at = 0
        for block in blocks:
            t = block[...]
            width = t.shape[0]
            e = jnp.exp2(dot_nt(q, t) * factor)
            for lane in range(0, width, LANES):
                piece = e[:, lane : lane + LANES]
                sums = piece if sums is None else sums + piece
            e16 = e.astype(BF)
            expo[rows, at : at + width] = e16
            add = dot_nn(e16, t)
            acc = add if acc is None else acc + add
            at += width
        total[rows, :] = acc
        if last:
            for k in range(ROWS // LANES):
                line = start // LANES + k
                part[line : line + 1, :] = to_lanes(sums[k * LANES : (k + 1) * LANES, :])
        else:
            part[rows, :] = sums


def scores(ours, theirs, blocks, prev, last, factor):
    width = sum(b.shape[0] for b in blocks)
    outs = [
        shape((2 * CHIP, width), BF),
        shape((8, LANES) if last else (2 * CHIP, LANES), F32),
        shape((2 * CHIP, EMB), F32),
    ]
    args = [ours, theirs, *blocks] + list(prev or ())
    kernel = functools.partial(score_kernel, len(blocks), prev is None, last, factor)
    cost = pl.CostEstimate(
        flops=4 * 2 * CHIP * width * EMB,
        bytes_accessed=2 * 2 * CHIP * width + 4 * 2 * CHIP * EMB,
        transcendentals=2 * CHIP * width,
    )
    return call(kernel, outs, [VMEM] * len(args), cost=cost)(*args)


def mix_rows(expos, scaled, total, columns, line, start, write):
    acc = None
    at = 0
    for expo in expos:
        width = expo.shape[1]
        add = dot_nn(expo[pl.ds(start, ROWS), :], scaled[pl.ds(at, width), :])
        acc = add if acc is None else acc + add
        at += width
    for k in range(ROWS // LANES):
        here = line + start // LANES + k
        value = total[pl.ds(start + k * LANES, LANES), :] * columns[:, here : here + 1]
        write(start + k * LANES, value + acc[k * LANES : (k + 1) * LANES, :])


def send_kernel(n_z, logit, place, sums, total, ours, *refs):
    n_exp = n_z // 2 + 1
    expos = refs[:n_exp]
    blocks = refs[n_exp : n_exp + n_z + 1]
    send, scaled, across, loss = refs[n_exp + n_z + 1 : n_exp + n_z + 5]
    lines = refs[n_exp + n_z + 5]
    xh, z, role = place[0], place[1], place[2]

    def full(x_at, z_at, side):
        mine = sums[(x_at * n_z + z_at) * 2 + side]
        partner = sums[((1 - x_at) * n_z + z_at) * 2 + side]
        return mine[:4] + partner[4:]

    order = [0]
    for k in range(1, n_z // 2):
        order += [n_z - k, k]
    order.append(n_z // 2)
    lines[...] = jnp.ones((LANES, LANES), F32)
    for k, shift in enumerate(order):
        lines[4 * k : 4 * k + 4, :] = 1.0 / full(xh, lax.rem(z + shift, n_z), 1 - role)
    mine = full(xh, z, role)
    lines[4 * n_z : 4 * n_z + 4, :] = 1.0 / mine
    lines[4 * n_z + 4 : 4 * n_z + 8, :] = 1.0 / full(1 - xh, z, role)
    columns = lines[...].T
    across[...] = columns

    at = 0
    for block in blocks:
        for start in range(0, block.shape[0], LANES):
            line = at // LANES
            t = block[pl.ds(start, LANES), :].astype(F32)
            scaled[pl.ds(at, LANES), :] = (t * columns[:, line : line + 1]).astype(BF)
            at += LANES

    def write(start, value):
        send[pl.ds(start - CHIP, LANES), :] = value.astype(BF)

    for start in range(CHIP, 2 * CHIP, ROWS):
        mix_rows(expos, scaled, total, columns, 4 * n_z, start, write)

    logs = jnp.log(mine) + jnp.log(full(xh, z, 1 - role))
    logs = jnp.where(role == 0, logs[:2], logs[2:])
    at = pl.multiple_of(role * ROWS, ROWS)
    both = ours[pl.ds(at, ROWS), :].astype(F32) * blocks[0][pl.ds(at, ROWS), :].astype(F32)
    both = both[:, :LANES] + both[:, LANES:]
    for k in range(2):
        positive = logit * to_lanes(both[k * LANES : (k + 1) * LANES, :])
        loss[:, k * LANES : (k + 1) * LANES] = 0.5 * logs[k : k + 1, :] - positive


def own_kernel(n_z, total, scaled, across, *refs):
    expos, own = refs[:-1], refs[-1]
    columns = across[...]

    def write(start, value):
        own[pl.ds(start, LANES), :] = value

    for start in range(0, CHIP, ROWS):
        mix_rows(expos, scaled, total, columns, 4 * n_z, start, write)


def unit_order(tall):
    unit = lax.broadcasted_iota(jnp.int32, (tall, tall), 1)
    origin = (unit // 4 % 8) * 32 + unit // 64 * 8 + (unit // 32 % 2) * 4 + unit % 4
    line = lax.broadcasted_iota(jnp.int32, (tall, tall), 0)
    return jnp.where(line == origin, 1.0, 0.0).astype(BF)


def turned(order, values):
    return lax.dot_general(
        order, values, (((0,), (1,)), ((), ())), preferred_element_type=F32
    ).astype(BF)


def slope_kernel(normed, slope, hidden):
    order = unit_order(TALL)
    for start in range(0, CHIP, ROWS):
        rows = pl.ds(start, ROWS)
        for at in range(0, HID, TALL):
            v = normed[rows, at : at + TALL]
            gate = sigmoid(v)
            h = v * gate
            slope[rows, at : at + TALL] = gate * (1.0 + v - h)
            hidden[at : at + TALL, start : start + ROWS] = turned(order, h.astype(BF))


def slopes(normed):
    cost = pl.CostEstimate(
        flops=2 * CHIP * HID * TALL, bytes_accessed=10 * CHIP * HID, transcendentals=CHIP * HID
    )
    outs = [shape((CHIP, HID), F32), shape((HID, CHIP), BF)]
    return call(slope_kernel, outs, [VMEM], cost=cost)(normed)


def backward_kernel(
    coef, place, own, recv, other, embed, inv, n1, f1, s1, h1, n2, f2, s2, h2, x,
    sa_mid, sa_out, goal_mid, goal_out,
    grads,
    w_mid, w_out, ge_s, p1_s, p2_s, sems,
):
    role = place[2]
    pairs = [((sa_out, goal_out), w_out), ((sa_mid, goal_mid), w_mid)]
    by_role(role, pairs, sems)
    for start in range(0, CHIP, ROWS):
        rows = pl.ds(start, ROWS)
        grad = coef * (
            own[rows, :] + recv[rows, :].astype(F32) - 2.0 * other[rows, :].astype(F32)
        )
        e = embed[rows, :]
        scale = inv[rows, :]
        along = jnp.mean(grad * e, axis=-1, keepdims=True)
        ge = (EMB ** (-0.5) * scale * (grad - e * (scale * scale * along))).astype(BF)
        ge_s[rows, :] = ge

        def step(back, normed, factor, slope, out):
            v = normed[rows, :]
            back = back * slope[rows, :]
            mean = jnp.mean(back, axis=-1, keepdims=True)
            tilt = jnp.mean(back * v, axis=-1, keepdims=True)
            pre = (factor[rows, :] * (back - mean - v * tilt)).astype(BF)
            out[rows, :] = pre
            return pre

        if start == 0:
            wait_role(role, pairs[:1], sems, 0)
        p2 = step(dot_nt(ge, w_out[...]), n2, f2, s2, p2_s)
        if start == 0:
            wait_role(role, pairs[1:], sems, 1)
        step(dot_nt(p2, w_mid[...]), n1, f1, s1, p1_s)
    tall = TALL
    order = unit_order(tall)

    def slot(y, x_at):
        return jnp.where(role == 0, y, x_at), jnp.where(role == 0, x_at, y)

    line = lax.broadcasted_iota(jnp.int32, (tall, LANES), 0)
    lane = lax.broadcasted_iota(jnp.int32, (tall, LANES), 1)
    wanted = lane // 16 == (line // 32 % 2) * 4 + line % 4
    pack_row = lax.broadcasted_iota(jnp.int32, (32, tall), 0)
    pack_col = lax.broadcasted_iota(jnp.int32, (32, tall), 1)
    pack = (pack_col // 64 == pack_row // 8) & (pack_col // 4 % 8 == pack_row % 8)
    pack = jnp.where(pack, 1.0, 0.0).astype(BF)
    packed = []
    for start in range(0, HID, tall):
        span = slice(start, start + tall)
        xh, half = start // tall // 2, start // tall % 2
        for left, right, tile in ((h1, p2_s, 0), (h2, ge_s, 8), (None, x, 10)):
            units = turned(order, p1_s[:, span]) if left is None else left[span, :]
            value = dot_nn(units, right[:, : right.shape[1] // EMB * EMB])
            for k in range(value.shape[1] // LANES):
                for part in range(8):
                    piece = value[part * 32 : part * 32 + 32, k * LANES : (k + 1) * LANES]
                    at = (tile + k) * 64 + half * 32
                    first, second = slot(part // 2, xh * 2 + part % 2)
                    grads[first, second, at : at + 32, :] = piece.astype(BF)
            if tile == 10:
                value = jnp.where(wanted, dot_nn(units, x[:, EMB:]), 0.0).astype(BF)
                packed.append(dot_nn(pack, value))
    for part in range(16):
        y, xh = part // 4, part // 2 % 2
        first, second = slot(y, part % 4)
        two = [packed[2 * xh + half][y * 8 : y * 8 + 8] for half in range(2)]
        grads[first, second, TILES * 64 : TILES * 64 + 16, :] = jnp.concatenate(two, axis=0).astype(BF)


def plus(parts, rows):
    value = parts[0, rows, :].astype(F32)
    for k in range(1, parts.shape[0]):
        value = value + parts[k, rows, :].astype(F32)
    return value


def add_kernel(parts, out):
    for dest in range(parts.shape[1]):
        value = parts[0, dest].astype(F32)
        for k in range(1, parts.shape[0]):
            value = value + parts[k, dest].astype(F32)
        out[dest] = value.astype(BF)


def sum_kernel(parts, out):
    tiles = [plus(parts, pl.ds(k * 64, 64)) for k in range(TILES)]
    extra = plus(parts, pl.ds(TILES * 64, 16))
    for z in range(out.shape[0]):
        rows = [tile[z * 8 : z * 8 + 8] for tile in tiles] + [extra]
        out[z] = jnp.concatenate(rows, axis=0).astype(BF)


def split_kernel(place, parts, keep, send, extra):
    role = place[2]
    value = plus(parts, slice(None))
    extra[...] = value[TILES * 8 :]
    for k in range(TILES):
        low, high = value[k * 8 : k * 8 + 4], value[k * 8 + 4 : k * 8 + 8]
        keep[k * 4 : k * 4 + 4, :] = jnp.where(role == 0, low, high)
        send[k * 4 : k * 4 + 4, :] = jnp.where(role == 0, high, low)
    blank = jnp.zeros((8, LANES), F32)
    for out, side in ((keep, role), (send, 1 - role)):
        out[TILES * 4 :, :] = blank + extra[pl.ds(place[1] * 2 + side, 1), :]


def last_kernel(place, keep, recv, obs_a, act_a, mid_a, out_a, obs_b, mid_b, out_b):
    role, xl = place[2], place[3]
    sa = jnp.where(role == 0, keep[...], recv[...])
    goal = jnp.where(role == 0, recv[...], keep[...])
    for value, mid, out, obs in ((sa, mid_a, out_a, obs_a), (goal, mid_b, out_b, obs_b)):
        for k in range(TILES):
            target, at = (mid, k) if k < 8 else (out, k - 8) if k < 10 else (obs, k - 10)
            target[:, at * LANES : (at + 1) * LANES] = value[k * 4 : k * 4 + 4]
    line = sa[TILES * 4 : TILES * 4 + 1]
    line = jnp.where(xl == 0, line[:, :64], line[:, 64:])
    for r in range(4):
        act_a[r : r + 1, :] = line[:, r * 16 : r * 16 + 16]


def shifted(value, axis, shift):
    count = lax.axis_size(axis)
    return lax.ppermute(value, axis, [(k, (k + shift) % count) for k in range(count)])


def body(
    observations,
    actions,
    replay_index,
    future_offset,
    sa_obs,
    sa_act,
    sa_mid,
    sa_out,
    goal_obs,
    goal_mid,
    goal_out,
):
    n_z = lax.axis_size("z")
    weights = (sa_obs, sa_act, sa_mid, sa_out, goal_obs, goal_mid, goal_out)
    sa_obs, sa_act, sa_mid, sa_out, goal_obs, goal_mid, goal_out = (
        pltpu.with_memory_space_constraint(weight, pltpu.HBM) for weight in weights
    )
    slabs = (replay_index, future_offset, observations[0], actions[0].T)
    slabs = [pltpu.with_memory_space_constraint(slab, pltpu.HBM) for slab in slabs]
    logit = 3.0 * math.sqrt(EMB)
    coef = logit / (2.0 * lax.axis_size("y") * lax.axis_size("xl"))
    place = jnp.stack([lax.axis_index(axis) for axis in ("xh", "z", "c", "xl")]).astype(jnp.int32)

    acts = actions.shape[2]
    tall = observations.shape[1]
    keep, send = call(
        pick_kernel,
        [shape((ROWS, WIDE), BF)] * 2,
        [SMEM] + [HBM] * 4,
        scratch=[
            pltpu.VMEM((1, ROWS), jnp.int32),
            pltpu.VMEM((1, ROWS), jnp.int32),
            pltpu.VMEM((tall, EMB), BF),
            pltpu.VMEM((acts, tall), BF),
            pltpu.SemaphoreType.DMA((4,)),
        ],
    )(place, *slabs)
    recv = shifted(send, "c", 1)
    x, n1, f1, n2, f2, embed, inv, unit = call(
        forward_kernel,
        [
            shape((CHIP, WIDE), BF),
            shape((CHIP, HID), F32),
            shape((CHIP, 1), F32),
            shape((CHIP, HID), F32),
            shape((CHIP, 1), F32),
            shape((CHIP, EMB), F32),
            shape((CHIP, 1), F32),
            shape((CHIP, EMB), BF),
        ],
        [SMEM, VMEM, VMEM] + [HBM] * 7,
        scratch=[
            pltpu.VMEM((WIDE, HID), BF),
            pltpu.VMEM((HID, HID), BF),
            pltpu.VMEM((HID, EMB), BF),
            pltpu.SemaphoreType.DMA((4,)),
        ],
    )(place, keep, recv, sa_obs, sa_act, sa_mid, sa_out, goal_obs, goal_mid, goal_out)

    other = shifted(unit, "c", 1)
    ahead = back = other
    theirs = shifted(unit, "xh", 1)
    steps = [[other]]
    factor = logit * math.log2(math.e)
    expos = []
    prev = None
    for k in range(n_z // 2 + 1):
        if k < n_z // 2 - 1:
            ahead, back = shifted(ahead, "z", 1), shifted(back, "z", -1)
            steps.append([ahead, back])
        elif k == n_z // 2 - 1:
            steps.append([shifted(ahead[:ROWS], "z", 1), shifted(back[ROWS:], "z", -1)])
        expo, part, total = scores(unit, theirs, steps[k], prev, k == n_z // 2, factor)
        expos.append(expo)
        prev = (part, total)
        if k == 1:
            s1, h1 = slopes(n1)
            part, s1, h1 = lax.optimization_barrier((part, s1, h1))
        if k == 2:
            s2, h2 = slopes(n2)
            part, s2, h2 = lax.optimization_barrier((part, s2, h2))
        prev = (part, total)
        if k < n_z // 2 - 1:
            ahead, back, part, total = lax.optimization_barrier((ahead, back, part, total))
            steps[-1] = [ahead, back]
            prev = (part, total)
    blocks = [block for step in steps for block in step]
    everyone = jnp.broadcast_to(part[None], (4 * n_z, 8, LANES))
    sums = lax.all_to_all(everyone, ("xh", "z", "c"), 0, 0)
    partial, scaled, across, loss = call(
        functools.partial(send_kernel, n_z, logit),
        [
            shape((CHIP, EMB), BF),
            shape((n_z * CHIP, EMB), BF),
            shape((LANES, LANES), F32),
            shape((1, ROWS), F32),
        ],
        [SMEM] + [VMEM] * (3 + len(expos) + len(blocks)),
        scratch=[pltpu.VMEM((LANES, LANES), F32)],
    )(place, sums, total, unit, *expos, *blocks)
    added = shifted(partial, "xh", 1)
    own = call(
        functools.partial(own_kernel, n_z),
        [shape((CHIP, EMB), F32)],
        [VMEM] * (3 + len(expos)),
        cost=pl.CostEstimate(
            flops=2 * CHIP * n_z * CHIP * EMB,
            bytes_accessed=2 * n_z * CHIP * (CHIP + EMB),
            transcendentals=0,
        ),
    )(total, scaled, across, *expos)[0]
    grads = call(
        functools.partial(backward_kernel, coef),
        [shape((4, 4, TILES * 64 + 16, LANES), BF)],
        [SMEM] + [VMEM] * 14 + [HBM] * 4,
        scratch=[
            pltpu.VMEM((HID, HID), BF),
            pltpu.VMEM((HID, EMB), BF),
            pltpu.VMEM((CHIP, EMB), BF),
            pltpu.VMEM((CHIP, HID), BF),
            pltpu.VMEM((CHIP, HID), BF),
            pltpu.SemaphoreType.DMA((2,)),
        ],
    )(
        place, own, added, other, embed, inv, n1, f1, s1, h1, n2, f2, s2, h2, x,
        sa_mid, sa_out, goal_mid, goal_out,
    )[0]

    along_y = [[y * 4 + x_at for y in range(4)] for x_at in range(4)]
    along_x = [[y * 4 + x_at for x_at in range(4)] for y in range(4)]

    def exchange(parts, low, high):
        groups = low + [[16 + member for member in group] for group in high]
        return lax.all_to_all(parts, ("c", "y", "xh", "xl"), 0, 0, axis_index_groups=groups)

    height = TILES * 64 + 16
    grads = exchange(grads, along_y, along_x)
    grads = call(add_kernel, [shape((4, height, LANES), BF)], [VMEM])(grads)[0]
    grads = exchange(grads, along_x, along_y)
    grads = call(sum_kernel, [shape((n_z, TILES * 8 + 16, LANES), BF)], [VMEM])(grads)[0]
    grads = lax.all_to_all(grads, "z", 0, 0)
    keep, send = call(
        split_kernel,
        [shape((TILES * 4 + 8, LANES), F32)] * 2,
        [SMEM, VMEM],
        scratch=[pltpu.VMEM((16, LANES), F32)],
    )(place, grads)
    recv = shifted(send, "c", 1)
    obs_a, act_a, mid_a, out_a, obs_b, mid_b, out_b = call(
        last_kernel,
        [
            shape((4, EMB), F32),
            shape((4, acts), F32),
            shape((4, HID), F32),
            shape((4, EMB), F32),
            shape((4, EMB), F32),
            shape((4, HID), F32),
            shape((4, EMB), F32),
        ],
        [SMEM] + [VMEM] * 2,
    )(place, keep, recv)
    return (loss, obs_a.T, act_a.T, mid_a, out_a, obs_b.T, mid_b, out_b)


def solution(mesh):
    fine = Mesh(mesh.devices.reshape(2, -1, 2, mesh.shape["dp"] // 2, 2), ("xh", "z", "c", "y", "xl"))
    neg = ("xh", "z", "c")
    dp = ("y", "xl")
    return jax.shard_map(
        body,
        mesh=fine,
        in_specs=(
            P(dp, neg, None),
            P(dp, neg, None),
            P(dp, neg),
            P(dp, neg),
            P(),
            P(),
            P(),
            P(),
            P(),
            P(),
            P(),
        ),
        out_specs=(
            P(dp, neg),
            P(None, neg + dp),
            P(None, neg + dp),
            P(neg + dp, None),
            P(neg + dp, None),
            P(None, neg + dp),
            P(neg + dp, None),
            P(neg + dp, None),
        ),
        check_vma=False,
    )
```

```python
import functools
import math

import jax
import jax.numpy as jnp
from jax import lax
from jax.experimental import pallas as pl
from jax.experimental.pallas import tpu as pltpu
from jax.sharding import Mesh
from jax.sharding import PartitionSpec as P

NORM_EPS = 1e-05
UNIT_EPS = 1e-06
ROWS = 256
CHIP = 512
HID = 1024
EMB = 256
WIDE = 384
TALL = 256
TILES = (HID + 2 * EMB) // 128
LANES = 128
BF = jnp.bfloat16
F32 = jnp.float32
VMEM = pl.BlockSpec(memory_space=pltpu.VMEM)
SMEM = pl.BlockSpec(memory_space=pltpu.SMEM)
HBM = pl.BlockSpec(memory_space=pltpu.HBM)
PARAMS = pltpu.CompilerParams(vmem_limit_bytes=20 * 1024 * 1024)


def shape(dims, dtype):
    return jax.ShapeDtypeStruct(dims, dtype)


def dot_nn(a, b):
    return lax.dot_general(a, b, (((1,), (0,)), ((), ())), preferred_element_type=F32)


def dot_nt(a, b):
    return lax.dot_general(a, b, (((1,), (1,)), ((), ())), preferred_element_type=F32)


def dot_tn(a, b):
    return lax.dot_general(a, b, (((0,), (0,)), ((), ())), preferred_element_type=F32)


def sigmoid(v):
    return 0.5 + 0.5 * jnp.tanh(0.5 * v)


def call(kernel, outs, in_specs, scratch=(), cost=None):
    specs = [VMEM] * len(outs)
    return pl.pallas_call(
        kernel,
        out_shape=outs,
        in_specs=in_specs,
        out_specs=specs,
        scratch_shapes=list(scratch),
        compiler_params=PARAMS,
        cost_estimate=cost,
    )


def pick_kernel(place, replay, offset, obs, act, keep, send, replay_s, offset_s, obs_s, act_s, sems):
    copies = [
        pltpu.make_async_copy(source, target, sems.at[n])
        for n, (source, target) in enumerate(
            ((replay, replay_s), (offset, offset_s), (obs, obs_s), (act, act_s))
        )
    ]
    for copy in copies:
        copy.start()
    for copy in copies:
        copy.wait()
    role = place[2]
    index = replay_s[...]
    ahead = index + offset_s[...]
    spot = lax.broadcasted_iota(jnp.int32, (obs_s.shape[0], ROWS), 0)
    for out, rows in (
        (keep, jnp.where(role == 0, index, ahead)),
        (send, jnp.where(role == 0, ahead, index)),
    ):
        hot = jnp.where(spot == rows, 1.0, 0.0).astype(BF)
        out[:, :EMB] = dot_tn(hot, obs_s[...]).astype(BF)
        extra = dot_nn(act_s[...], hot)
        copies = LANES // extra.shape[0]
        out[:, EMB:] = jnp.concatenate([extra] * copies, axis=0).T.astype(BF)


def by_role(role, pairs, sems):
    for k in range(2):

        @pl.when(role == k)
        def _():
            for n, (sources, target) in enumerate(pairs):
                if sources[k] is not None:
                    pltpu.make_async_copy(sources[k], target, sems.at[n]).start()


def wait_role(role, pairs, sems, first):
    for k in range(2):

        @pl.when(role == k)
        def _():
            for n, (sources, target) in enumerate(pairs):
                if sources[k] is not None:
                    pltpu.make_async_copy(sources[k], target, sems.at[first + n]).wait()


def forward_kernel(
    place, keep, recv, sa_obs, sa_act, sa_mid, sa_out, goal_obs, goal_mid, goal_out,
    x, n1, f1, n2, f2, embed, inv, unit,
    w_first, w_mid, w_out, sems,
):
    role = place[2]
    acts = sa_act.shape[0]
    w_first[EMB:, :] = jnp.zeros((WIDE - EMB, HID), BF)
    pairs = [
        ((sa_obs, goal_obs), w_first.at[pl.ds(0, EMB)]),
        ((sa_act, None), w_first.at[pl.ds(EMB, acts)]),
        ((sa_mid, goal_mid), w_mid),
        ((sa_out, goal_out), w_out),
    ]
    by_role(role, pairs, sems)
    own = pl.multiple_of(role * ROWS, ROWS)
    other = pl.multiple_of((1 - role) * ROWS, ROWS)
    x[pl.ds(own, ROWS), :] = keep[...]
    x[pl.ds(other, ROWS), :] = recv[...]
    for start in range(0, CHIP, ROWS):
        rows = pl.ds(start, ROWS)

        def norm(values, normed, factor):
            center = values - jnp.mean(values, axis=-1, keepdims=True)
            scale = lax.rsqrt(jnp.mean(center * center, axis=-1, keepdims=True) + NORM_EPS)
            v = center * scale
            normed[rows, :] = v
            factor[rows, :] = scale
            return (v * sigmoid(v)).astype(BF)

        if start == 0:
            wait_role(role, pairs[:2], sems, 0)
        h1 = norm(dot_nn(x[rows, :], w_first[...]), n1, f1)
        if start == 0:
            wait_role(role, pairs[2:], sems, 2)
        h2 = norm(dot_nn(h1, w_mid[...]), n2, f2)
        e = dot_nn(h2, w_out[...])
        scale = lax.rsqrt(jnp.mean(e * e, axis=-1, keepdims=True) + UNIT_EPS)
        embed[rows, :] = e
        inv[rows, :] = scale
        unit[rows, :] = (e * scale * EMB ** (-0.5)).astype(BF)


def to_lanes(values):
    return jnp.sum(values.T, axis=0, keepdims=True)


def score_kernel(n_blocks, first, last, factor, *refs):
    refs = list(refs)
    ours, theirs = refs[:2]
    blocks = refs[2 : 2 + n_blocks]
    refs = refs[2 + n_blocks :]
    if not first:
        old_sum, old_total = refs[:2]
        refs = refs[2:]
    expo, part, total = refs[:3]
    for start in range(0, 2 * CHIP, ROWS):
        source = ours if start < CHIP else theirs
        q = source[pl.ds(start % CHIP, ROWS), :]
        rows = pl.ds(start, ROWS)
        acc = None if first else old_total[rows, :]
        sums = None if first else old_sum[rows, :]
        at = 0
        for block in blocks:
            t = block[...]
            width = t.shape[0]
            e = jnp.exp2(dot_nt(q, t) * factor)
            for lane in range(0, width, LANES):
                piece = e[:, lane : lane + LANES]
                sums = piece if sums is None else sums + piece
            e16 = e.astype(BF)
            expo[rows, at : at + width] = e16
            add = dot_nn(e16, t)
            acc = add if acc is None else acc + add
            at += width
        total[rows, :] = acc
        if last:
            for k in range(ROWS // LANES):
                line = start // LANES + k
                part[line : line + 1, :] = to_lanes(sums[k * LANES : (k + 1) * LANES, :])
        else:
            part[rows, :] = sums


def scores(ours, theirs, blocks, prev, last, factor):
    width = sum(b.shape[0] for b in blocks)
    outs = [
        shape((2 * CHIP, width), BF),
        shape((8, LANES) if last else (2 * CHIP, LANES), F32),
        shape((2 * CHIP, EMB), F32),
    ]
    args = [ours, theirs, *blocks] + list(prev or ())
    kernel = functools.partial(score_kernel, len(blocks), prev is None, last, factor)
    cost = pl.CostEstimate(
        flops=4 * 2 * CHIP * width * EMB,
        bytes_accessed=2 * 2 * CHIP * width + 4 * 2 * CHIP * EMB,
        transcendentals=2 * CHIP * width,
    )
    return call(kernel, outs, [VMEM] * len(args), cost=cost)(*args)


def mix_rows(expos, scaled, total, columns, line, start, write):
    acc = None
    at = 0
    for expo in expos:
        width = expo.shape[1]
        add = dot_nn(expo[pl.ds(start, ROWS), :], scaled[pl.ds(at, width), :])
        acc = add if acc is None else acc + add
        at += width
    for k in range(ROWS // LANES):
        here = line + start // LANES + k
        value = total[pl.ds(start + k * LANES, LANES), :] * columns[:, here : here + 1]
        write(start + k * LANES, value + acc[k * LANES : (k + 1) * LANES, :])


def send_kernel(n_z, logit, place, sums, total, ours, *refs):
    n_exp = 3
    expos = refs[:n_exp]
    blocks = refs[n_exp : n_exp + n_z + 1]
    send, scaled, across, loss = refs[n_exp + n_z + 1 : n_exp + n_z + 5]
    lines = refs[n_exp + n_z + 5]
    xh, z, role = place[0], place[1], place[2]

    def full(x_at, z_at, side):
        mine = sums[x_at * n_z + z_at]
        partner = sums[(1 - x_at) * n_z + z_at]
        return mine[side * 8 : side * 8 + 4] + partner[side * 8 + 4 : side * 8 + 8]

    order = [0]
    for k in range(1, n_z // 2):
        order += [n_z - k, k]
    order.append(n_z // 2)
    lines[...] = jnp.ones((LANES, LANES), F32)
    for k, shift in enumerate(order):
        lines[4 * k : 4 * k + 4, :] = 1.0 / full(xh, lax.rem(z + shift, n_z), 1)
    mine = full(xh, z, 0)
    lines[4 * n_z : 4 * n_z + 4, :] = 1.0 / mine
    lines[4 * n_z + 4 : 4 * n_z + 8, :] = 1.0 / full(1 - xh, z, 0)
    columns = lines[...].T
    across[...] = columns

    at = 0
    for block in blocks:
        for start in range(0, block.shape[0], LANES):
            line = at // LANES
            t = block[pl.ds(start, LANES), :].astype(F32)
            scaled[pl.ds(at, LANES), :] = (t * columns[:, line : line + 1]).astype(BF)
            at += LANES

    def write(start, value):
        send[pl.ds(start - CHIP, LANES), :] = value.astype(BF)

    for start in range(CHIP, 2 * CHIP, ROWS):
        mix_rows(expos, scaled, total, columns, 4 * n_z, start, write)

    logs = jnp.log(mine) + jnp.log(full(xh, z, 1))
    logs = jnp.where(role == 0, logs[:2], logs[2:])
    at = pl.multiple_of(role * ROWS, ROWS)
    both = ours[pl.ds(at, ROWS), :].astype(F32) * blocks[0][pl.ds(at, ROWS), :].astype(F32)
    both = both[:, :LANES] + both[:, LANES:]
    for k in range(2):
        positive = logit * to_lanes(both[k * LANES : (k + 1) * LANES, :])
        loss[:, k * LANES : (k + 1) * LANES] = 0.5 * logs[k : k + 1, :] - positive


def own_kernel(n_z, total, scaled, across, *refs):
    expos, own = refs[:-1], refs[-1]
    columns = across[...]

    def write(start, value):
        own[pl.ds(start, LANES), :] = value

    for start in range(0, CHIP, ROWS):
        mix_rows(expos, scaled, total, columns, 4 * n_z, start, write)


def unit_order(tall):
    unit = lax.broadcasted_iota(jnp.int32, (tall, tall), 1)
    origin = (unit // 4 % 8) * 32 + unit // 64 * 8 + (unit // 32 % 2) * 4 + unit % 4
    line = lax.broadcasted_iota(jnp.int32, (tall, tall), 0)
    return jnp.where(line == origin, 1.0, 0.0).astype(BF)


def turned(order, values):
    return lax.dot_general(
        order, values, (((0,), (1,)), ((), ())), preferred_element_type=F32
    ).astype(BF)


def slope_kernel(normed, slope, hidden):
    order = unit_order(TALL)
    for start in range(0, CHIP, ROWS):
        rows = pl.ds(start, ROWS)
        for at in range(0, HID, TALL):
            v = normed[rows, at : at + TALL]
            gate = sigmoid(v)
            h = v * gate
            slope[rows, at : at + TALL] = gate * (1.0 + v - h)
            hidden[at : at + TALL, start : start + ROWS] = turned(order, h.astype(BF))


def slopes(normed):
    cost = pl.CostEstimate(
        flops=2 * CHIP * HID * TALL, bytes_accessed=10 * CHIP * HID, transcendentals=CHIP * HID
    )
    outs = [shape((CHIP, HID), F32), shape((HID, CHIP), BF)]
    return call(slope_kernel, outs, [VMEM], cost=cost)(normed)


def backward_kernel(
    coef, place, own, recv, other, embed, inv, n1, f1, s1, h1, n2, f2, s2, h2, x,
    sa_mid, sa_out, goal_mid, goal_out,
    grads,
    w_mid, w_out, ge_s, p1_s, p2_s, sems,
):
    role = place[2]
    pairs = [((sa_out, goal_out), w_out), ((sa_mid, goal_mid), w_mid)]
    by_role(role, pairs, sems)
    for start in range(0, CHIP, ROWS):
        rows = pl.ds(start, ROWS)
        grad = coef * (
            own[rows, :] + recv[rows, :].astype(F32) - 2.0 * other[rows, :].astype(F32)
        )
        e = embed[rows, :]
        scale = inv[rows, :]
        along = jnp.mean(grad * e, axis=-1, keepdims=True)
        ge = (EMB ** (-0.5) * scale * (grad - e * (scale * scale * along))).astype(BF)
        ge_s[rows, :] = ge

        def step(back, normed, factor, slope, out):
            v = normed[rows, :]
            back = back * slope[rows, :]
            mean = jnp.mean(back, axis=-1, keepdims=True)
            tilt = jnp.mean(back * v, axis=-1, keepdims=True)
            pre = (factor[rows, :] * (back - mean - v * tilt)).astype(BF)
            out[rows, :] = pre
            return pre

        if start == 0:
            wait_role(role, pairs[:1], sems, 0)
        p2 = step(dot_nt(ge, w_out[...]), n2, f2, s2, p2_s)
        if start == 0:
            wait_role(role, pairs[1:], sems, 1)
        step(dot_nt(p2, w_mid[...]), n1, f1, s1, p1_s)
    tall = TALL
    order = unit_order(tall)

    def slot(y, x_at):
        return jnp.where(role == 0, y, x_at), jnp.where(role == 0, x_at, y)

    row = lax.broadcasted_iota(jnp.int32, (tall, LANES), 0)
    lane = lax.broadcasted_iota(jnp.int32, (tall, LANES), 1)
    wanted = lane // 16 == (row // 32 % 2) * 4 + row % 4
    pack_row = lax.broadcasted_iota(jnp.int32, (32, tall), 0)
    pack_col = lax.broadcasted_iota(jnp.int32, (32, tall), 1)
    pack = (pack_col // 64 == pack_row // 8) & (pack_col // 4 % 8 == pack_row % 8)
    pack = jnp.where(pack, 1.0, 0.0).astype(BF)
    packed = []
    for start in range(0, HID, tall):
        span = slice(start, start + tall)
        xh, half = start // tall // 2, start // tall % 2
        for left, right, tile in ((h1, p2_s, 0), (h2, ge_s, 8), (None, x, 10)):
            units = turned(order, p1_s[:, span]) if left is None else left[span, :]
            value = dot_nn(units, right[:, : right.shape[1] // EMB * EMB])
            for part in range(8):
                first, second = slot(part // 2, xh * 2 + part % 2)
                for z in range(4):
                    line = part * 32 + z * 8
                    base = second * (4 * TILES * 8) + (half * 2 + z // 2) * TILES * 8
                    for k in range(0, value.shape[1] // LANES, 2):
                        two = [
                            value[line : line + 8, at * LANES : (at + 1) * LANES] for at in (k, k + 1)
                        ]
                        at = pl.multiple_of(base + (tile + k) * 8, 16)
                        piece = jnp.concatenate(two, axis=0).astype(BF)
                        grads[first * 2 + z % 2, pl.ds(at, 16), :] = piece
            if tile == 10:
                value = jnp.where(wanted, dot_nn(units, x[:, EMB:]), 0.0).astype(BF)
                packed.append(dot_nn(pack, value))
    halves = {}
    for y in range(4):
        for xh in range(2):
            pieces = [packed[2 * xh + half][y * 8 : y * 8 + 8] for half in range(2)]
            for parity in range(2):
                rows = [p[z * 4 + parity * 2 :][:2] for p in pieces for z in range(2)]
                for xl in range(2):
                    halves[y, xh * 2 + xl, parity] = jnp.concatenate(rows, axis=0)
    low = 16 * TILES * 8
    for first in range(4):
        for parity in range(2):
            for pair in (0, 2):
                rows = [
                    jnp.where(role == 0, halves[first, at, parity], halves[at, first, parity])
                    for at in (pair, pair + 1)
                ]
                piece = jnp.concatenate(rows, axis=0).astype(BF)
                grads[first * 2 + parity, low + pair * 8 : low + pair * 8 + 16, :] = piece


def plus(parts, rows):
    value = parts[0, rows, :].astype(F32)
    for k in range(1, parts.shape[0]):
        value = value + parts[k, rows, :].astype(F32)
    return value


def sum_kernel(parts, out):
    height = TILES * 8
    for part in range(16):
        extra = pl.ds(16 * height + part // 8 * 16, 16)
        out[part, :height, :] = plus(parts, pl.ds(part * height, height)).astype(BF)
        out[part, height:, :] = plus(parts, extra).astype(BF)


def split_kernel(place, parts, keep, send, extra):
    role = place[2]
    value = plus(parts, slice(None))
    extra[...] = value[TILES * 8 :]
    for k in range(TILES):
        low, high = value[k * 8 : k * 8 + 4], value[k * 8 + 4 : k * 8 + 8]
        keep[k * 4 : k * 4 + 4, :] = jnp.where(role == 0, low, high)
        send[k * 4 : k * 4 + 4, :] = jnp.where(role == 0, high, low)
    blank = jnp.zeros((8, LANES), F32)
    part = (place[0] * 2 + place[3]) % 2 * 4 + place[1] // 2
    for out, side in ((keep, role), (send, 1 - role)):
        out[TILES * 4 :, :] = blank + extra[pl.ds(part * 2 + side, 1), :]


def last_kernel(place, keep, recv, obs_a, act_a, mid_a, out_a, obs_b, mid_b, out_b):
    role, xl = place[2], place[3]
    sa = jnp.where(role == 0, keep[...], recv[...])
    goal = jnp.where(role == 0, recv[...], keep[...])
    for value, mid, out, obs in ((sa, mid_a, out_a, obs_a), (goal, mid_b, out_b, obs_b)):
        for k in range(TILES):
            target, at = (mid, k) if k < 8 else (out, k - 8) if k < 10 else (obs, k - 10)
            target[:, at * LANES : (at + 1) * LANES] = value[k * 4 : k * 4 + 4]
    line = sa[TILES * 4 : TILES * 4 + 1]
    line = jnp.where(xl == 0, line[:, :64], line[:, 64:])
    for r in range(4):
        act_a[r : r + 1, :] = line[:, r * 16 : r * 16 + 16]


def shifted(value, axis, shift):
    count = lax.axis_size(axis)
    return lax.ppermute(value, axis, [(k, (k + shift) % count) for k in range(count)])


def body(
    observations,
    actions,
    replay_index,
    future_offset,
    sa_obs,
    sa_act,
    sa_mid,
    sa_out,
    goal_obs,
    goal_mid,
    goal_out,
):
    n_z = lax.axis_size("z")
    weights = (sa_obs, sa_act, sa_mid, sa_out, goal_obs, goal_mid, goal_out)
    sa_obs, sa_act, sa_mid, sa_out, goal_obs, goal_mid, goal_out = (
        pltpu.with_memory_space_constraint(weight, pltpu.HBM) for weight in weights
    )
    slabs = (replay_index, future_offset, observations[0], actions[0].T)
    slabs = [pltpu.with_memory_space_constraint(slab, pltpu.HBM) for slab in slabs]
    logit = 3.0 * math.sqrt(EMB)
    coef = logit / (2.0 * lax.axis_size("y") * lax.axis_size("xl"))
    place = jnp.stack([lax.axis_index(axis) for axis in ("xh", "z", "c", "xl")]).astype(jnp.int32)

    acts = actions.shape[2]
    tall = observations.shape[1]
    keep, send = call(
        pick_kernel,
        [shape((ROWS, WIDE), BF)] * 2,
        [SMEM] + [HBM] * 4,
        scratch=[
            pltpu.VMEM((1, ROWS), jnp.int32),
            pltpu.VMEM((1, ROWS), jnp.int32),
            pltpu.VMEM((tall, EMB), BF),
            pltpu.VMEM((acts, tall), BF),
            pltpu.SemaphoreType.DMA((4,)),
        ],
    )(place, *slabs)
    recv = shifted(send, "c", 1)
    x, n1, f1, n2, f2, embed, inv, unit = call(
        forward_kernel,
        [
            shape((CHIP, WIDE), BF),
            shape((CHIP, HID), F32),
            shape((CHIP, 1), F32),
            shape((CHIP, HID), F32),
            shape((CHIP, 1), F32),
            shape((CHIP, EMB), F32),
            shape((CHIP, 1), F32),
            shape((CHIP, EMB), BF),
        ],
        [SMEM, VMEM, VMEM] + [HBM] * 7,
        scratch=[
            pltpu.VMEM((WIDE, HID), BF),
            pltpu.VMEM((HID, HID), BF),
            pltpu.VMEM((HID, EMB), BF),
            pltpu.SemaphoreType.DMA((4,)),
        ],
    )(place, keep, recv, sa_obs, sa_act, sa_mid, sa_out, goal_obs, goal_mid, goal_out)

    def crossed(value, shift):
        hop = [((k + shift) % n_z * 2 + 1 - c) for k in range(n_z) for c in range(2)]
        return lax.ppermute(value, ("z", "c"), list(enumerate(hop)))

    ahead, back = crossed(unit, 1), crossed(unit, -1)
    s1, h1 = slopes(n1)
    s2, h2 = slopes(n2)
    ahead, back, s1, h1, s2, h2, late = lax.optimization_barrier((ahead, back, s1, h1, s2, h2, unit))
    steps = [[ahead, back]]
    for k in range(2, n_z // 2 - 1):
        ahead, back = shifted(ahead, "z", 1), shifted(back, "z", -1)
        steps.append([ahead, back])
    other, theirs = shifted(late, "c", 1), shifted(late, "xh", 1)
    early = [other] + [block for step in steps for block in step]
    ahead, back = shifted(ahead, "z", 1), shifted(back, "z", -1)
    factor = logit * math.log2(math.e)
    expo, part, total = scores(unit, theirs, early, None, False, factor)
    ahead, back, part, total = lax.optimization_barrier((ahead, back, part, total))
    last = [shifted(ahead[:ROWS], "z", 1), shifted(back[ROWS:], "z", -1)]
    expos = [expo]
    for final, step in enumerate(([ahead, back], last)):
        expo, part, total = scores(unit, theirs, step, (part, total), final == 1, factor)
        expos.append(expo)
    blocks = early + [ahead, back] + last
    both = jnp.concatenate([part, shifted(part, "c", 1)], axis=0)
    everyone = jnp.broadcast_to(both[None], (2 * n_z, 16, LANES))
    sums = lax.all_to_all(everyone, ("xh", "z"), 0, 0)
    partial, scaled, across, loss = call(
        functools.partial(send_kernel, n_z, logit),
        [
            shape((CHIP, EMB), BF),
            shape((n_z * CHIP, EMB), BF),
            shape((LANES, LANES), F32),
            shape((1, ROWS), F32),
        ],
        [SMEM] + [VMEM] * (3 + len(expos) + len(blocks)),
        scratch=[pltpu.VMEM((LANES, LANES), F32)],
    )(place, sums, total, unit, *expos, *blocks)
    added = shifted(partial, "xh", 1)
    own = call(
        functools.partial(own_kernel, n_z),
        [shape((CHIP, EMB), F32)],
        [VMEM] * (3 + len(expos)),
        cost=pl.CostEstimate(
            flops=2 * CHIP * n_z * CHIP * EMB,
            bytes_accessed=2 * n_z * CHIP * (CHIP + EMB),
            transcendentals=0,
        ),
    )(total, scaled, across, *expos)[0]
    grads = call(
        functools.partial(backward_kernel, coef),
        [shape((8, 16 * TILES * 8 + 32, LANES), BF)],
        [SMEM] + [VMEM] * 14 + [HBM] * 4,
        scratch=[
            pltpu.VMEM((HID, HID), BF),
            pltpu.VMEM((HID, EMB), BF),
            pltpu.VMEM((CHIP, EMB), BF),
            pltpu.VMEM((CHIP, HID), BF),
            pltpu.VMEM((CHIP, HID), BF),
            pltpu.SemaphoreType.DMA((2,)),
        ],
    )(
        place, own, added, other, embed, inv, n1, f1, s1, h1, n2, f2, s2, h2, x,
        sa_mid, sa_out, goal_mid, goal_out,
    )[0]

    def member(c, first, second, z):
        y, x_at = (first, second) if c == 0 else (second, first)
        return ((c * 4 + y) * 4 + x_at) * n_z + z % n_z

    half = n_z // 2
    near = [
        [member(c, a, b, 2 * q + p if c == 0 or p else 2 * q + 2) for a in range(4) for p in range(2)]
        for c in range(2)
        for b in range(4)
        for q in range(half)
    ]
    far = [
        [member(c, a, b, 2 * q + p) for b in range(4) for q in range(half)]
        for c in range(2)
        for a in range(4)
        for p in range(2)
    ]
    axes = ("c", "y", "xh", "xl", "z")
    grads = lax.all_to_all(grads, axes, 0, 0, axis_index_groups=near)
    grads = call(sum_kernel, [shape((16, TILES * 8 + 16, LANES), BF)], [VMEM])(grads)[0]
    grads = lax.all_to_all(grads, axes, 0, 0, axis_index_groups=far)
    keep, send = call(
        split_kernel,
        [shape((TILES * 4 + 8, LANES), F32)] * 2,
        [SMEM, VMEM],
        scratch=[pltpu.VMEM((16, LANES), F32)],
    )(place, grads)
    recv = shifted(send, "c", 1)
    obs_a, act_a, mid_a, out_a, obs_b, mid_b, out_b = call(
        last_kernel,
        [
            shape((4, EMB), F32),
            shape((4, acts), F32),
            shape((4, HID), F32),
            shape((4, EMB), F32),
            shape((4, EMB), F32),
            shape((4, HID), F32),
            shape((4, EMB), F32),
        ],
        [SMEM] + [VMEM] * 2,
    )(place, keep, recv)
    return (loss, obs_a.T, act_a.T, mid_a, out_a, obs_b.T, mid_b, out_b)


def solution(mesh):
    fine = Mesh(mesh.devices.reshape(2, -1, 2, mesh.shape["dp"] // 2, 2), ("xh", "z", "c", "y", "xl"))
    neg = ("xh", "z", "c")
    dp = ("y", "xl")
    return jax.shard_map(
        body,
        mesh=fine,
        in_specs=(
            P(dp, neg, None),
            P(dp, neg, None),
            P(dp, neg),
            P(dp, neg),
            P(),
            P(),
            P(),
            P(),
            P(),
            P(),
            P(),
        ),
        out_specs=(
            P(dp, neg),
            P(None, neg + dp),
            P(None, neg + dp),
            P(neg + dp, None),
            P(neg + dp, None),
            P(None, neg + dp),
            P(neg + dp, None),
            P(neg + dp, None),
        ),
        check_vma=False,
    )
```

```python
import functools
import math

import jax
import jax.numpy as jnp
from jax import lax
from jax.experimental import pallas as pl
from jax.experimental.pallas import tpu as pltpu
from jax.sharding import Mesh
from jax.sharding import PartitionSpec as P

NORM_EPS = 1e-05
UNIT_EPS = 1e-06
ROWS = 256
CHIP = 512
HID = 1024
EMB = 256
WIDE = 384
TALL = 256
TILES = (HID + 2 * EMB) // 128
LANES = 128
BF = jnp.bfloat16
F32 = jnp.float32
VMEM = pl.BlockSpec(memory_space=pltpu.VMEM)
SMEM = pl.BlockSpec(memory_space=pltpu.SMEM)
HBM = pl.BlockSpec(memory_space=pltpu.HBM)
PARAMS = pltpu.CompilerParams(vmem_limit_bytes=20 * 1024 * 1024)


def shape(dims, dtype):
    return jax.ShapeDtypeStruct(dims, dtype)


def dot_nn(a, b):
    return lax.dot_general(a, b, (((1,), (0,)), ((), ())), preferred_element_type=F32)


def dot_nt(a, b):
    return lax.dot_general(a, b, (((1,), (1,)), ((), ())), preferred_element_type=F32)


def dot_tn(a, b):
    return lax.dot_general(a, b, (((0,), (0,)), ((), ())), preferred_element_type=F32)


def sigmoid(v):
    return 0.5 + 0.5 * jnp.tanh(0.5 * v)


def call(kernel, outs, in_specs, scratch=(), cost=None):
    specs = [VMEM] * len(outs)
    return pl.pallas_call(
        kernel,
        out_shape=outs,
        in_specs=in_specs,
        out_specs=specs,
        scratch_shapes=list(scratch),
        compiler_params=PARAMS,
        cost_estimate=cost,
    )


def pick_kernel(place, replay, offset, obs, act, keep, send, replay_s, offset_s, obs_s, act_s, sems):
    copies = [
        pltpu.make_async_copy(source, target, sems.at[n])
        for n, (source, target) in enumerate(
            ((replay, replay_s), (offset, offset_s), (obs, obs_s), (act, act_s))
        )
    ]
    for copy in copies:
        copy.start()
    for copy in copies:
        copy.wait()
    role = place[2]
    index = replay_s[...]
    ahead = index + offset_s[...]
    spot = lax.broadcasted_iota(jnp.int32, (obs_s.shape[0], ROWS), 0)
    for out, rows in (
        (keep, jnp.where(role == 0, index, ahead)),
        (send, jnp.where(role == 0, ahead, index)),
    ):
        hot = jnp.where(spot == rows, 1.0, 0.0).astype(BF)
        out[:, :EMB] = dot_tn(hot, obs_s[...]).astype(BF)
        extra = dot_nn(act_s[...], hot)
        copies = LANES // extra.shape[0]
        out[:, EMB:] = jnp.concatenate([extra] * copies, axis=0).T.astype(BF)


def by_role(role, pairs, sems):
    for k in range(2):

        @pl.when(role == k)
        def _():
            for n, (sources, target) in enumerate(pairs):
                if sources[k] is not None:
                    pltpu.make_async_copy(sources[k], target, sems.at[n]).start()


def wait_role(role, pairs, sems, first):
    for k in range(2):

        @pl.when(role == k)
        def _():
            for n, (sources, target) in enumerate(pairs):
                if sources[k] is not None:
                    pltpu.make_async_copy(sources[k], target, sems.at[first + n]).wait()


def forward_kernel(
    place, keep, recv, sa_obs, sa_act, sa_mid, sa_out, goal_obs, goal_mid, goal_out,
    x, n1, f1, n2, f2, embed, inv, unit,
    w_first, w_mid, w_out, sems,
):
    role = place[2]
    acts = sa_act.shape[0]
    w_first[EMB:, :] = jnp.zeros((WIDE - EMB, HID), BF)
    pairs = [
        ((sa_obs, goal_obs), w_first.at[pl.ds(0, EMB)]),
        ((sa_act, None), w_first.at[pl.ds(EMB, acts)]),
        ((sa_mid, goal_mid), w_mid),
        ((sa_out, goal_out), w_out),
    ]
    by_role(role, pairs, sems)
    own = pl.multiple_of(role * ROWS, ROWS)
    other = pl.multiple_of((1 - role) * ROWS, ROWS)
    x[pl.ds(own, ROWS), :] = keep[...]
    x[pl.ds(other, ROWS), :] = recv[...]
    for start in range(0, CHIP, ROWS):
        rows = pl.ds(start, ROWS)

        def norm(values, normed, factor):
            center = values - jnp.mean(values, axis=-1, keepdims=True)
            scale = lax.rsqrt(jnp.mean(center * center, axis=-1, keepdims=True) + NORM_EPS)
            v = center * scale
            normed[rows, :] = v
            factor[rows, :] = scale
            return (v * sigmoid(v)).astype(BF)

        if start == 0:
            wait_role(role, pairs[:2], sems, 0)
        h1 = norm(dot_nn(x[rows, :], w_first[...]), n1, f1)
        if start == 0:
            wait_role(role, pairs[2:], sems, 2)
        h2 = norm(dot_nn(h1, w_mid[...]), n2, f2)
        e = dot_nn(h2, w_out[...])
        scale = lax.rsqrt(jnp.mean(e * e, axis=-1, keepdims=True) + UNIT_EPS)
        embed[rows, :] = e
        inv[rows, :] = scale
        unit[rows, :] = (e * scale * EMB ** (-0.5)).astype(BF)


def to_lanes(values):
    return jnp.sum(values.T, axis=0, keepdims=True)


def score_kernel(n_blocks, first, last, factor, *refs):
    refs = list(refs)
    ours, theirs = refs[:2]
    blocks = refs[2 : 2 + n_blocks]
    refs = refs[2 + n_blocks :]
    if not first:
        old_sum, old_total = refs[:2]
        refs = refs[2:]
    expo, part, total = refs[:3]
    for start in range(0, 2 * CHIP, ROWS):
        source = ours if start < CHIP else theirs
        q = source[pl.ds(start % CHIP, ROWS), :]
        rows = pl.ds(start, ROWS)
        acc = None if first else old_total[rows, :]
        sums = None if first else old_sum[rows, :]
        at = 0
        for block in blocks:
            t = block[...]
            width = t.shape[0]
            e = jnp.exp2(dot_nt(q, t) * factor)
            for lane in range(0, width, LANES):
                piece = e[:, lane : lane + LANES]
                sums = piece if sums is None else sums + piece
            e16 = e.astype(BF)
            expo[rows, at : at + width] = e16
            add = dot_nn(e16, t)
            acc = add if acc is None else acc + add
            at += width
        total[rows, :] = acc
        if last:
            for k in range(ROWS // LANES):
                line = start // LANES + k
                part[line : line + 1, :] = to_lanes(sums[k * LANES : (k + 1) * LANES, :])
        else:
            part[rows, :] = sums


def scores(ours, theirs, blocks, prev, last, factor):
    width = sum(b.shape[0] for b in blocks)
    outs = [
        shape((2 * CHIP, width), BF),
        shape((8, LANES) if last else (2 * CHIP, LANES), F32),
        shape((2 * CHIP, EMB), F32),
    ]
    args = [ours, theirs, *blocks] + list(prev or ())
    kernel = functools.partial(score_kernel, len(blocks), prev is None, last, factor)
    cost = pl.CostEstimate(
        flops=4 * 2 * CHIP * width * EMB,
        bytes_accessed=2 * 2 * CHIP * width + 4 * 2 * CHIP * EMB,
        transcendentals=2 * CHIP * width,
    )
    return call(kernel, outs, [VMEM] * len(args), cost=cost)(*args)


def mix_rows(expos, scaled, total, columns, line, start, write):
    acc = None
    at = 0
    for expo in expos:
        width = expo.shape[1]
        add = dot_nn(expo[pl.ds(start, ROWS), :], scaled[pl.ds(at, width), :])
        acc = add if acc is None else acc + add
        at += width
    for k in range(ROWS // LANES):
        here = line + start // LANES + k
        value = total[pl.ds(start + k * LANES, LANES), :] * columns[:, here : here + 1]
        write(start + k * LANES, value + acc[k * LANES : (k + 1) * LANES, :])


def send_kernel(n_z, logit, place, sums, total, ours, *refs):
    n_exp = 3
    expos = refs[:n_exp]
    blocks = refs[n_exp : n_exp + n_z + 1]
    send, scaled, across, loss = refs[n_exp + n_z + 1 : n_exp + n_z + 5]
    lines = refs[n_exp + n_z + 5]
    xh, z, role = place[0], place[1], place[2]

    def full(x_at, z_at, side):
        mine = sums[x_at * n_z + z_at]
        partner = sums[(1 - x_at) * n_z + z_at]
        return mine[side * 8 : side * 8 + 4] + partner[side * 8 + 4 : side * 8 + 8]

    order = [0]
    for k in range(1, n_z // 2):
        order += [n_z - k, k]
    order.append(n_z // 2)
    lines[...] = jnp.ones((LANES, LANES), F32)
    for k, shift in enumerate(order):
        lines[4 * k : 4 * k + 4, :] = 1.0 / full(xh, lax.rem(z + shift, n_z), 1)
    mine = full(xh, z, 0)
    lines[4 * n_z : 4 * n_z + 4, :] = 1.0 / mine
    lines[4 * n_z + 4 : 4 * n_z + 8, :] = 1.0 / full(1 - xh, z, 0)
    columns = lines[...].T
    across[...] = columns

    at = 0
    for block in blocks:
        for start in range(0, block.shape[0], LANES):
            line = at // LANES
            t = block[pl.ds(start, LANES), :].astype(F32)
            scaled[pl.ds(at, LANES), :] = (t * columns[:, line : line + 1]).astype(BF)
            at += LANES

    def write(start, value):
        send[pl.ds(start - CHIP, LANES), :] = value.astype(BF)

    for start in range(CHIP, 2 * CHIP, ROWS):
        mix_rows(expos, scaled, total, columns, 4 * n_z, start, write)

    logs = jnp.log(mine) + jnp.log(full(xh, z, 1))
    logs = jnp.where(role == 0, logs[:2], logs[2:])
    at = pl.multiple_of(role * ROWS, ROWS)
    both = ours[pl.ds(at, ROWS), :].astype(F32) * blocks[0][pl.ds(at, ROWS), :].astype(F32)
    both = both[:, :LANES] + both[:, LANES:]
    for k in range(2):
        positive = logit * to_lanes(both[k * LANES : (k + 1) * LANES, :])
        loss[:, k * LANES : (k + 1) * LANES] = 0.5 * logs[k : k + 1, :] - positive


def own_kernel(n_z, total, scaled, across, *refs):
    expos, own = refs[:-1], refs[-1]
    columns = across[...]

    def write(start, value):
        own[pl.ds(start, LANES), :] = value

    for start in range(0, CHIP, ROWS):
        mix_rows(expos, scaled, total, columns, 4 * n_z, start, write)


def unit_order(tall):
    unit = lax.broadcasted_iota(jnp.int32, (tall, tall), 1)
    origin = (unit // 4 % 8) * 32 + unit // 64 * 8 + (unit // 32 % 2) * 4 + unit % 4
    line = lax.broadcasted_iota(jnp.int32, (tall, tall), 0)
    return jnp.where(line == origin, 1.0, 0.0).astype(BF)


def turned(order, values):
    return lax.dot_general(
        order, values, (((0,), (1,)), ((), ())), preferred_element_type=F32
    ).astype(BF)


def slope_kernel(normed, slope, hidden):
    order = unit_order(TALL)
    for start in range(0, CHIP, ROWS):
        rows = pl.ds(start, ROWS)
        for at in range(0, HID, TALL):
            v = normed[rows, at : at + TALL]
            gate = sigmoid(v)
            h = v * gate
            slope[rows, at : at + TALL] = gate * (1.0 + v - h)
            hidden[at : at + TALL, start : start + ROWS] = turned(order, h.astype(BF))


def slopes(normed):
    cost = pl.CostEstimate(
        flops=2 * CHIP * HID * TALL, bytes_accessed=10 * CHIP * HID, transcendentals=CHIP * HID
    )
    outs = [shape((CHIP, HID), F32), shape((HID, CHIP), BF)]
    return call(slope_kernel, outs, [VMEM], cost=cost)(normed)


def backward_kernel(
    coef, place, own, recv, other, embed, inv, n1, f1, s1, h1, n2, f2, s2, h2, x,
    sa_mid, sa_out, goal_mid, goal_out,
    grads,
    w_mid, w_out, ge_s, p1_s, p2_s, sems,
):
    role = place[2]
    pairs = [((sa_out, goal_out), w_out), ((sa_mid, goal_mid), w_mid)]
    by_role(role, pairs, sems)
    for start in range(0, CHIP, ROWS):
        rows = pl.ds(start, ROWS)
        grad = coef * (
            own[rows, :] + recv[rows, :].astype(F32) - 2.0 * other[rows, :].astype(F32)
        )
        e = embed[rows, :]
        scale = inv[rows, :]
        along = jnp.mean(grad * e, axis=-1, keepdims=True)
        ge = (EMB ** (-0.5) * scale * (grad - e * (scale * scale * along))).astype(BF)
        ge_s[rows, :] = ge

        def step(back, normed, factor, slope, out):
            v = normed[rows, :]
            back = back * slope[rows, :]
            mean = jnp.mean(back, axis=-1, keepdims=True)
            tilt = jnp.mean(back * v, axis=-1, keepdims=True)
            pre = (factor[rows, :] * (back - mean - v * tilt)).astype(BF)
            out[rows, :] = pre
            return pre

        if start == 0:
            wait_role(role, pairs[:1], sems, 0)
        p2 = step(dot_nt(ge, w_out[...]), n2, f2, s2, p2_s)
        if start == 0:
            wait_role(role, pairs[1:], sems, 1)
        step(dot_nt(p2, w_mid[...]), n1, f1, s1, p1_s)
    tall = TALL
    order = unit_order(tall)

    def slot(y, x_at):
        return jnp.where(role == 0, y, x_at), jnp.where(role == 0, x_at, y)

    row = lax.broadcasted_iota(jnp.int32, (tall, LANES), 0)
    lane = lax.broadcasted_iota(jnp.int32, (tall, LANES), 1)
    wanted = lane // 16 == (row // 32 % 2) * 4 + row % 4
    pack_row = lax.broadcasted_iota(jnp.int32, (32, tall), 0)
    pack_col = lax.broadcasted_iota(jnp.int32, (32, tall), 1)
    pack = (pack_col // 64 == pack_row // 8) & (pack_col // 4 % 8 == pack_row % 8)
    pack = jnp.where(pack, 1.0, 0.0).astype(BF)
    packed = []
    for xh in range(2):
        start = xh * CHIP
        for left, right, tile in ((h1, p2_s, 0), (h2, ge_s, 8), (None, x, 10)):
            if left is None:
                spans = [slice(start + half * tall, start + (half + 1) * tall) for half in range(2)]
                units = jnp.concatenate([turned(order, p1_s[:, span]) for span in spans], axis=0)
            else:
                units = left[start : start + CHIP, :]
            value = dot_nn(units, right[:, : right.shape[1] // EMB * EMB])
            for part in range(8):
                first, second = slot(part // 2, xh * 2 + part % 2)
                for z in range(8):
                    line = z // 4 * tall + part * 32 + z % 4 * 8
                    base = second * (4 * TILES * 8) + z // 2 * TILES * 8
                    for k in range(0, value.shape[1] // LANES, 2):
                        two = [
                            value[line : line + 8, at * LANES : (at + 1) * LANES] for at in (k, k + 1)
                        ]
                        at = pl.multiple_of(base + (tile + k) * 8, 16)
                        piece = jnp.concatenate(two, axis=0).astype(BF)
                        grads[first * 2 + z % 2, pl.ds(at, 16), :] = piece
            if tile == 10:
                value = dot_nn(units, x[:, EMB:])
                for half in range(2):
                    mine = jnp.where(wanted, value[half * tall : (half + 1) * tall], 0.0)
                    packed.append(dot_nn(pack, mine.astype(BF)))
    halves = {}
    for y in range(4):
        for xh in range(2):
            pieces = [packed[2 * xh + half][y * 8 : y * 8 + 8] for half in range(2)]
            for parity in range(2):
                rows = [p[z * 4 + parity * 2 :][:2] for p in pieces for z in range(2)]
                for xl in range(2):
                    halves[y, xh * 2 + xl, parity] = jnp.concatenate(rows, axis=0)
    low = 16 * TILES * 8
    for first in range(4):
        for parity in range(2):
            for pair in (0, 2):
                rows = [
                    jnp.where(role == 0, halves[first, at, parity], halves[at, first, parity])
                    for at in (pair, pair + 1)
                ]
                piece = jnp.concatenate(rows, axis=0).astype(BF)
                grads[first * 2 + parity, low + pair * 8 : low + pair * 8 + 16, :] = piece


def plus(parts, rows):
    value = parts[0, rows, :].astype(F32)
    for k in range(1, parts.shape[0]):
        value = value + parts[k, rows, :].astype(F32)
    return value


def sum_kernel(parts, out):
    height = TILES * 8
    for part in range(16):
        extra = pl.ds(16 * height + part // 8 * 16, 16)
        out[part, :height, :] = plus(parts, pl.ds(part * height, height)).astype(BF)
        out[part, height:, :] = plus(parts, extra).astype(BF)


def split_kernel(place, parts, keep, send, extra):
    role = place[2]
    value = plus(parts, slice(None))
    extra[...] = value[TILES * 8 :]
    for k in range(TILES):
        low, high = value[k * 8 : k * 8 + 4], value[k * 8 + 4 : k * 8 + 8]
        keep[k * 4 : k * 4 + 4, :] = jnp.where(role == 0, low, high)
        send[k * 4 : k * 4 + 4, :] = jnp.where(role == 0, high, low)
    blank = jnp.zeros((8, LANES), F32)
    part = (place[0] * 2 + place[3]) % 2 * 4 + place[1] // 2
    for out, side in ((keep, role), (send, 1 - role)):
        out[TILES * 4 :, :] = blank + extra[pl.ds(part * 2 + side, 1), :]


def last_kernel(place, keep, recv, obs_a, act_a, mid_a, out_a, obs_b, mid_b, out_b):
    role, xl = place[2], place[3]
    sa = jnp.where(role == 0, keep[...], recv[...])
    goal = jnp.where(role == 0, recv[...], keep[...])
    for value, mid, out, obs in ((sa, mid_a, out_a, obs_a), (goal, mid_b, out_b, obs_b)):
        for k in range(TILES):
            target, at = (mid, k) if k < 8 else (out, k - 8) if k < 10 else (obs, k - 10)
            target[:, at * LANES : (at + 1) * LANES] = value[k * 4 : k * 4 + 4]
    line = sa[TILES * 4 : TILES * 4 + 1]
    line = jnp.where(xl == 0, line[:, :64], line[:, 64:])
    for r in range(4):
        act_a[r : r + 1, :] = line[:, r * 16 : r * 16 + 16]


def shifted(value, axis, shift):
    count = lax.axis_size(axis)
    return lax.ppermute(value, axis, [(k, (k + shift) % count) for k in range(count)])


def body(
    observations,
    actions,
    replay_index,
    future_offset,
    sa_obs,
    sa_act,
    sa_mid,
    sa_out,
    goal_obs,
    goal_mid,
    goal_out,
):
    n_z = lax.axis_size("z")
    weights = (sa_obs, sa_act, sa_mid, sa_out, goal_obs, goal_mid, goal_out)
    sa_obs, sa_act, sa_mid, sa_out, goal_obs, goal_mid, goal_out = (
        pltpu.with_memory_space_constraint(weight, pltpu.HBM) for weight in weights
    )
    slabs = (replay_index, future_offset, observations[0], actions[0].T)
    slabs = [pltpu.with_memory_space_constraint(slab, pltpu.HBM) for slab in slabs]
    logit = 3.0 * math.sqrt(EMB)
    coef = logit / (2.0 * lax.axis_size("y") * lax.axis_size("xl"))
    place = jnp.stack([lax.axis_index(axis) for axis in ("xh", "z", "c", "xl")]).astype(jnp.int32)

    acts = actions.shape[2]
    tall = observations.shape[1]
    keep, send = call(
        pick_kernel,
        [shape((ROWS, WIDE), BF)] * 2,
        [SMEM] + [HBM] * 4,
        scratch=[
            pltpu.VMEM((1, ROWS), jnp.int32),
            pltpu.VMEM((1, ROWS), jnp.int32),
            pltpu.VMEM((tall, EMB), BF),
            pltpu.VMEM((acts, tall), BF),
            pltpu.SemaphoreType.DMA((4,)),
        ],
    )(place, *slabs)
    recv = shifted(send, "c", 1)
    x, n1, f1, n2, f2, embed, inv, unit = call(
        forward_kernel,
        [
            shape((CHIP, WIDE), BF),
            shape((CHIP, HID), F32),
            shape((CHIP, 1), F32),
            shape((CHIP, HID), F32),
            shape((CHIP, 1), F32),
            shape((CHIP, EMB), F32),
            shape((CHIP, 1), F32),
            shape((CHIP, EMB), BF),
        ],
        [SMEM, VMEM, VMEM] + [HBM] * 7,
        scratch=[
            pltpu.VMEM((WIDE, HID), BF),
            pltpu.VMEM((HID, HID), BF),
            pltpu.VMEM((HID, EMB), BF),
            pltpu.SemaphoreType.DMA((4,)),
        ],
    )(place, keep, recv, sa_obs, sa_act, sa_mid, sa_out, goal_obs, goal_mid, goal_out)

    def crossed(value, shift):
        hop = [((k + shift) % n_z * 2 + 1 - c) for k in range(n_z) for c in range(2)]
        return lax.ppermute(value, ("z", "c"), list(enumerate(hop)))

    ahead, back = crossed(unit, 1), crossed(unit, -1)
    s1, h1 = slopes(n1)
    s2, h2 = slopes(n2)
    back, ahead, s1, h1, s2, h2, late = lax.optimization_barrier((back, ahead, s1, h1, s2, h2, unit))
    steps = [[ahead, back]]
    for k in range(2, n_z // 2 - 1):
        ahead, back = shifted(ahead, "z", 1), shifted(back, "z", -1)
        steps.append([ahead, back])
    other, theirs = shifted(late, "c", 1), shifted(late, "xh", 1)
    early = [other] + [block for step in steps for block in step]
    ahead, back = shifted(ahead, "z", 1), shifted(back, "z", -1)
    factor = logit * math.log2(math.e)
    expo, part, total = scores(unit, theirs, early, None, False, factor)
    ahead, back, part, total = lax.optimization_barrier((ahead, back, part, total))
    last = [shifted(back[:ROWS], "z", -1), shifted(ahead[ROWS:], "z", 1)]
    expos = [expo]
    for final, step in enumerate(([ahead, back], last)):
        expo, part, total = scores(unit, theirs, step, (part, total), final == 1, factor)
        expos.append(expo)
    blocks = early + [ahead, back] + last
    both = jnp.concatenate([part, shifted(part, "c", 1)], axis=0)
    everyone = jnp.broadcast_to(both[None], (2 * n_z, 16, LANES))
    sums = lax.all_to_all(everyone, ("xh", "z"), 0, 0)
    partial, scaled, across, loss = call(
        functools.partial(send_kernel, n_z, logit),
        [
            shape((CHIP, EMB), BF),
            shape((n_z * CHIP, EMB), BF),
            shape((LANES, LANES), F32),
            shape((1, ROWS), F32),
        ],
        [SMEM] + [VMEM] * (3 + len(expos) + len(blocks)),
        scratch=[pltpu.VMEM((LANES, LANES), F32)],
    )(place, sums, total, unit, *expos, *blocks)
    added = shifted(partial, "xh", 1)
    own = call(
        functools.partial(own_kernel, n_z),
        [shape((CHIP, EMB), F32)],
        [VMEM] * (3 + len(expos)),
        cost=pl.CostEstimate(
            flops=2 * CHIP * n_z * CHIP * EMB,
            bytes_accessed=2 * n_z * CHIP * (CHIP + EMB),
            transcendentals=0,
        ),
    )(total, scaled, across, *expos)[0]
    grads = call(
        functools.partial(backward_kernel, coef),
        [shape((8, 16 * TILES * 8 + 32, LANES), BF)],
        [SMEM] + [VMEM] * 14 + [HBM] * 4,
        scratch=[
            pltpu.VMEM((HID, HID), BF),
            pltpu.VMEM((HID, EMB), BF),
            pltpu.VMEM((CHIP, EMB), BF),
            pltpu.VMEM((CHIP, HID), BF),
            pltpu.VMEM((CHIP, HID), BF),
            pltpu.SemaphoreType.DMA((2,)),
        ],
    )(
        place, own, added, other, embed, inv, n1, f1, s1, h1, n2, f2, s2, h2, x,
        sa_mid, sa_out, goal_mid, goal_out,
    )[0]

    def member(c, first, second, z):
        y, x_at = (first, second) if c == 0 else (second, first)
        return ((c * 4 + y) * 4 + x_at) * n_z + z % n_z

    half = n_z // 2
    near = [
        [member(c, a, b, 2 * q + p if c == 0 or p else 2 * q + 2) for a in range(4) for p in range(2)]
        for c in range(2)
        for b in range(4)
        for q in range(half)
    ]
    far = [
        [member(c, a, b, 2 * q + p) for b in range(4) for q in range(half)]
        for c in range(2)
        for a in range(4)
        for p in range(2)
    ]
    axes = ("c", "y", "xh", "xl", "z")
    grads = lax.all_to_all(grads, axes, 0, 0, axis_index_groups=near)
    grads = call(sum_kernel, [shape((16, TILES * 8 + 16, LANES), BF)], [VMEM])(grads)[0]
    grads = lax.all_to_all(grads, axes, 0, 0, axis_index_groups=far)
    keep, send = call(
        split_kernel,
        [shape((TILES * 4 + 8, LANES), F32)] * 2,
        [SMEM, VMEM],
        scratch=[pltpu.VMEM((16, LANES), F32)],
    )(place, grads)
    recv = shifted(send, "c", 1)
    obs_a, act_a, mid_a, out_a, obs_b, mid_b, out_b = call(
        last_kernel,
        [
            shape((4, EMB), F32),
            shape((4, acts), F32),
            shape((4, HID), F32),
            shape((4, EMB), F32),
            shape((4, EMB), F32),
            shape((4, HID), F32),
            shape((4, EMB), F32),
        ],
        [SMEM] + [VMEM] * 2,
    )(place, keep, recv)
    return (loss, obs_a.T, act_a.T, mid_a, out_a, obs_b.T, mid_b, out_b)


def solution(mesh):
    fine = Mesh(mesh.devices.reshape(2, -1, 2, mesh.shape["dp"] // 2, 2), ("xh", "z", "c", "y", "xl"))
    neg = ("xh", "z", "c")
    dp = ("y", "xl")
    return jax.shard_map(
        body,
        mesh=fine,
        in_specs=(
            P(dp, neg, None),
            P(dp, neg, None),
            P(dp, neg),
            P(dp, neg),
            P(),
            P(),
            P(),
            P(),
            P(),
            P(),
            P(),
        ),
        out_specs=(
            P(dp, neg),
            P(None, neg + dp),
            P(None, neg + dp),
            P(neg + dp, None),
            P(neg + dp, None),
            P(None, neg + dp),
            P(neg + dp, None),
            P(neg + dp, None),
        ),
        check_vma=False,
    )
```

```python
import functools
import math

import jax
import jax.numpy as jnp
from jax import lax
from jax.experimental import pallas as pl
from jax.experimental.pallas import tpu as pltpu
from jax.sharding import Mesh
from jax.sharding import PartitionSpec as P

NORM_EPS = 1e-05
UNIT_EPS = 1e-06
ROWS = 256
CHIP = 512
HID = 1024
EMB = 256
WIDE = 384
TALL = 256
TILES = (HID + 2 * EMB) // 128
LANES = 128
BF = jnp.bfloat16
F32 = jnp.float32
VMEM = pl.BlockSpec(memory_space=pltpu.VMEM)
SMEM = pl.BlockSpec(memory_space=pltpu.SMEM)
HBM = pl.BlockSpec(memory_space=pltpu.HBM)
PARAMS = pltpu.CompilerParams(vmem_limit_bytes=20 * 1024 * 1024)


def shape(dims, dtype):
    return jax.ShapeDtypeStruct(dims, dtype)


def dot_nn(a, b):
    return lax.dot_general(a, b, (((1,), (0,)), ((), ())), preferred_element_type=F32)


def dot_nt(a, b):
    return lax.dot_general(a, b, (((1,), (1,)), ((), ())), preferred_element_type=F32)


def dot_tn(a, b):
    return lax.dot_general(a, b, (((0,), (0,)), ((), ())), preferred_element_type=F32)


def sigmoid(v):
    return 0.5 + 0.5 * jnp.tanh(0.5 * v)


def call(kernel, outs, in_specs, scratch=(), cost=None):
    specs = [VMEM] * len(outs)
    return pl.pallas_call(
        kernel,
        out_shape=outs,
        in_specs=in_specs,
        out_specs=specs,
        scratch_shapes=list(scratch),
        compiler_params=PARAMS,
        cost_estimate=cost,
    )


def pick_kernel(place, replay, offset, obs, act, keep, send, replay_s, offset_s, obs_s, act_s, sems):
    copies = [
        pltpu.make_async_copy(source, target, sems.at[n])
        for n, (source, target) in enumerate(
            ((replay, replay_s), (offset, offset_s), (obs, obs_s), (act, act_s))
        )
    ]
    for copy in copies:
        copy.start()
    for copy in copies:
        copy.wait()
    role = place[2]
    index = replay_s[...]
    ahead = index + offset_s[...]
    spot = lax.broadcasted_iota(jnp.int32, (obs_s.shape[0], ROWS), 0)
    for out, rows in (
        (keep, jnp.where(role == 0, index, ahead)),
        (send, jnp.where(role == 0, ahead, index)),
    ):
        hot = jnp.where(spot == rows, 1.0, 0.0).astype(BF)
        out[:, :EMB] = dot_tn(hot, obs_s[...]).astype(BF)
        extra = dot_nn(act_s[...], hot)
        copies = LANES // extra.shape[0]
        out[:, EMB:] = jnp.concatenate([extra] * copies, axis=0).T.astype(BF)


def by_role(role, pairs, sems):
    for k in range(2):

        @pl.when(role == k)
        def _():
            for n, (sources, target) in enumerate(pairs):
                if sources[k] is not None:
                    pltpu.make_async_copy(sources[k], target, sems.at[n]).start()


def wait_role(role, pairs, sems, first):
    for k in range(2):

        @pl.when(role == k)
        def _():
            for n, (sources, target) in enumerate(pairs):
                if sources[k] is not None:
                    pltpu.make_async_copy(sources[k], target, sems.at[first + n]).wait()


def forward_kernel(
    place, keep, recv, sa_obs, sa_act, sa_mid, sa_out, goal_obs, goal_mid, goal_out,
    x, n1, f1, n2, f2, embed, inv, unit,
    w_first, w_mid, w_out, sems,
):
    role = place[2]
    acts = sa_act.shape[0]
    w_first[EMB:, :] = jnp.zeros((WIDE - EMB, HID), BF)
    pairs = [
        ((sa_obs, goal_obs), w_first.at[pl.ds(0, EMB)]),
        ((sa_act, None), w_first.at[pl.ds(EMB, acts)]),
        ((sa_mid, goal_mid), w_mid),
        ((sa_out, goal_out), w_out),
    ]
    by_role(role, pairs, sems)
    own = pl.multiple_of(role * ROWS, ROWS)
    other = pl.multiple_of((1 - role) * ROWS, ROWS)
    x[pl.ds(own, ROWS), :] = keep[...]
    x[pl.ds(other, ROWS), :] = recv[...]
    for start in range(0, CHIP, CHIP):
        rows = pl.ds(start, CHIP)

        def norm(values, normed, factor):
            center = values - jnp.mean(values, axis=-1, keepdims=True)
            scale = lax.rsqrt(jnp.mean(center * center, axis=-1, keepdims=True) + NORM_EPS)
            v = center * scale
            normed[rows, :] = v
            factor[rows, :] = scale
            return (v * sigmoid(v)).astype(BF)

        if start == 0:
            wait_role(role, pairs[:2], sems, 0)
        h1 = norm(dot_nn(x[rows, :], w_first[...]), n1, f1)
        if start == 0:
            wait_role(role, pairs[2:], sems, 2)
        h2 = norm(dot_nn(h1, w_mid[...]), n2, f2)
        e = dot_nn(h2, w_out[...])
        scale = lax.rsqrt(jnp.mean(e * e, axis=-1, keepdims=True) + UNIT_EPS)
        embed[rows, :] = e
        inv[rows, :] = scale
        unit[rows, :] = (e * scale * EMB ** (-0.5)).astype(BF)


def to_lanes(values):
    return jnp.sum(values.T, axis=0, keepdims=True)


def ring_order(n_z):
    order = [0, n_z - 1, 1]
    for k in range(2, n_z // 2):
        order += [n_z - k, k]
    return order + [n_z // 2]


def score_kernel(n_blocks, first, last, factor, place, *refs):
    refs = list(refs)
    ours, theirs = refs[:2]
    blocks = refs[2 : 2 + n_blocks]
    refs = refs[2 + n_blocks :]
    if not first:
        old_sum, old_total = refs[:2]
        refs = refs[2:]
    if last:
        old_columns = refs[:-4]
        refs = refs[-4:]
    expo, part, total, columns = refs
    down = [None] * n_blocks
    for start in range(0, 2 * CHIP, ROWS):
        source = ours if start < CHIP else theirs
        q = source[pl.ds(start % CHIP, ROWS), :]
        rows = pl.ds(start, ROWS)
        acc = None if first else old_total[rows, :]
        sums = None if first else old_sum[rows, :]
        at = 0
        for n, block in enumerate(blocks):
            t = block[...]
            width = t.shape[0]
            e = jnp.exp2(dot_nt(q, t) * factor)
            for lane in range(0, width, LANES):
                piece = e[:, lane : lane + LANES]
                sums = piece if sums is None else sums + piece
            fold = jnp.sum(e.reshape(ROWS // 8, 8, width), axis=0)
            down[n] = fold if down[n] is None else down[n] + fold
            e16 = e.astype(BF)
            expo[rows, at : at + width] = e16
            add = dot_nn(e16, t)
            acc = add if acc is None else acc + add
            at += width
        total[rows, :] = acc
        if last:
            for k in range(ROWS // LANES):
                line = start // LANES + k
                part[line : line + 1, :] = to_lanes(sums[k * LANES : (k + 1) * LANES, :])
        else:
            part[rows, :] = sums
    lines = []
    for fold in down:
        whole = jnp.sum(fold, axis=0, keepdims=True)
        lines += [whole[:, k : k + LANES] for k in range(0, whole.shape[1], LANES)]
    if last:
        n_z = columns.shape[0]
        held = [ref[k : k + 4, :] for ref in old_columns for k in range(0, ref.shape[0], 4)]
        held.append(jnp.concatenate(lines, axis=0))
        for shift, value in zip(ring_order(n_z), held):
            columns[lax.rem(place[1] + shift, n_z)] = value
    else:
        for k, line in enumerate(lines):
            columns[k : k + 1, :] = line


def scores(place, ours, theirs, blocks, prev, held, factor):
    width = sum(b.shape[0] for b in blocks)
    last = held is not None
    lines = (2 * sum(c.shape[0] for c in held) + 2 * width // LANES) // 8 if last else width // LANES
    outs = [
        shape((2 * CHIP, width), BF),
        shape((8, LANES) if last else (2 * CHIP, LANES), F32),
        shape((2 * CHIP, EMB), F32),
        shape((lines, 4, LANES) if last else (lines, LANES), F32),
    ]
    args = [place, ours, theirs, *blocks] + list(prev or ()) + list(held or ())
    kernel = functools.partial(score_kernel, len(blocks), prev is None, last, factor)
    cost = pl.CostEstimate(
        flops=4 * 2 * CHIP * width * EMB,
        bytes_accessed=2 * 2 * CHIP * width + 4 * 2 * CHIP * EMB,
        transcendentals=2 * CHIP * width,
    )
    return call(kernel, outs, [SMEM] + [VMEM] * (len(args) - 1), cost=cost)(*args)


def mix_rows(expos, scaled, total, columns, line, start, write):
    acc = None
    at = 0
    for expo in expos:
        width = expo.shape[1]
        add = dot_nn(expo[pl.ds(start, ROWS), :], scaled[pl.ds(at, width), :])
        acc = add if acc is None else acc + add
        at += width
    for k in range(ROWS // LANES):
        here = line + start // LANES + k
        value = total[pl.ds(start + k * LANES, LANES), :] * columns[:, here : here + 1]
        write(start + k * LANES, value + acc[k * LANES : (k + 1) * LANES, :])


def send_kernel(n_z, logit, place, sums, part, partner, total, ours, *refs):
    n_exp = 3
    expos = refs[:n_exp]
    blocks = refs[n_exp : n_exp + n_z + 1]
    send, scaled, across, loss = refs[n_exp + n_z + 1 : n_exp + n_z + 5]
    lines, whole = refs[n_exp + n_z + 5 :]
    z, role = place[1], place[2]
    column = sums[0]
    for k in range(1, n_z):
        column = column + sums[k]
    whole[...] = column
    mine = part[:4, :] + partner[4:, :]
    theirs = part[4:, :] + partner[:4, :]
    lines[...] = jnp.ones((LANES, LANES), F32)
    for k, shift in enumerate(ring_order(n_z)):
        lines[4 * k : 4 * k + 4, :] = 1.0 / whole[lax.rem(z + shift, n_z)]
    lines[4 * n_z : 4 * n_z + 4, :] = 1.0 / mine
    lines[4 * n_z + 4 : 4 * n_z + 8, :] = 1.0 / theirs
    columns = lines[...].T
    across[...] = columns

    at = 0
    for block in blocks:
        for start in range(0, block.shape[0], LANES):
            line = at // LANES
            t = block[pl.ds(start, LANES), :].astype(F32)
            scaled[pl.ds(at, LANES), :] = (t * columns[:, line : line + 1]).astype(BF)
            at += LANES

    def write(start, value):
        send[pl.ds(start - CHIP, LANES), :] = value.astype(BF)

    for start in range(CHIP, 2 * CHIP, ROWS):
        mix_rows(expos, scaled, total, columns, 4 * n_z, start, write)

    logs = jnp.log(mine) + jnp.log(whole[z])
    logs = jnp.where(role == 0, logs[:2], logs[2:])
    at = pl.multiple_of(role * ROWS, ROWS)
    both = ours[pl.ds(at, ROWS), :].astype(F32) * blocks[0][pl.ds(at, ROWS), :].astype(F32)
    both = both[:, :LANES] + both[:, LANES:]
    for k in range(2):
        positive = logit * to_lanes(both[k * LANES : (k + 1) * LANES, :])
        loss[:, k * LANES : (k + 1) * LANES] = 0.5 * logs[k : k + 1, :] - positive


def own_kernel(n_z, total, scaled, across, *refs):
    expos, own = refs[:-1], refs[-1]
    columns = across[...]

    def write(start, value):
        own[pl.ds(start, LANES), :] = value

    for start in range(0, CHIP, ROWS):
        mix_rows(expos, scaled, total, columns, 4 * n_z, start, write)


def unit_order(tall):
    unit = lax.broadcasted_iota(jnp.int32, (tall, tall), 1)
    origin = (unit // 4 % 8) * 32 + unit // 64 * 8 + (unit // 32 % 2) * 4 + unit % 4
    line = lax.broadcasted_iota(jnp.int32, (tall, tall), 0)
    return jnp.where(line == origin, 1.0, 0.0).astype(BF)


def turned(order, values):
    return lax.dot_general(
        order, values, (((0,), (1,)), ((), ())), preferred_element_type=F32
    ).astype(BF)


def slope_kernel(normed, slope, hidden):
    order = unit_order(TALL)
    for start in range(0, CHIP, ROWS):
        rows = pl.ds(start, ROWS)
        for at in range(0, HID, TALL):
            v = normed[rows, at : at + TALL]
            gate = sigmoid(v)
            h = v * gate
            slope[rows, at : at + TALL] = gate * (1.0 + v - h)
            hidden[at : at + TALL, start : start + ROWS] = turned(order, h.astype(BF))


def slopes(normed):
    cost = pl.CostEstimate(
        flops=2 * CHIP * HID * TALL, bytes_accessed=10 * CHIP * HID, transcendentals=CHIP * HID
    )
    outs = [shape((CHIP, HID), F32), shape((HID, CHIP), BF)]
    return call(slope_kernel, outs, [VMEM], cost=cost)(normed)


def backward_kernel(
    coef, place, own, recv, other, embed, inv, n1, f1, s1, h1, n2, f2, s2, h2, x,
    sa_mid, sa_out, goal_mid, goal_out,
    grads,
    w_mid, w_out, ge_s, p1_s, p2_s, sems,
):
    role = place[2]
    pairs = [((sa_out, goal_out), w_out), ((sa_mid, goal_mid), w_mid)]
    by_role(role, pairs, sems)
    for start in range(0, CHIP, CHIP):
        rows = pl.ds(start, CHIP)
        grad = coef * (
            own[rows, :] + recv[rows, :].astype(F32) - 2.0 * other[rows, :].astype(F32)
        )
        e = embed[rows, :]
        scale = inv[rows, :]
        along = jnp.mean(grad * e, axis=-1, keepdims=True)
        ge = (EMB ** (-0.5) * scale * (grad - e * (scale * scale * along))).astype(BF)
        ge_s[rows, :] = ge

        def step(back, normed, factor, slope, out):
            v = normed[rows, :]
            back = back * slope[rows, :]
            mean = jnp.mean(back, axis=-1, keepdims=True)
            tilt = jnp.mean(back * v, axis=-1, keepdims=True)
            pre = (factor[rows, :] * (back - mean - v * tilt)).astype(BF)
            out[rows, :] = pre
            return pre

        if start == 0:
            wait_role(role, pairs[:1], sems, 0)
        p2 = step(dot_nt(ge, w_out[...]), n2, f2, s2, p2_s)
        if start == 0:
            wait_role(role, pairs[1:], sems, 1)
        step(dot_nt(p2, w_mid[...]), n1, f1, s1, p1_s)
    tall = TALL
    order = unit_order(tall)

    def slot(y, x_at):
        return jnp.where(role == 0, y, x_at), jnp.where(role == 0, x_at, y)

    row = lax.broadcasted_iota(jnp.int32, (tall, LANES), 0)
    lane = lax.broadcasted_iota(jnp.int32, (tall, LANES), 1)
    wanted = lane // 16 == (row // 32 % 2) * 4 + row % 4
    pack_row = lax.broadcasted_iota(jnp.int32, (32, tall), 0)
    pack_col = lax.broadcasted_iota(jnp.int32, (32, tall), 1)
    pack = (pack_col // 64 == pack_row // 8) & (pack_col // 4 % 8 == pack_row % 8)
    pack = jnp.where(pack, 1.0, 0.0).astype(BF)
    packed = []
    for xh in range(2):
        start = xh * CHIP
        for left, right, tile in ((h1, p2_s, 0), (h2, ge_s, 8), (None, x, 10)):
            if left is None:
                spans = [slice(start + half * tall, start + (half + 1) * tall) for half in range(2)]
                units = jnp.concatenate([turned(order, p1_s[:, span]) for span in spans], axis=0)
            else:
                units = left[start : start + CHIP, :]
            value = dot_nn(units, right[:, : right.shape[1] // EMB * EMB])
            for part in range(8):
                first, second = slot(part // 2, xh * 2 + part % 2)
                for z in range(8):
                    line = z // 4 * tall + part * 32 + z % 4 * 8
                    base = second * (4 * TILES * 8) + z // 2 * TILES * 8
                    for k in range(0, value.shape[1] // LANES, 2):
                        two = [
                            value[line : line + 8, at * LANES : (at + 1) * LANES] for at in (k, k + 1)
                        ]
                        at = pl.multiple_of(base + (tile + k) * 8, 16)
                        piece = jnp.concatenate(two, axis=0).astype(BF)
                        grads[first * 2 + z % 2, pl.ds(at, 16), :] = piece
            if tile == 10:
                value = dot_nn(units, x[:, EMB:])
                for half in range(2):
                    mine = jnp.where(wanted, value[half * tall : (half + 1) * tall], 0.0)
                    packed.append(dot_nn(pack, mine.astype(BF)))
    halves = {}
    for y in range(4):
        for xh in range(2):
            pieces = [packed[2 * xh + half][y * 8 : y * 8 + 8] for half in range(2)]
            for parity in range(2):
                rows = [p[z * 4 + parity * 2 :][:2] for p in pieces for z in range(2)]
                for xl in range(2):
                    halves[y, xh * 2 + xl, parity] = jnp.concatenate(rows, axis=0)
    low = 16 * TILES * 8
    for first in range(4):
        for parity in range(2):
            for pair in (0, 2):
                rows = [
                    jnp.where(role == 0, halves[first, at, parity], halves[at, first, parity])
                    for at in (pair, pair + 1)
                ]
                piece = jnp.concatenate(rows, axis=0).astype(BF)
                grads[first * 2 + parity, low + pair * 8 : low + pair * 8 + 16, :] = piece


def plus(parts, rows):
    value = parts[0, rows, :].astype(F32)
    for k in range(1, parts.shape[0]):
        value = value + parts[k, rows, :].astype(F32)
    return value


def sum_kernel(parts, out):
    height = TILES * 8
    for part in range(16):
        extra = pl.ds(16 * height + part // 8 * 16, 16)
        out[part, :height, :] = plus(parts, pl.ds(part * height, height)).astype(BF)
        out[part, height:, :] = plus(parts, extra).astype(BF)


def split_kernel(place, parts, keep, send, extra):
    role = place[2]
    value = plus(parts, slice(None))
    extra[...] = value[TILES * 8 :]
    for k in range(TILES):
        low, high = value[k * 8 : k * 8 + 4], value[k * 8 + 4 : k * 8 + 8]
        keep[k * 4 : k * 4 + 4, :] = jnp.where(role == 0, low, high)
        send[k * 4 : k * 4 + 4, :] = jnp.where(role == 0, high, low)
    blank = jnp.zeros((8, LANES), F32)
    part = (place[0] * 2 + place[3]) % 2 * 4 + place[1] // 2
    for out, side in ((keep, role), (send, 1 - role)):
        out[TILES * 4 :, :] = blank + extra[pl.ds(part * 2 + side, 1), :]


def last_kernel(place, keep, recv, obs_a, act_a, mid_a, out_a, obs_b, mid_b, out_b):
    role, xl = place[2], place[3]
    sa = jnp.where(role == 0, keep[...], recv[...])
    goal = jnp.where(role == 0, recv[...], keep[...])
    for value, mid, out, obs in ((sa, mid_a, out_a, obs_a), (goal, mid_b, out_b, obs_b)):
        for k in range(TILES):
            target, at = (mid, k) if k < 8 else (out, k - 8) if k < 10 else (obs, k - 10)
            target[:, at * LANES : (at + 1) * LANES] = value[k * 4 : k * 4 + 4]
    line = sa[TILES * 4 : TILES * 4 + 1]
    line = jnp.where(xl == 0, line[:, :64], line[:, 64:])
    for r in range(4):
        act_a[r : r + 1, :] = line[:, r * 16 : r * 16 + 16]


def shifted(value, axis, shift):
    count = lax.axis_size(axis)
    return lax.ppermute(value, axis, [(k, (k + shift) % count) for k in range(count)])


def body(
    observations,
    actions,
    replay_index,
    future_offset,
    sa_obs,
    sa_act,
    sa_mid,
    sa_out,
    goal_obs,
    goal_mid,
    goal_out,
):
    n_z = lax.axis_size("z")
    weights = (sa_obs, sa_act, sa_mid, sa_out, goal_obs, goal_mid, goal_out)
    sa_obs, sa_act, sa_mid, sa_out, goal_obs, goal_mid, goal_out = (
        pltpu.with_memory_space_constraint(weight, pltpu.HBM) for weight in weights
    )
    slabs = (replay_index, future_offset, observations[0], actions[0].T)
    slabs = [pltpu.with_memory_space_constraint(slab, pltpu.HBM) for slab in slabs]
    logit = 3.0 * math.sqrt(EMB)
    coef = logit / (2.0 * lax.axis_size("y") * lax.axis_size("xl"))
    place = jnp.stack([lax.axis_index(axis) for axis in ("xh", "z", "c", "xl")]).astype(jnp.int32)

    acts = actions.shape[2]
    tall = observations.shape[1]
    keep, send = call(
        pick_kernel,
        [shape((ROWS, WIDE), BF)] * 2,
        [SMEM] + [HBM] * 4,
        scratch=[
            pltpu.VMEM((1, ROWS), jnp.int32),
            pltpu.VMEM((1, ROWS), jnp.int32),
            pltpu.VMEM((tall, EMB), BF),
            pltpu.VMEM((acts, tall), BF),
            pltpu.SemaphoreType.DMA((4,)),
        ],
    )(place, *slabs)
    recv = shifted(send, "c", 1)
    x, n1, f1, n2, f2, embed, inv, unit = call(
        forward_kernel,
        [
            shape((CHIP, WIDE), BF),
            shape((CHIP, HID), F32),
            shape((CHIP, 1), F32),
            shape((CHIP, HID), F32),
            shape((CHIP, 1), F32),
            shape((CHIP, EMB), F32),
            shape((CHIP, 1), F32),
            shape((CHIP, EMB), BF),
        ],
        [SMEM, VMEM, VMEM] + [HBM] * 7,
        scratch=[
            pltpu.VMEM((WIDE, HID), BF),
            pltpu.VMEM((HID, HID), BF),
            pltpu.VMEM((HID, EMB), BF),
            pltpu.SemaphoreType.DMA((4,)),
        ],
    )(place, keep, recv, sa_obs, sa_act, sa_mid, sa_out, goal_obs, goal_mid, goal_out)

    def crossed(value, shift):
        hop = [((k + shift) % n_z * 2 + 1 - c) for k in range(n_z) for c in range(2)]
        return lax.ppermute(value, ("z", "c"), list(enumerate(hop)))

    ahead, back = crossed(unit, 1), crossed(unit, -1)
    s1, h1 = slopes(n1)
    s2, h2 = slopes(n2)
    back, ahead, s1, h1, s2, h2, late = lax.optimization_barrier((back, ahead, s1, h1, s2, h2, unit))
    steps = [[ahead, back]]
    for k in range(2, n_z // 2 - 1):
        ahead, back = shifted(ahead, "z", 1), shifted(back, "z", -1)
        steps.append([ahead, back])
    other, theirs = shifted(late, "c", 1), shifted(late, "xh", 1)
    early = [other] + [block for step in steps for block in step]
    ahead, back = shifted(ahead, "z", 1), shifted(back, "z", -1)
    factor = logit * math.log2(math.e)
    expo, part, total, columns = scores(place, unit, theirs, early, None, None, factor)
    held = [columns]
    ahead, back, part, total = lax.optimization_barrier((ahead, back, part, total))
    last = [shifted(back[:ROWS], "z", -1), shifted(ahead[ROWS:], "z", 1)]
    expos = [expo]
    expo, part, total, columns = scores(place, unit, theirs, [ahead, back], (part, total), None, factor)
    expos.append(expo)
    held.append(columns)
    expo, part, total, columns = scores(place, unit, theirs, last, (part, total), held, factor)
    expos.append(expo)
    blocks = early + [ahead, back] + last
    partner = shifted(part, "xh", 1)
    sums = lax.all_to_all(jnp.broadcast_to(columns[None], (n_z, n_z, 4, LANES)), "z", 0, 0)
    partial, scaled, across, loss = call(
        functools.partial(send_kernel, n_z, logit),
        [
            shape((CHIP, EMB), BF),
            shape((n_z * CHIP, EMB), BF),
            shape((LANES, LANES), F32),
            shape((1, ROWS), F32),
        ],
        [SMEM] + [VMEM] * (5 + len(expos) + len(blocks)),
        scratch=[pltpu.VMEM((LANES, LANES), F32), pltpu.VMEM((n_z, 4, LANES), F32)],
    )(place, sums, part, partner, total, unit, *expos, *blocks)
    added = shifted(partial, "xh", 1)
    own = call(
        functools.partial(own_kernel, n_z),
        [shape((CHIP, EMB), F32)],
        [VMEM] * (3 + len(expos)),
        cost=pl.CostEstimate(
            flops=2 * CHIP * n_z * CHIP * EMB,
            bytes_accessed=2 * n_z * CHIP * (CHIP + EMB),
            transcendentals=0,
        ),
    )(total, scaled, across, *expos)[0]
    grads = call(
        functools.partial(backward_kernel, coef),
        [shape((8, 16 * TILES * 8 + 32, LANES), BF)],
        [SMEM] + [VMEM] * 14 + [HBM] * 4,
        scratch=[
            pltpu.VMEM((HID, HID), BF),
            pltpu.VMEM((HID, EMB), BF),
            pltpu.VMEM((CHIP, EMB), BF),
            pltpu.VMEM((CHIP, HID), BF),
            pltpu.VMEM((CHIP, HID), BF),
            pltpu.SemaphoreType.DMA((2,)),
        ],
    )(
        place, own, added, other, embed, inv, n1, f1, s1, h1, n2, f2, s2, h2, x,
        sa_mid, sa_out, goal_mid, goal_out,
    )[0]

    def member(c, first, second, z):
        y, x_at = (first, second) if c == 0 else (second, first)
        return ((c * 4 + y) * 4 + x_at) * n_z + z % n_z

    half = n_z // 2
    near = [
        [member(c, a, b, 2 * q + p if c == 0 or p else 2 * q + 2) for a in range(4) for p in range(2)]
        for c in range(2)
        for b in range(4)
        for q in range(half)
    ]
    far = [
        [member(c, a, b, 2 * q + p) for b in range(4) for q in range(half)]
        for c in range(2)
        for a in range(4)
        for p in range(2)
    ]
    axes = ("c", "y", "xh", "xl", "z")
    grads = lax.all_to_all(grads, axes, 0, 0, axis_index_groups=near)
    grads = call(sum_kernel, [shape((16, TILES * 8 + 16, LANES), BF)], [VMEM])(grads)[0]
    grads = lax.all_to_all(grads, axes, 0, 0, axis_index_groups=far)
    keep, send = call(
        split_kernel,
        [shape((TILES * 4 + 8, LANES), F32)] * 2,
        [SMEM, VMEM],
        scratch=[pltpu.VMEM((16, LANES), F32)],
    )(place, grads)
    recv = shifted(send, "c", 1)
    obs_a, act_a, mid_a, out_a, obs_b, mid_b, out_b = call(
        last_kernel,
        [
            shape((4, EMB), F32),
            shape((4, acts), F32),
            shape((4, HID), F32),
            shape((4, EMB), F32),
            shape((4, EMB), F32),
            shape((4, HID), F32),
            shape((4, EMB), F32),
        ],
        [SMEM] + [VMEM] * 2,
    )(place, keep, recv)
    return (loss, obs_a.T, act_a.T, mid_a, out_a, obs_b.T, mid_b, out_b)


def solution(mesh):
    fine = Mesh(mesh.devices.reshape(2, -1, 2, mesh.shape["dp"] // 2, 2), ("xh", "z", "c", "y", "xl"))
    neg = ("xh", "z", "c")
    dp = ("y", "xl")
    return jax.shard_map(
        body,
        mesh=fine,
        in_specs=(
            P(dp, neg, None),
            P(dp, neg, None),
            P(dp, neg),
            P(dp, neg),
            P(),
            P(),
            P(),
            P(),
            P(),
            P(),
            P(),
        ),
        out_specs=(
            P(dp, neg),
            P(None, neg + dp),
            P(None, neg + dp),
            P(neg + dp, None),
            P(neg + dp, None),
            P(None, neg + dp),
            P(neg + dp, None),
            P(neg + dp, None),
        ),
        check_vma=False,
    )
```

```python
import functools
import math

import jax
import jax.numpy as jnp
from jax import lax
from jax.experimental import pallas as pl
from jax.experimental.pallas import tpu as pltpu
from jax.sharding import Mesh
from jax.sharding import PartitionSpec as P

NORM_EPS = 1e-05
UNIT_EPS = 1e-06
ROWS = 256
CHIP = 512
HID = 1024
EMB = 256
WIDE = 384
TALL = 256
TILES = (HID + 2 * EMB) // 128
LANES = 128
BF = jnp.bfloat16
F32 = jnp.float32
VMEM = pl.BlockSpec(memory_space=pltpu.VMEM)
SMEM = pl.BlockSpec(memory_space=pltpu.SMEM)
HBM = pl.BlockSpec(memory_space=pltpu.HBM)
PARAMS = pltpu.CompilerParams(vmem_limit_bytes=20 * 1024 * 1024)


def shape(dims, dtype):
    return jax.ShapeDtypeStruct(dims, dtype)


def dot_nn(a, b):
    return lax.dot_general(a, b, (((1,), (0,)), ((), ())), preferred_element_type=F32)


def dot_nt(a, b):
    return lax.dot_general(a, b, (((1,), (1,)), ((), ())), preferred_element_type=F32)


def dot_tn(a, b):
    return lax.dot_general(a, b, (((0,), (0,)), ((), ())), preferred_element_type=F32)


def sigmoid(v):
    return 0.5 + 0.5 * jnp.tanh(0.5 * v)


def call(kernel, outs, in_specs, scratch=(), cost=None):
    specs = [VMEM] * len(outs)
    return pl.pallas_call(
        kernel,
        out_shape=outs,
        in_specs=in_specs,
        out_specs=specs,
        scratch_shapes=list(scratch),
        compiler_params=PARAMS,
        cost_estimate=cost,
    )


def pick_kernel(place, replay, offset, obs, act, keep, send, replay_s, offset_s, obs_s, act_s, sems):
    copies = [
        pltpu.make_async_copy(source, target, sems.at[n])
        for n, (source, target) in enumerate(
            ((replay, replay_s), (offset, offset_s), (obs, obs_s), (act, act_s))
        )
    ]
    for copy in copies:
        copy.start()
    for copy in copies:
        copy.wait()
    role = place[2]
    index = replay_s[...]
    ahead = index + offset_s[...]
    spot = lax.broadcasted_iota(jnp.int32, (obs_s.shape[0], ROWS), 0)
    for out, rows in (
        (keep, jnp.where(role == 0, index, ahead)),
        (send, jnp.where(role == 0, ahead, index)),
    ):
        hot = jnp.where(spot == rows, 1.0, 0.0).astype(BF)
        out[:, :EMB] = dot_tn(hot, obs_s[...]).astype(BF)
        extra = dot_nn(act_s[...], hot)
        copies = LANES // extra.shape[0]
        out[:, EMB:] = jnp.concatenate([extra] * copies, axis=0).T.astype(BF)


def by_role(role, pairs, sems):
    for k in range(2):

        @pl.when(role == k)
        def _():
            for n, (sources, target) in enumerate(pairs):
                if sources[k] is not None:
                    pltpu.make_async_copy(sources[k], target, sems.at[n]).start()


def wait_role(role, pairs, sems, first):
    for k in range(2):

        @pl.when(role == k)
        def _():
            for n, (sources, target) in enumerate(pairs):
                if sources[k] is not None:
                    pltpu.make_async_copy(sources[k], target, sems.at[first + n]).wait()


def forward_kernel(
    place, keep, recv, sa_obs, sa_act, sa_mid, sa_out, goal_obs, goal_mid, goal_out,
    x, n1, f1, n2, f2, embed, inv, unit,
    w_first, w_mid, w_out, sems,
):
    role = place[2]
    acts = sa_act.shape[0]
    w_first[EMB:, :] = jnp.zeros((WIDE - EMB, HID), BF)
    pairs = [
        ((sa_obs, goal_obs), w_first.at[pl.ds(0, EMB)]),
        ((sa_act, None), w_first.at[pl.ds(EMB, acts)]),
        ((sa_mid, goal_mid), w_mid),
        ((sa_out, goal_out), w_out),
    ]
    by_role(role, pairs, sems)
    own = pl.multiple_of(role * ROWS, ROWS)
    other = pl.multiple_of((1 - role) * ROWS, ROWS)
    x[pl.ds(own, ROWS), :] = keep[...]
    x[pl.ds(other, ROWS), :] = recv[...]
    for start in range(0, CHIP, CHIP):
        rows = pl.ds(start, CHIP)

        def norm(values, normed, factor):
            center = values - jnp.mean(values, axis=-1, keepdims=True)
            scale = lax.rsqrt(jnp.mean(center * center, axis=-1, keepdims=True) + NORM_EPS)
            v = center * scale
            normed[rows, :] = v
            factor[rows, :] = scale
            return (v * sigmoid(v)).astype(BF)

        if start == 0:
            wait_role(role, pairs[:2], sems, 0)
        h1 = norm(dot_nn(x[rows, :], w_first[...]), n1, f1)
        if start == 0:
            wait_role(role, pairs[2:], sems, 2)
        h2 = norm(dot_nn(h1, w_mid[...]), n2, f2)
        e = dot_nn(h2, w_out[...])
        scale = lax.rsqrt(jnp.mean(e * e, axis=-1, keepdims=True) + UNIT_EPS)
        embed[rows, :] = e
        inv[rows, :] = scale
        unit[rows, :] = (e * scale * EMB ** (-0.5)).astype(BF)


def to_lanes(values):
    return jnp.sum(values.T, axis=0, keepdims=True)


def ring_order(n_z):
    order = [0, n_z - 1, 1]
    for k in range(2, n_z // 2):
        order += [n_z - k, k]
    return order + [n_z // 2]


def score_kernel(n_blocks, first, last, factor, place, *refs):
    refs = list(refs)
    ours, theirs = refs[:2]
    blocks = refs[2 : 2 + n_blocks]
    refs = refs[2 + n_blocks :]
    if not first:
        old_sum, old_total = refs[:2]
        refs = refs[2:]
    if last:
        old_columns = refs[:-4]
        refs = refs[-4:]
    expo, part, total, columns = refs
    down = [None] * n_blocks
    for start in range(0, 2 * CHIP, ROWS):
        source = ours if start < CHIP else theirs
        q = source[pl.ds(start % CHIP, ROWS), :]
        rows = pl.ds(start, ROWS)
        acc = None if first else old_total[rows, :]
        sums = None if first else old_sum[rows, :]
        at = 0
        for n, block in enumerate(blocks):
            t = block[...]
            width = t.shape[0]
            e = jnp.exp2(dot_nt(q, t) * factor)
            for lane in range(0, width, LANES):
                piece = e[:, lane : lane + LANES]
                sums = piece if sums is None else sums + piece
            fold = jnp.sum(e.reshape(ROWS // 8, 8, width), axis=0)
            down[n] = fold if down[n] is None else down[n] + fold
            e16 = e.astype(BF)
            expo[rows, at : at + width] = e16
            add = dot_nn(e16, t)
            acc = add if acc is None else acc + add
            at += width
        total[rows, :] = acc
        if last:
            for k in range(ROWS // LANES):
                line = start // LANES + k
                part[line : line + 1, :] = to_lanes(sums[k * LANES : (k + 1) * LANES, :])
        else:
            part[rows, :] = sums
    lines = []
    for fold in down:
        whole = jnp.sum(fold, axis=0, keepdims=True)
        lines += [whole[:, k : k + LANES] for k in range(0, whole.shape[1], LANES)]
    if last:
        n_z = columns.shape[0]
        held = [ref[k : k + 4, :] for ref in old_columns for k in range(0, ref.shape[0], 4)]
        held.append(jnp.concatenate(lines, axis=0))
        for shift, value in zip(ring_order(n_z), held):
            columns[lax.rem(place[1] + shift, n_z)] = value
    else:
        for k, line in enumerate(lines):
            columns[k : k + 1, :] = line


def scores(place, ours, theirs, blocks, prev, held, factor):
    width = sum(b.shape[0] for b in blocks)
    last = held is not None
    lines = (2 * sum(c.shape[0] for c in held) + 2 * width // LANES) // 8 if last else width // LANES
    outs = [
        shape((2 * CHIP, width), BF),
        shape((8, LANES) if last else (2 * CHIP, LANES), F32),
        shape((2 * CHIP, EMB), F32),
        shape((lines, 4, LANES) if last else (lines, LANES), F32),
    ]
    args = [place, ours, theirs, *blocks] + list(prev or ()) + list(held or ())
    kernel = functools.partial(score_kernel, len(blocks), prev is None, last, factor)
    cost = pl.CostEstimate(
        flops=4 * 2 * CHIP * width * EMB,
        bytes_accessed=2 * 2 * CHIP * width + 4 * 2 * CHIP * EMB,
        transcendentals=2 * CHIP * width,
    )
    return call(kernel, outs, [SMEM] + [VMEM] * (len(args) - 1), cost=cost)(*args)


def mix_rows(expos, scaled, total, columns, line, start, write):
    acc = None
    at = 0
    for expo in expos:
        width = expo.shape[1]
        add = dot_nn(expo[pl.ds(start, ROWS), :], scaled[pl.ds(at, width), :])
        acc = add if acc is None else acc + add
        at += width
    for k in range(ROWS // LANES):
        here = line + start // LANES + k
        value = total[pl.ds(start + k * LANES, LANES), :] * columns[:, here : here + 1]
        write(start + k * LANES, value + acc[k * LANES : (k + 1) * LANES, :])


def send_kernel(n_z, logit, place, sums, part, partner, total, ours, *refs):
    n_exp = 3
    expos = refs[:n_exp]
    blocks = refs[n_exp : n_exp + n_z + 1]
    send, scaled, across, loss = refs[n_exp + n_z + 1 : n_exp + n_z + 5]
    lines, whole = refs[n_exp + n_z + 5 :]
    z, role = place[1], place[2]
    column = sums[0]
    for k in range(1, n_z):
        column = column + sums[k]
    whole[...] = column
    mine = part[:4, :] + partner[4:, :]
    theirs = part[4:, :] + partner[:4, :]
    lines[...] = jnp.ones((LANES, LANES), F32)
    for k, shift in enumerate(ring_order(n_z)):
        lines[4 * k : 4 * k + 4, :] = 1.0 / whole[lax.rem(z + shift, n_z)]
    lines[4 * n_z : 4 * n_z + 4, :] = 1.0 / mine
    lines[4 * n_z + 4 : 4 * n_z + 8, :] = 1.0 / theirs
    columns = lines[...].T
    across[...] = columns

    at = 0
    for block in blocks:
        for start in range(0, block.shape[0], LANES):
            line = at // LANES
            t = block[pl.ds(start, LANES), :].astype(F32)
            scaled[pl.ds(at, LANES), :] = (t * columns[:, line : line + 1]).astype(BF)
            at += LANES

    def write(start, value):
        send[pl.ds(start - CHIP, LANES), :] = value.astype(BF)

    for start in range(CHIP, 2 * CHIP, ROWS):
        mix_rows(expos, scaled, total, columns, 4 * n_z, start, write)

    logs = jnp.log(mine) + jnp.log(whole[z])
    logs = jnp.where(role == 0, logs[:2], logs[2:])
    at = pl.multiple_of(role * ROWS, ROWS)
    both = ours[pl.ds(at, ROWS), :].astype(F32) * blocks[0][pl.ds(at, ROWS), :].astype(F32)
    both = both[:, :LANES] + both[:, LANES:]
    for k in range(2):
        positive = logit * to_lanes(both[k * LANES : (k + 1) * LANES, :])
        loss[:, k * LANES : (k + 1) * LANES] = 0.5 * logs[k : k + 1, :] - positive


def own_kernel(n_z, total, scaled, across, *refs):
    expos, own = refs[:-1], refs[-1]
    columns = across[...]

    def write(start, value):
        own[pl.ds(start, LANES), :] = value

    for start in range(0, CHIP, ROWS):
        mix_rows(expos, scaled, total, columns, 4 * n_z, start, write)


def unit_order(tall):
    unit = lax.broadcasted_iota(jnp.int32, (tall, tall), 1)
    origin = (unit // 4 % 8) * 32 + unit // 64 * 8 + (unit // 32 % 2) * 4 + unit % 4
    line = lax.broadcasted_iota(jnp.int32, (tall, tall), 0)
    return jnp.where(line == origin, 1.0, 0.0).astype(BF)


def turned(order, values):
    return lax.dot_general(
        order, values, (((0,), (1,)), ((), ())), preferred_element_type=F32
    ).astype(BF)


def slope_kernel(normed, slope, hidden):
    order = unit_order(TALL)
    for start in range(0, CHIP, ROWS):
        rows = pl.ds(start, ROWS)
        for at in range(0, HID, TALL):
            v = normed[rows, at : at + TALL]
            gate = sigmoid(v)
            h = v * gate
            slope[rows, at : at + TALL] = gate * (1.0 + v - h)
            hidden[at : at + TALL, start : start + ROWS] = turned(order, h.astype(BF))


def slopes(normed):
    cost = pl.CostEstimate(
        flops=2 * CHIP * HID * TALL, bytes_accessed=10 * CHIP * HID, transcendentals=CHIP * HID
    )
    outs = [shape((CHIP, HID), F32), shape((HID, CHIP), BF)]
    return call(slope_kernel, outs, [VMEM], cost=cost)(normed)


def backward_kernel(
    coef, place, own, recv, other, embed, inv, n1, f1, s1, h1, n2, f2, s2, h2, x,
    sa_mid, sa_out, goal_mid, goal_out,
    grads,
    w_mid, w_out, ge_s, p1_s, p2_s, sems,
):
    role = place[2]
    pairs = [((sa_out, goal_out), w_out), ((sa_mid, goal_mid), w_mid)]
    by_role(role, pairs, sems)
    for start in range(0, CHIP, CHIP):
        rows = pl.ds(start, CHIP)
        grad = coef * (
            own[rows, :] + recv[rows, :].astype(F32) - 2.0 * other[rows, :].astype(F32)
        )
        e = embed[rows, :]
        scale = inv[rows, :]
        along = jnp.mean(grad * e, axis=-1, keepdims=True)
        ge = (EMB ** (-0.5) * scale * (grad - e * (scale * scale * along))).astype(BF)
        ge_s[rows, :] = ge

        def step(back, normed, factor, slope, out):
            v = normed[rows, :]
            back = back * slope[rows, :]
            mean = jnp.mean(back, axis=-1, keepdims=True)
            tilt = jnp.mean(back * v, axis=-1, keepdims=True)
            pre = (factor[rows, :] * (back - mean - v * tilt)).astype(BF)
            out[rows, :] = pre
            return pre

        if start == 0:
            wait_role(role, pairs[:1], sems, 0)
        p2 = step(dot_nt(ge, w_out[...]), n2, f2, s2, p2_s)
        if start == 0:
            wait_role(role, pairs[1:], sems, 1)
        step(dot_nt(p2, w_mid[...]), n1, f1, s1, p1_s)
    tall = TALL
    order = unit_order(tall)

    def slot(y, x_at):
        return jnp.where(role == 0, y, x_at), jnp.where(role == 0, x_at, y)

    row = lax.broadcasted_iota(jnp.int32, (tall, LANES), 0)
    lane = lax.broadcasted_iota(jnp.int32, (tall, LANES), 1)
    wanted = lane // 16 == (row // 32 % 2) * 4 + row % 4
    pack_row = lax.broadcasted_iota(jnp.int32, (32, tall), 0)
    pack_col = lax.broadcasted_iota(jnp.int32, (32, tall), 1)
    pack = (pack_col // 64 == pack_row // 8) & (pack_col // 4 % 8 == pack_row % 8)
    pack = jnp.where(pack, 1.0, 0.0).astype(BF)
    packed = []
    for xh in range(2):
        start = xh * CHIP
        for left, right, tile in ((h1, p2_s, 0), (h2, ge_s, 8), (None, x, 10)):
            if left is None:
                spans = [slice(start + half * tall, start + (half + 1) * tall) for half in range(2)]
                units = jnp.concatenate([turned(order, p1_s[:, span]) for span in spans], axis=0)
            else:
                units = left[start : start + CHIP, :]
            value = dot_nn(units, right[:, : right.shape[1] // EMB * EMB])
            for part in range(8):
                first, second = slot(part // 2, xh * 2 + part % 2)
                for z in range(8):
                    line = z // 4 * tall + part * 32 + z % 4 * 8
                    base = second * (4 * TILES * 8) + z // 2 * TILES * 8
                    for k in range(0, value.shape[1] // LANES, 2):
                        two = [
                            value[line : line + 8, at * LANES : (at + 1) * LANES] for at in (k, k + 1)
                        ]
                        at = pl.multiple_of(base + (tile + k) * 8, 16)
                        piece = jnp.concatenate(two, axis=0).astype(BF)
                        grads[first * 2 + z % 2, pl.ds(at, 16), :] = piece
            if tile == 10:
                value = dot_nn(units, x[:, EMB:])
                for half in range(2):
                    mine = jnp.where(wanted, value[half * tall : (half + 1) * tall], 0.0)
                    packed.append(dot_nn(pack, mine.astype(BF)))
    halves = {}
    for y in range(4):
        for xh in range(2):
            pieces = [packed[2 * xh + half][y * 8 : y * 8 + 8] for half in range(2)]
            for parity in range(2):
                rows = [p[z * 4 + parity * 2 :][:2] for p in pieces for z in range(2)]
                for xl in range(2):
                    halves[y, xh * 2 + xl, parity] = jnp.concatenate(rows, axis=0)
    low = 16 * TILES * 8
    for first in range(4):
        for parity in range(2):
            for pair in (0, 2):
                rows = [
                    jnp.where(role == 0, halves[first, at, parity], halves[at, first, parity])
                    for at in (pair, pair + 1)
                ]
                piece = jnp.concatenate(rows, axis=0).astype(BF)
                grads[first * 2 + parity, low + pair * 8 : low + pair * 8 + 16, :] = piece


def plus(parts, rows):
    value = parts[0, rows, :].astype(F32)
    for k in range(1, parts.shape[0]):
        value = value + parts[k, rows, :].astype(F32)
    return value


def sum_kernel(parts, out):
    height = TILES * 8
    for part in range(16):
        extra = pl.ds(16 * height + part // 8 * 16, 16)
        out[part, :height, :] = plus(parts, pl.ds(part * height, height)).astype(BF)
        out[part, height:, :] = plus(parts, extra).astype(BF)


def split_kernel(place, parts, keep, send, extra):
    role = place[2]
    value = plus(parts, slice(None))
    extra[...] = value[TILES * 8 :]
    for k in range(TILES):
        low, high = value[k * 8 : k * 8 + 4], value[k * 8 + 4 : k * 8 + 8]
        keep[k * 4 : k * 4 + 4, :] = jnp.where(role == 0, low, high)
        send[k * 4 : k * 4 + 4, :] = jnp.where(role == 0, high, low)
    blank = jnp.zeros((8, LANES), F32)
    part = (place[0] * 2 + place[3]) % 2 * 4 + place[1] // 2
    for out, side in ((keep, role), (send, 1 - role)):
        out[TILES * 4 :, :] = blank + extra[pl.ds(part * 2 + side, 1), :]


def last_kernel(place, keep, recv, obs_a, act_a, mid_a, out_a, obs_b, mid_b, out_b):
    role, xl = place[2], place[3]
    sa = jnp.where(role == 0, keep[...], recv[...])
    goal = jnp.where(role == 0, recv[...], keep[...])
    for value, mid, out, obs in ((sa, mid_a, out_a, obs_a), (goal, mid_b, out_b, obs_b)):
        for k in range(TILES):
            target, at = (mid, k) if k < 8 else (out, k - 8) if k < 10 else (obs, k - 10)
            target[:, at * LANES : (at + 1) * LANES] = value[k * 4 : k * 4 + 4]
    line = sa[TILES * 4 : TILES * 4 + 1]
    line = jnp.where(xl == 0, line[:, :64], line[:, 64:])
    for r in range(4):
        act_a[r : r + 1, :] = line[:, r * 16 : r * 16 + 16]


def shifted(value, axis, shift):
    count = lax.axis_size(axis)
    return lax.ppermute(value, axis, [(k, (k + shift) % count) for k in range(count)])


def body(
    observations,
    actions,
    replay_index,
    future_offset,
    sa_obs,
    sa_act,
    sa_mid,
    sa_out,
    goal_obs,
    goal_mid,
    goal_out,
):
    n_z = lax.axis_size("z")
    weights = (sa_obs, sa_act, sa_mid, sa_out, goal_obs, goal_mid, goal_out)
    sa_obs, sa_act, sa_mid, sa_out, goal_obs, goal_mid, goal_out = (
        pltpu.with_memory_space_constraint(weight, pltpu.HBM) for weight in weights
    )
    slabs = (replay_index, future_offset, observations[0], actions[0].T)
    slabs = [pltpu.with_memory_space_constraint(slab, pltpu.HBM) for slab in slabs]
    logit = 3.0 * math.sqrt(EMB)
    coef = logit / (2.0 * lax.axis_size("y") * lax.axis_size("xl"))
    place = jnp.stack([lax.axis_index(axis) for axis in ("xh", "z", "c", "xl")]).astype(jnp.int32)

    acts = actions.shape[2]
    tall = observations.shape[1]
    keep, send = call(
        pick_kernel,
        [shape((ROWS, WIDE), BF)] * 2,
        [SMEM] + [HBM] * 4,
        scratch=[
            pltpu.VMEM((1, ROWS), jnp.int32),
            pltpu.VMEM((1, ROWS), jnp.int32),
            pltpu.VMEM((tall, EMB), BF),
            pltpu.VMEM((acts, tall), BF),
            pltpu.SemaphoreType.DMA((4,)),
        ],
    )(place, *slabs)
    recv = shifted(send, "c", 1)
    x, n1, f1, n2, f2, embed, inv, unit = call(
        forward_kernel,
        [
            shape((CHIP, WIDE), BF),
            shape((CHIP, HID), F32),
            shape((CHIP, 1), F32),
            shape((CHIP, HID), F32),
            shape((CHIP, 1), F32),
            shape((CHIP, EMB), F32),
            shape((CHIP, 1), F32),
            shape((CHIP, EMB), BF),
        ],
        [SMEM, VMEM, VMEM] + [HBM] * 7,
        scratch=[
            pltpu.VMEM((WIDE, HID), BF),
            pltpu.VMEM((HID, HID), BF),
            pltpu.VMEM((HID, EMB), BF),
            pltpu.SemaphoreType.DMA((4,)),
        ],
    )(place, keep, recv, sa_obs, sa_act, sa_mid, sa_out, goal_obs, goal_mid, goal_out)

    def crossed(value, shift):
        hop = [((k + shift) % n_z * 2 + 1 - c) for k in range(n_z) for c in range(2)]
        return lax.ppermute(value, ("z", "c"), list(enumerate(hop)))

    ahead, back = crossed(unit, 1), crossed(unit, -1)
    s1, h1 = slopes(n1)
    s2, h2 = slopes(n2)
    back, ahead, s1, h1, s2, h2, late = lax.optimization_barrier((back, ahead, s1, h1, s2, h2, unit))
    steps = [[ahead, back]]
    for k in range(2, n_z // 2 - 1):
        ahead, back = shifted(ahead, "z", 1), shifted(back, "z", -1)
        steps.append([ahead, back])
    other, theirs = shifted(late, "c", 1), shifted(late, "xh", 1)
    early = [other] + [block for step in steps for block in step]
    ahead, back = shifted(ahead, "z", 1), shifted(back, "z", -1)
    factor = logit * math.log2(math.e)
    expo, part, total, columns = scores(place, unit, theirs, early, None, None, factor)
    held = [columns]
    ahead, back, part, total = lax.optimization_barrier((ahead, back, part, total))
    last = [shifted(back[:ROWS], "z", -1), shifted(ahead[ROWS:], "z", 1)]
    expos = [expo]
    expo, part, total, columns = scores(place, unit, theirs, [ahead, back], (part, total), None, factor)
    expos.append(expo)
    held.append(columns)
    expo, part, total, columns = scores(place, unit, theirs, last, (part, total), held, factor)
    expos.append(expo)
    blocks = early + [ahead, back] + last
    partner = shifted(part, "xh", 1)
    partner, columns = lax.optimization_barrier((partner, columns))
    sums = lax.all_to_all(jnp.broadcast_to(columns[None], (n_z, n_z, 4, LANES)), "z", 0, 0)
    partial, scaled, across, loss = call(
        functools.partial(send_kernel, n_z, logit),
        [
            shape((CHIP, EMB), BF),
            shape((n_z * CHIP, EMB), BF),
            shape((LANES, LANES), F32),
            shape((1, ROWS), F32),
        ],
        [SMEM] + [VMEM] * (5 + len(expos) + len(blocks)),
        scratch=[pltpu.VMEM((LANES, LANES), F32), pltpu.VMEM((n_z, 4, LANES), F32)],
    )(place, sums, part, partner, total, unit, *expos, *blocks)
    added = shifted(partial, "xh", 1)
    own = call(
        functools.partial(own_kernel, n_z),
        [shape((CHIP, EMB), F32)],
        [VMEM] * (3 + len(expos)),
        cost=pl.CostEstimate(
            flops=2 * CHIP * n_z * CHIP * EMB,
            bytes_accessed=2 * n_z * CHIP * (CHIP + EMB),
            transcendentals=0,
        ),
    )(total, scaled, across, *expos)[0]
    grads = call(
        functools.partial(backward_kernel, coef),
        [shape((8, 16 * TILES * 8 + 32, LANES), BF)],
        [SMEM] + [VMEM] * 14 + [HBM] * 4,
        scratch=[
            pltpu.VMEM((HID, HID), BF),
            pltpu.VMEM((HID, EMB), BF),
            pltpu.VMEM((CHIP, EMB), BF),
            pltpu.VMEM((CHIP, HID), BF),
            pltpu.VMEM((CHIP, HID), BF),
            pltpu.SemaphoreType.DMA((2,)),
        ],
    )(
        place, own, added, other, embed, inv, n1, f1, s1, h1, n2, f2, s2, h2, x,
        sa_mid, sa_out, goal_mid, goal_out,
    )[0]

    def member(c, first, second, z):
        y, x_at = (first, second) if c == 0 else (second, first)
        return ((c * 4 + y) * 4 + x_at) * n_z + z % n_z

    half = n_z // 2
    near = [
        [member(c, a, b, 2 * q + p if c == 0 or p else 2 * q + 2) for a in range(4) for p in range(2)]
        for c in range(2)
        for b in range(4)
        for q in range(half)
    ]
    far = [
        [member(c, a, b, 2 * q + p) for b in range(4) for q in range(half)]
        for c in range(2)
        for a in range(4)
        for p in range(2)
    ]
    axes = ("c", "y", "xh", "xl", "z")
    grads = lax.all_to_all(grads, axes, 0, 0, axis_index_groups=near)
    grads = call(sum_kernel, [shape((16, TILES * 8 + 16, LANES), BF)], [VMEM])(grads)[0]
    grads = lax.all_to_all(grads, axes, 0, 0, axis_index_groups=far)
    keep, send = call(
        split_kernel,
        [shape((TILES * 4 + 8, LANES), F32)] * 2,
        [SMEM, VMEM],
        scratch=[pltpu.VMEM((16, LANES), F32)],
    )(place, grads)
    recv = shifted(send, "c", 1)
    obs_a, act_a, mid_a, out_a, obs_b, mid_b, out_b = call(
        last_kernel,
        [
            shape((4, EMB), F32),
            shape((4, acts), F32),
            shape((4, HID), F32),
            shape((4, EMB), F32),
            shape((4, EMB), F32),
            shape((4, HID), F32),
            shape((4, EMB), F32),
        ],
        [SMEM] + [VMEM] * 2,
    )(place, keep, recv)
    return (loss, obs_a.T, act_a.T, mid_a, out_a, obs_b.T, mid_b, out_b)


def solution(mesh):
    fine = Mesh(mesh.devices.reshape(2, -1, 2, mesh.shape["dp"] // 2, 2), ("xh", "z", "c", "y", "xl"))
    neg = ("xh", "z", "c")
    dp = ("y", "xl")
    return jax.shard_map(
        body,
        mesh=fine,
        in_specs=(
            P(dp, neg, None),
            P(dp, neg, None),
            P(dp, neg),
            P(dp, neg),
            P(),
            P(),
            P(),
            P(),
            P(),
            P(),
            P(),
        ),
        out_specs=(
            P(dp, neg),
            P(None, neg + dp),
            P(None, neg + dp),
            P(neg + dp, None),
            P(neg + dp, None),
            P(None, neg + dp),
            P(neg + dp, None),
            P(neg + dp, None),
        ),
        check_vma=False,
    )
```

```python
import functools
import math

import jax
import jax.numpy as jnp
from jax import lax
from jax.experimental import pallas as pl
from jax.experimental.pallas import tpu as pltpu
from jax.sharding import Mesh
from jax.sharding import PartitionSpec as P

NORM_EPS = 1e-05
UNIT_EPS = 1e-06
ROWS = 256
CHIP = 512
HID = 1024
EMB = 256
WIDE = 384
TALL = 256
TILES = (HID + 2 * EMB) // 128
LANES = 128
BF = jnp.bfloat16
F32 = jnp.float32
VMEM = pl.BlockSpec(memory_space=pltpu.VMEM)
SMEM = pl.BlockSpec(memory_space=pltpu.SMEM)
HBM = pl.BlockSpec(memory_space=pltpu.HBM)
PARAMS = pltpu.CompilerParams(vmem_limit_bytes=20 * 1024 * 1024)


def shape(dims, dtype):
    return jax.ShapeDtypeStruct(dims, dtype)


def dot_nn(a, b):
    return lax.dot_general(a, b, (((1,), (0,)), ((), ())), preferred_element_type=F32)


def dot_nt(a, b):
    return lax.dot_general(a, b, (((1,), (1,)), ((), ())), preferred_element_type=F32)


def dot_tn(a, b):
    return lax.dot_general(a, b, (((0,), (0,)), ((), ())), preferred_element_type=F32)


def sigmoid(v):
    return 0.5 + 0.5 * jnp.tanh(0.5 * v)


def call(kernel, outs, in_specs, scratch=(), cost=None):
    specs = [VMEM] * len(outs)
    return pl.pallas_call(
        kernel,
        out_shape=outs,
        in_specs=in_specs,
        out_specs=specs,
        scratch_shapes=list(scratch),
        compiler_params=PARAMS,
        cost_estimate=cost,
    )


def pick_kernel(place, replay, offset, obs, act, keep, send, replay_s, offset_s, obs_s, act_s, sems):
    copies = [
        pltpu.make_async_copy(source, target, sems.at[n])
        for n, (source, target) in enumerate(
            ((replay, replay_s), (offset, offset_s), (obs, obs_s), (act, act_s))
        )
    ]
    for copy in copies:
        copy.start()
    for copy in copies:
        copy.wait()
    role = place[2]
    index = replay_s[...]
    ahead = index + offset_s[...]
    spot = lax.broadcasted_iota(jnp.int32, (obs_s.shape[0], ROWS), 0)
    for out, rows in (
        (keep, jnp.where(role == 0, index, ahead)),
        (send, jnp.where(role == 0, ahead, index)),
    ):
        hot = jnp.where(spot == rows, 1.0, 0.0).astype(BF)
        out[:, :EMB] = dot_tn(hot, obs_s[...]).astype(BF)
        extra = dot_nn(act_s[...], hot)
        copies = LANES // extra.shape[0]
        out[:, EMB:] = jnp.concatenate([extra] * copies, axis=0).T.astype(BF)


def by_role(role, pairs, sems):
    for k in range(2):

        @pl.when(role == k)
        def _():
            for n, (sources, target) in enumerate(pairs):
                if sources[k] is not None:
                    pltpu.make_async_copy(sources[k], target, sems.at[n]).start()


def wait_role(role, pairs, sems, first):
    for k in range(2):

        @pl.when(role == k)
        def _():
            for n, (sources, target) in enumerate(pairs):
                if sources[k] is not None:
                    pltpu.make_async_copy(sources[k], target, sems.at[first + n]).wait()


def forward_kernel(
    place, keep, recv, sa_obs, sa_act, sa_mid, sa_out, goal_obs, goal_mid, goal_out,
    x, n1, f1, n2, f2, embed, inv, unit,
    w_first, w_mid, w_out, sems,
):
    role = place[2]
    acts = sa_act.shape[0]
    w_first[EMB:, :] = jnp.zeros((WIDE - EMB, HID), BF)
    pairs = [
        ((sa_obs, goal_obs), w_first.at[pl.ds(0, EMB)]),
        ((sa_act, None), w_first.at[pl.ds(EMB, acts)]),
        ((sa_mid, goal_mid), w_mid),
        ((sa_out, goal_out), w_out),
    ]
    by_role(role, pairs, sems)
    own = pl.multiple_of(role * ROWS, ROWS)
    other = pl.multiple_of((1 - role) * ROWS, ROWS)
    x[pl.ds(own, ROWS), :] = keep[...]
    x[pl.ds(other, ROWS), :] = recv[...]
    for start in range(0, CHIP, CHIP):
        rows = pl.ds(start, CHIP)

        def norm(values, normed, factor):
            center = values - jnp.mean(values, axis=-1, keepdims=True)
            scale = lax.rsqrt(jnp.mean(center * center, axis=-1, keepdims=True) + NORM_EPS)
            v = center * scale
            normed[rows, :] = v
            factor[rows, :] = scale
            return (v * sigmoid(v)).astype(BF)

        if start == 0:
            wait_role(role, pairs[:2], sems, 0)
        h1 = norm(dot_nn(x[rows, :], w_first[...]), n1, f1)
        if start == 0:
            wait_role(role, pairs[2:], sems, 2)
        h2 = norm(dot_nn(h1, w_mid[...]), n2, f2)
        e = dot_nn(h2, w_out[...])
        scale = lax.rsqrt(jnp.mean(e * e, axis=-1, keepdims=True) + UNIT_EPS)
        embed[rows, :] = e
        inv[rows, :] = scale
        unit[rows, :] = (e * scale * EMB ** (-0.5)).astype(BF)


def to_lanes(values):
    return jnp.sum(values.T, axis=0, keepdims=True)


def ring_order(place, n_z):
    order = [0]
    for k in range(1, n_z // 2):
        order += [k, n_z - k]
    order.append(n_z // 2)
    z, role = place[1], place[2]
    return [lax.rem(z + jnp.where(role == 0, shift, n_z - shift), n_z) for shift in order]


def score_kernel(n_blocks, first, last, factor, place, *refs):
    refs = list(refs)
    ours, theirs = refs[:2]
    blocks = refs[2 : 2 + n_blocks]
    refs = refs[2 + n_blocks :]
    if not first:
        old_sum, old_total = refs[:2]
        refs = refs[2:]
    if last:
        old_columns = refs[:-4]
        refs = refs[-4:]
    expo, part, total, columns = refs
    down = [None] * n_blocks
    for start in range(0, 2 * CHIP, ROWS):
        source = ours if start < CHIP else theirs
        q = source[pl.ds(start % CHIP, ROWS), :]
        rows = pl.ds(start, ROWS)
        acc = None if first else old_total[rows, :]
        sums = None if first else old_sum[rows, :]
        at = 0
        for n, block in enumerate(blocks):
            t = block[...]
            width = t.shape[0]
            e = jnp.exp2(dot_nt(q, t) * factor)
            for lane in range(0, width, LANES):
                piece = e[:, lane : lane + LANES]
                sums = piece if sums is None else sums + piece
            fold = jnp.sum(e.reshape(ROWS // 8, 8, width), axis=0)
            down[n] = fold if down[n] is None else down[n] + fold
            e16 = e.astype(BF)
            expo[rows, at : at + width] = e16
            add = dot_nn(e16, t)
            acc = add if acc is None else acc + add
            at += width
        total[rows, :] = acc
        if last:
            for k in range(ROWS // LANES):
                line = start // LANES + k
                part[line : line + 1, :] = to_lanes(sums[k * LANES : (k + 1) * LANES, :])
        else:
            part[rows, :] = sums
    lines = []
    for fold in down:
        whole = jnp.sum(fold, axis=0, keepdims=True)
        lines += [whole[:, k : k + LANES] for k in range(0, whole.shape[1], LANES)]
    if last:
        n_z = columns.shape[0]
        held = [ref[k : k + 4, :] for ref in old_columns for k in range(0, ref.shape[0], 4)]
        held.append(jnp.concatenate(lines, axis=0))
        for origin, value in zip(ring_order(place, n_z), held):
            columns[origin] = value
    else:
        for k, line in enumerate(lines):
            columns[k : k + 1, :] = line


def scores(place, ours, theirs, blocks, prev, held, factor):
    width = sum(b.shape[0] for b in blocks)
    last = held is not None
    lines = (2 * sum(c.shape[0] for c in held) + 2 * width // LANES) // 8 if last else width // LANES
    outs = [
        shape((2 * CHIP, width), BF),
        shape((8, LANES) if last else (2 * CHIP, LANES), F32),
        shape((2 * CHIP, EMB), F32),
        shape((lines, 4, LANES) if last else (lines, LANES), F32),
    ]
    args = [place, ours, theirs, *blocks] + list(prev or ()) + list(held or ())
    kernel = functools.partial(score_kernel, len(blocks), prev is None, last, factor)
    cost = pl.CostEstimate(
        flops=4 * 2 * CHIP * width * EMB,
        bytes_accessed=2 * 2 * CHIP * width + 4 * 2 * CHIP * EMB,
        transcendentals=2 * CHIP * width,
    )
    return call(kernel, outs, [SMEM] + [VMEM] * (len(args) - 1), cost=cost)(*args)


def mix_rows(expos, scaled, total, columns, line, start, write):
    acc = None
    at = 0
    for expo in expos:
        width = expo.shape[1]
        add = dot_nn(expo[pl.ds(start, ROWS), :], scaled[pl.ds(at, width), :])
        acc = add if acc is None else acc + add
        at += width
    for k in range(ROWS // LANES):
        here = line + start // LANES + k
        value = total[pl.ds(start + k * LANES, LANES), :] * columns[:, here : here + 1]
        write(start + k * LANES, value + acc[k * LANES : (k + 1) * LANES, :])


def send_kernel(n_z, logit, place, sums, part, partner, total, ours, *refs):
    n_exp = 3
    expos = refs[:n_exp]
    blocks = refs[n_exp : n_exp + n_z + 1]
    send, scaled, across, loss = refs[n_exp + n_z + 1 : n_exp + n_z + 5]
    lines, whole = refs[n_exp + n_z + 5 :]
    z, role = place[1], place[2]
    column = sums[0]
    for k in range(1, n_z):
        column = column + sums[k]
    whole[...] = column
    mine = part[:4, :] + partner[4:, :]
    theirs = part[4:, :] + partner[:4, :]
    lines[...] = jnp.ones((LANES, LANES), F32)
    for k, origin in enumerate(ring_order(place, n_z)):
        lines[4 * k : 4 * k + 4, :] = 1.0 / whole[origin]
    lines[4 * n_z : 4 * n_z + 4, :] = 1.0 / mine
    lines[4 * n_z + 4 : 4 * n_z + 8, :] = 1.0 / theirs
    columns = lines[...].T
    across[...] = columns

    at = 0
    for block in blocks:
        for start in range(0, block.shape[0], LANES):
            line = at // LANES
            t = block[pl.ds(start, LANES), :].astype(F32)
            scaled[pl.ds(at, LANES), :] = (t * columns[:, line : line + 1]).astype(BF)
            at += LANES

    def write(start, value):
        send[pl.ds(start - CHIP, LANES), :] = value.astype(BF)

    for start in range(CHIP, 2 * CHIP, ROWS):
        mix_rows(expos, scaled, total, columns, 4 * n_z, start, write)

    logs = jnp.log(mine) + jnp.log(whole[z])
    logs = jnp.where(role == 0, logs[:2], logs[2:])
    at = pl.multiple_of(role * ROWS, ROWS)
    both = ours[pl.ds(at, ROWS), :].astype(F32) * blocks[0][pl.ds(at, ROWS), :].astype(F32)
    both = both[:, :LANES] + both[:, LANES:]
    for k in range(2):
        positive = logit * to_lanes(both[k * LANES : (k + 1) * LANES, :])
        loss[:, k * LANES : (k + 1) * LANES] = 0.5 * logs[k : k + 1, :] - positive


def own_kernel(n_z, total, scaled, across, *refs):
    expos, own = refs[:-1], refs[-1]
    columns = across[...]

    def write(start, value):
        own[pl.ds(start, LANES), :] = value

    for start in range(0, CHIP, ROWS):
        mix_rows(expos, scaled, total, columns, 4 * n_z, start, write)


def unit_order(tall):
    unit = lax.broadcasted_iota(jnp.int32, (tall, tall), 1)
    origin = (unit // 4 % 8) * 32 + unit // 64 * 8 + (unit // 32 % 2) * 4 + unit % 4
    line = lax.broadcasted_iota(jnp.int32, (tall, tall), 0)
    return jnp.where(line == origin, 1.0, 0.0).astype(BF)


def turned(order, values):
    return lax.dot_general(
        order, values, (((0,), (1,)), ((), ())), preferred_element_type=F32
    ).astype(BF)


def slope_kernel(normed, slope, hidden):
    order = unit_order(TALL)
    for start in range(0, CHIP, ROWS):
        rows = pl.ds(start, ROWS)
        for at in range(0, HID, TALL):
            v = normed[rows, at : at + TALL]
            gate = sigmoid(v)
            h = v * gate
            slope[rows, at : at + TALL] = gate * (1.0 + v - h)
            hidden[at : at + TALL, start : start + ROWS] = turned(order, h.astype(BF))


def slopes(normed):
    cost = pl.CostEstimate(
        flops=2 * CHIP * HID * TALL, bytes_accessed=10 * CHIP * HID, transcendentals=CHIP * HID
    )
    outs = [shape((CHIP, HID), F32), shape((HID, CHIP), BF)]
    return call(slope_kernel, outs, [VMEM], cost=cost)(normed)


def backward_kernel(
    coef, place, own, recv, other, embed, inv, n1, f1, s1, h1, n2, f2, s2, h2, x,
    sa_mid, sa_out, goal_mid, goal_out,
    grads,
    w_mid, w_out, ge_s, p1_s, p2_s, sems,
):
    role = place[2]
    pairs = [((sa_out, goal_out), w_out), ((sa_mid, goal_mid), w_mid)]
    by_role(role, pairs, sems)
    for start in range(0, CHIP, CHIP):
        rows = pl.ds(start, CHIP)
        grad = coef * (
            own[rows, :] + recv[rows, :].astype(F32) - 2.0 * other[rows, :].astype(F32)
        )
        e = embed[rows, :]
        scale = inv[rows, :]
        along = jnp.mean(grad * e, axis=-1, keepdims=True)
        ge = (EMB ** (-0.5) * scale * (grad - e * (scale * scale * along))).astype(BF)
        ge_s[rows, :] = ge

        def step(back, normed, factor, slope, out):
            v = normed[rows, :]
            back = back * slope[rows, :]
            mean = jnp.mean(back, axis=-1, keepdims=True)
            tilt = jnp.mean(back * v, axis=-1, keepdims=True)
            pre = (factor[rows, :] * (back - mean - v * tilt)).astype(BF)
            out[rows, :] = pre
            return pre

        if start == 0:
            wait_role(role, pairs[:1], sems, 0)
        p2 = step(dot_nt(ge, w_out[...]), n2, f2, s2, p2_s)
        if start == 0:
            wait_role(role, pairs[1:], sems, 1)
        step(dot_nt(p2, w_mid[...]), n1, f1, s1, p1_s)
    tall = TALL
    order = unit_order(tall)

    def slot(y, x_at):
        return jnp.where(role == 0, y, x_at), jnp.where(role == 0, x_at, y)

    row = lax.broadcasted_iota(jnp.int32, (tall, LANES), 0)
    lane = lax.broadcasted_iota(jnp.int32, (tall, LANES), 1)
    wanted = lane // 16 == (row // 32 % 2) * 4 + row % 4
    pack_row = lax.broadcasted_iota(jnp.int32, (32, tall), 0)
    pack_col = lax.broadcasted_iota(jnp.int32, (32, tall), 1)
    pack = (pack_col // 64 == pack_row // 8) & (pack_col // 4 % 8 == pack_row % 8)
    pack = jnp.where(pack, 1.0, 0.0).astype(BF)
    packed = []
    for xh in range(2):
        start = xh * CHIP
        for left, right, tile in ((h1, p2_s, 0), (h2, ge_s, 8), (None, x, 10)):
            if left is None:
                spans = [slice(start + half * tall, start + (half + 1) * tall) for half in range(2)]
                units = jnp.concatenate([turned(order, p1_s[:, span]) for span in spans], axis=0)
            else:
                units = left[start : start + CHIP, :]
            value = dot_nn(units, right[:, : right.shape[1] // EMB * EMB])
            for part in range(8):
                first, second = slot(part // 2, xh * 2 + part % 2)
                for z in range(8):
                    line = z // 4 * tall + part * 32 + z % 4 * 8
                    base = second * (4 * TILES * 8) + z // 2 * TILES * 8
                    for k in range(0, value.shape[1] // LANES, 2):
                        two = [
                            value[line : line + 8, at * LANES : (at + 1) * LANES] for at in (k, k + 1)
                        ]
                        at = pl.multiple_of(base + (tile + k) * 8, 16)
                        piece = jnp.concatenate(two, axis=0).astype(BF)
                        grads[first * 2 + z % 2, pl.ds(at, 16), :] = piece
            if tile == 10:
                value = dot_nn(units, x[:, EMB:])
                for half in range(2):
                    mine = jnp.where(wanted, value[half * tall : (half + 1) * tall], 0.0)
                    packed.append(dot_nn(pack, mine.astype(BF)))
    halves = {}
    for y in range(4):
        for xh in range(2):
            pieces = [packed[2 * xh + half][y * 8 : y * 8 + 8] for half in range(2)]
            for parity in range(2):
                rows = [p[z * 4 + parity * 2 :][:2] for p in pieces for z in range(2)]
                for xl in range(2):
                    halves[y, xh * 2 + xl, parity] = jnp.concatenate(rows, axis=0)
    low = 16 * TILES * 8
    for first in range(4):
        for parity in range(2):
            for pair in (0, 2):
                rows = [
                    jnp.where(role == 0, halves[first, at, parity], halves[at, first, parity])
                    for at in (pair, pair + 1)
                ]
                piece = jnp.concatenate(rows, axis=0).astype(BF)
                grads[first * 2 + parity, low + pair * 8 : low + pair * 8 + 16, :] = piece


def plus(parts, rows):
    value = parts[0, rows, :].astype(F32)
    for k in range(1, parts.shape[0]):
        value = value + parts[k, rows, :].astype(F32)
    return value


def sum_kernel(parts, out):
    height = TILES * 8
    for part in range(16):
        extra = pl.ds(16 * height + part // 8 * 16, 16)
        out[part, :height, :] = plus(parts, pl.ds(part * height, height)).astype(BF)
        out[part, height:, :] = plus(parts, extra).astype(BF)


def split_kernel(place, parts, keep, send, extra):
    role = place[2]
    value = plus(parts, slice(None))
    extra[...] = value[TILES * 8 :]
    for k in range(TILES):
        low, high = value[k * 8 : k * 8 + 4], value[k * 8 + 4 : k * 8 + 8]
        keep[k * 4 : k * 4 + 4, :] = jnp.where(role == 0, low, high)
        send[k * 4 : k * 4 + 4, :] = jnp.where(role == 0, high, low)
    blank = jnp.zeros((8, LANES), F32)
    part = (place[0] * 2 + place[3]) % 2 * 4 + place[1] // 2
    for out, side in ((keep, role), (send, 1 - role)):
        out[TILES * 4 :, :] = blank + extra[pl.ds(part * 2 + side, 1), :]


def last_kernel(place, keep, recv, obs_a, act_a, mid_a, out_a, obs_b, mid_b, out_b):
    role, xl = place[2], place[3]
    sa = jnp.where(role == 0, keep[...], recv[...])
    goal = jnp.where(role == 0, recv[...], keep[...])
    for value, mid, out, obs in ((sa, mid_a, out_a, obs_a), (goal, mid_b, out_b, obs_b)):
        for k in range(TILES):
            target, at = (mid, k) if k < 8 else (out, k - 8) if k < 10 else (obs, k - 10)
            target[:, at * LANES : (at + 1) * LANES] = value[k * 4 : k * 4 + 4]
    line = sa[TILES * 4 : TILES * 4 + 1]
    line = jnp.where(xl == 0, line[:, :64], line[:, 64:])
    for r in range(4):
        act_a[r : r + 1, :] = line[:, r * 16 : r * 16 + 16]


def shifted(value, axis, shift):
    count = lax.axis_size(axis)
    return lax.ppermute(value, axis, [(k, (k + shift) % count) for k in range(count)])


def body(
    observations,
    actions,
    replay_index,
    future_offset,
    sa_obs,
    sa_act,
    sa_mid,
    sa_out,
    goal_obs,
    goal_mid,
    goal_out,
):
    n_z = lax.axis_size("z")
    weights = (sa_obs, sa_act, sa_mid, sa_out, goal_obs, goal_mid, goal_out)
    sa_obs, sa_act, sa_mid, sa_out, goal_obs, goal_mid, goal_out = (
        pltpu.with_memory_space_constraint(weight, pltpu.HBM) for weight in weights
    )
    slabs = (replay_index, future_offset, observations[0], actions[0].T)
    slabs = [pltpu.with_memory_space_constraint(slab, pltpu.HBM) for slab in slabs]
    logit = 3.0 * math.sqrt(EMB)
    coef = logit / (2.0 * lax.axis_size("y") * lax.axis_size("xl"))
    place = jnp.stack([lax.axis_index(axis) for axis in ("xh", "z", "c", "xl")]).astype(jnp.int32)

    acts = actions.shape[2]
    tall = observations.shape[1]
    keep, send = call(
        pick_kernel,
        [shape((ROWS, WIDE), BF)] * 2,
        [SMEM] + [HBM] * 4,
        scratch=[
            pltpu.VMEM((1, ROWS), jnp.int32),
            pltpu.VMEM((1, ROWS), jnp.int32),
            pltpu.VMEM((tall, EMB), BF),
            pltpu.VMEM((acts, tall), BF),
            pltpu.SemaphoreType.DMA((4,)),
        ],
    )(place, *slabs)
    recv = shifted(send, "c", 1)
    x, n1, f1, n2, f2, embed, inv, unit = call(
        forward_kernel,
        [
            shape((CHIP, WIDE), BF),
            shape((CHIP, HID), F32),
            shape((CHIP, 1), F32),
            shape((CHIP, HID), F32),
            shape((CHIP, 1), F32),
            shape((CHIP, EMB), F32),
            shape((CHIP, 1), F32),
            shape((CHIP, EMB), BF),
        ],
        [SMEM, VMEM, VMEM] + [HBM] * 7,
        scratch=[
            pltpu.VMEM((WIDE, HID), BF),
            pltpu.VMEM((HID, HID), BF),
            pltpu.VMEM((HID, EMB), BF),
            pltpu.SemaphoreType.DMA((4,)),
        ],
    )(place, keep, recv, sa_obs, sa_act, sa_mid, sa_out, goal_obs, goal_mid, goal_out)

    def hop(value, way, cross=0):
        pairs = []
        for k in range(n_z):
            for c in range(2):
                to = c ^ cross
                pairs.append((k * 2 + c, (k + (way if to else -way)) % n_z * 2 + to))
        return lax.ppermute(value, ("z", "c"), pairs)

    ahead, back = hop(unit, 1, 1), hop(unit, -1, 1)
    s1, h1 = slopes(n1)
    s2, h2 = slopes(n2)
    back, ahead, s1, h1, s2, h2, late = lax.optimization_barrier((back, ahead, s1, h1, s2, h2, unit))
    steps = [[ahead, back]]
    for k in range(2, n_z // 2 - 1):
        ahead, back = hop(ahead, 1), hop(back, -1)
        steps.append([ahead, back])
    other, theirs = shifted(late, "c", 1), shifted(late, "xh", 1)
    early = [other] + [block for step in steps for block in step]
    ahead, back = hop(ahead, 1), hop(back, -1)
    factor = logit * math.log2(math.e)
    expo, part, total, columns = scores(place, unit, theirs, early, None, None, factor)
    held = [columns]
    ahead, back, part, total = lax.optimization_barrier((ahead, back, part, total))
    last = [hop(back[:ROWS], -1), hop(ahead[ROWS:], 1)]
    expos = [expo]
    expo, part, total, columns = scores(place, unit, theirs, [ahead, back], (part, total), None, factor)
    expos.append(expo)
    held.append(columns)
    expo, part, total, columns = scores(place, unit, theirs, last, (part, total), held, factor)
    expos.append(expo)
    blocks = early + [ahead, back] + last
    partner = shifted(part, "xh", 1)
    partner, columns = lax.optimization_barrier((partner, columns))
    sums = lax.all_to_all(jnp.broadcast_to(columns[None], (n_z, n_z, 4, LANES)), "z", 0, 0)
    partial, scaled, across, loss = call(
        functools.partial(send_kernel, n_z, logit),
        [
            shape((CHIP, EMB), BF),
            shape((n_z * CHIP, EMB), BF),
            shape((LANES, LANES), F32),
            shape((1, ROWS), F32),
        ],
        [SMEM] + [VMEM] * (5 + len(expos) + len(blocks)),
        scratch=[pltpu.VMEM((LANES, LANES), F32), pltpu.VMEM((n_z, 4, LANES), F32)],
    )(place, sums, part, partner, total, unit, *expos, *blocks)
    added = shifted(partial, "xh", 1)
    own = call(
        functools.partial(own_kernel, n_z),
        [shape((CHIP, EMB), F32)],
        [VMEM] * (3 + len(expos)),
        cost=pl.CostEstimate(
            flops=2 * CHIP * n_z * CHIP * EMB,
            bytes_accessed=2 * n_z * CHIP * (CHIP + EMB),
            transcendentals=0,
        ),
    )(total, scaled, across, *expos)[0]
    grads = call(
        functools.partial(backward_kernel, coef),
        [shape((8, 16 * TILES * 8 + 32, LANES), BF)],
        [SMEM] + [VMEM] * 14 + [HBM] * 4,
        scratch=[
            pltpu.VMEM((HID, HID), BF),
            pltpu.VMEM((HID, EMB), BF),
            pltpu.VMEM((CHIP, EMB), BF),
            pltpu.VMEM((CHIP, HID), BF),
            pltpu.VMEM((CHIP, HID), BF),
            pltpu.SemaphoreType.DMA((2,)),
        ],
    )(
        place, own, added, other, embed, inv, n1, f1, s1, h1, n2, f2, s2, h2, x,
        sa_mid, sa_out, goal_mid, goal_out,
    )[0]

    def member(c, first, second, z):
        y, x_at = (first, second) if c == 0 else (second, first)
        return ((c * 4 + y) * 4 + x_at) * n_z + z % n_z

    half = n_z // 2
    near = [
        [member(c, a, b, 2 * q + p if c == 0 or p else 2 * q + 2) for a in range(4) for p in range(2)]
        for c in range(2)
        for b in range(4)
        for q in range(half)
    ]
    far = [
        [member(c, a, b, 2 * q + p) for b in range(4) for q in range(half)]
        for c in range(2)
        for a in range(4)
        for p in range(2)
    ]
    axes = ("c", "y", "xh", "xl", "z")
    grads = lax.all_to_all(grads, axes, 0, 0, axis_index_groups=near)
    grads = call(sum_kernel, [shape((16, TILES * 8 + 16, LANES), BF)], [VMEM])(grads)[0]
    grads = lax.all_to_all(grads, axes, 0, 0, axis_index_groups=far)
    keep, send = call(
        split_kernel,
        [shape((TILES * 4 + 8, LANES), F32)] * 2,
        [SMEM, VMEM],
        scratch=[pltpu.VMEM((16, LANES), F32)],
    )(place, grads)
    recv = shifted(send, "c", 1)
    obs_a, act_a, mid_a, out_a, obs_b, mid_b, out_b = call(
        last_kernel,
        [
            shape((4, EMB), F32),
            shape((4, acts), F32),
            shape((4, HID), F32),
            shape((4, EMB), F32),
            shape((4, EMB), F32),
            shape((4, HID), F32),
            shape((4, EMB), F32),
        ],
        [SMEM] + [VMEM] * 2,
    )(place, keep, recv)
    return (loss, obs_a.T, act_a.T, mid_a, out_a, obs_b.T, mid_b, out_b)


def solution(mesh):
    fine = Mesh(mesh.devices.reshape(2, -1, 2, mesh.shape["dp"] // 2, 2), ("xh", "z", "c", "y", "xl"))
    neg = ("xh", "z", "c")
    dp = ("y", "xl")
    return jax.shard_map(
        body,
        mesh=fine,
        in_specs=(
            P(dp, neg, None),
            P(dp, neg, None),
            P(dp, neg),
            P(dp, neg),
            P(),
            P(),
            P(),
            P(),
            P(),
            P(),
            P(),
        ),
        out_specs=(
            P(dp, neg),
            P(None, neg + dp),
            P(None, neg + dp),
            P(neg + dp, None),
            P(neg + dp, None),
            P(None, neg + dp),
            P(neg + dp, None),
            P(neg + dp, None),
        ),
        check_vma=False,
    )
```

```python
import functools
import math

import jax
import jax.numpy as jnp
from jax import lax
from jax.experimental import pallas as pl
from jax.experimental.pallas import tpu as pltpu
from jax.sharding import Mesh
from jax.sharding import PartitionSpec as P

NORM_EPS = 1e-05
UNIT_EPS = 1e-06
ROWS = 256
CHIP = 512
HID = 1024
EMB = 256
WIDE = 384
TALL = 256
TILES = (HID + 2 * EMB) // 128
LANES = 128
BF = jnp.bfloat16
F32 = jnp.float32
VMEM = pl.BlockSpec(memory_space=pltpu.VMEM)
SMEM = pl.BlockSpec(memory_space=pltpu.SMEM)
HBM = pl.BlockSpec(memory_space=pltpu.HBM)
PARAMS = pltpu.CompilerParams(vmem_limit_bytes=20 * 1024 * 1024)


def shape(dims, dtype):
    return jax.ShapeDtypeStruct(dims, dtype)


def dot_nn(a, b):
    return lax.dot_general(a, b, (((1,), (0,)), ((), ())), preferred_element_type=F32)


def dot_nt(a, b):
    return lax.dot_general(a, b, (((1,), (1,)), ((), ())), preferred_element_type=F32)


def dot_tn(a, b):
    return lax.dot_general(a, b, (((0,), (0,)), ((), ())), preferred_element_type=F32)


def sigmoid(v):
    return 0.5 + 0.5 * jnp.tanh(0.5 * v)


def call(kernel, outs, in_specs, scratch=(), cost=None):
    specs = [VMEM] * len(outs)
    return pl.pallas_call(
        kernel,
        out_shape=outs,
        in_specs=in_specs,
        out_specs=specs,
        scratch_shapes=list(scratch),
        compiler_params=PARAMS,
        cost_estimate=cost,
    )


def pick_kernel(place, replay, offset, obs, act, keep, send, replay_s, offset_s, obs_s, act_s, sems):
    copies = [
        pltpu.make_async_copy(source, target, sems.at[n])
        for n, (source, target) in enumerate(
            ((replay, replay_s), (offset, offset_s), (obs, obs_s), (act, act_s))
        )
    ]
    for copy in copies:
        copy.start()
    for copy in copies:
        copy.wait()
    role = place[2]
    index = replay_s[...]
    ahead = index + offset_s[...]
    spot = lax.broadcasted_iota(jnp.int32, (obs_s.shape[0], ROWS), 0)
    for out, rows in (
        (keep, jnp.where(role == 0, index, ahead)),
        (send, jnp.where(role == 0, ahead, index)),
    ):
        hot = jnp.where(spot == rows, 1.0, 0.0).astype(BF)
        out[:, :EMB] = dot_tn(hot, obs_s[...]).astype(BF)
        extra = dot_nn(act_s[...], hot)
        copies = LANES // extra.shape[0]
        out[:, EMB:] = jnp.concatenate([extra] * copies, axis=0).T.astype(BF)


def by_role(role, pairs, sems):
    for k in range(2):

        @pl.when(role == k)
        def _():
            for n, (sources, target) in enumerate(pairs):
                if sources[k] is not None:
                    pltpu.make_async_copy(sources[k], target, sems.at[n]).start()


def wait_role(role, pairs, sems, first):
    for k in range(2):

        @pl.when(role == k)
        def _():
            for n, (sources, target) in enumerate(pairs):
                if sources[k] is not None:
                    pltpu.make_async_copy(sources[k], target, sems.at[first + n]).wait()


def forward_kernel(
    place, keep, recv, sa_obs, sa_act, sa_mid, sa_out, goal_obs, goal_mid, goal_out,
    x, n1, f1, n2, f2, embed, inv, unit,
    w_first, w_mid, w_out, sems,
):
    role = place[2]
    acts = sa_act.shape[0]
    w_first[EMB:, :] = jnp.zeros((WIDE - EMB, HID), BF)
    pairs = [
        ((sa_obs, goal_obs), w_first.at[pl.ds(0, EMB)]),
        ((sa_act, None), w_first.at[pl.ds(EMB, acts)]),
        ((sa_mid, goal_mid), w_mid),
        ((sa_out, goal_out), w_out),
    ]
    by_role(role, pairs, sems)
    own = pl.multiple_of(role * ROWS, ROWS)
    other = pl.multiple_of((1 - role) * ROWS, ROWS)
    x[pl.ds(own, ROWS), :] = keep[...]
    x[pl.ds(other, ROWS), :] = recv[...]
    for start in range(0, CHIP, CHIP):
        rows = pl.ds(start, CHIP)

        def norm(values, normed, factor):
            center = values - jnp.mean(values, axis=-1, keepdims=True)
            scale = lax.rsqrt(jnp.mean(center * center, axis=-1, keepdims=True) + NORM_EPS)
            v = center * scale
            normed[rows, :] = v
            factor[rows, :] = scale
            return (v * sigmoid(v)).astype(BF)

        if start == 0:
            wait_role(role, pairs[:2], sems, 0)
        h1 = norm(dot_nn(x[rows, :], w_first[...]), n1, f1)
        if start == 0:
            wait_role(role, pairs[2:], sems, 2)
        h2 = norm(dot_nn(h1, w_mid[...]), n2, f2)
        e = dot_nn(h2, w_out[...])
        scale = lax.rsqrt(jnp.mean(e * e, axis=-1, keepdims=True) + UNIT_EPS)
        embed[rows, :] = e
        inv[rows, :] = scale
        unit[rows, :] = (e * scale * EMB ** (-0.5)).astype(BF)


def to_lanes(values):
    return jnp.sum(values.T, axis=0, keepdims=True)


def ring_order(n_z):
    order = [0, n_z - 1, 1]
    for k in range(2, n_z // 2):
        order += [n_z - k, k]
    return order + [n_z // 2]


def score_kernel(n_blocks, first, last, factor, place, *refs):
    refs = list(refs)
    ours, theirs = refs[:2]
    blocks = refs[2 : 2 + n_blocks]
    refs = refs[2 + n_blocks :]
    if not first:
        old_sum, old_total = refs[:2]
        refs = refs[2:]
    if last:
        old_columns = refs[:-4]
        refs = refs[-4:]
    expo, part, total, columns = refs
    down = [None] * n_blocks
    for start in range(0, 2 * CHIP, ROWS):
        source = ours if start < CHIP else theirs
        q = source[pl.ds(start % CHIP, ROWS), :]
        rows = pl.ds(start, ROWS)
        acc = None if first else old_total[rows, :]
        sums = None if first else old_sum[rows, :]
        at = 0
        for n, block in enumerate(blocks):
            t = block[...]
            width = t.shape[0]
            e = jnp.exp2(dot_nt(q, t) * factor)
            for lane in range(0, width, LANES):
                piece = e[:, lane : lane + LANES]
                sums = piece if sums is None else sums + piece
            fold = jnp.sum(e.reshape(ROWS // 8, 8, width), axis=0)
            down[n] = fold if down[n] is None else down[n] + fold
            e16 = e.astype(BF)
            expo[rows, at : at + width] = e16
            add = dot_nn(e16, t)
            acc = add if acc is None else acc + add
            at += width
        total[rows, :] = acc
        if last:
            for k in range(ROWS // LANES):
                line = start // LANES + k
                part[line : line + 1, :] = to_lanes(sums[k * LANES : (k + 1) * LANES, :])
        else:
            part[rows, :] = sums
    lines = []
    for fold in down:
        whole = jnp.sum(fold, axis=0, keepdims=True)
        lines += [whole[:, k : k + LANES] for k in range(0, whole.shape[1], LANES)]
    if last:
        n_z = columns.shape[0]
        held = [ref[k : k + 4, :] for ref in old_columns for k in range(0, ref.shape[0], 4)]
        held.append(jnp.concatenate(lines, axis=0))
        for shift, value in zip(ring_order(n_z), held):
            columns[lax.rem(place[1] + shift, n_z)] = value
    else:
        for k, line in enumerate(lines):
            columns[k : k + 1, :] = line


def scores(place, ours, theirs, blocks, prev, held, factor):
    width = sum(b.shape[0] for b in blocks)
    last = held is not None
    lines = (2 * sum(c.shape[0] for c in held) + 2 * width // LANES) // 8 if last else width // LANES
    outs = [
        shape((2 * CHIP, width), BF),
        shape((8, LANES) if last else (2 * CHIP, LANES), F32),
        shape((2 * CHIP, EMB), F32),
        shape((lines, 4, LANES) if last else (lines, LANES), F32),
    ]
    args = [place, ours, theirs, *blocks] + list(prev or ()) + list(held or ())
    kernel = functools.partial(score_kernel, len(blocks), prev is None, last, factor)
    cost = pl.CostEstimate(
        flops=4 * 2 * CHIP * width * EMB,
        bytes_accessed=2 * 2 * CHIP * width + 4 * 2 * CHIP * EMB,
        transcendentals=2 * CHIP * width,
    )
    return call(kernel, outs, [SMEM] + [VMEM] * (len(args) - 1), cost=cost)(*args)


def mix_rows(expos, scaled, total, columns, line, start, write):
    acc = None
    at = 0
    for expo in expos:
        width = expo.shape[1]
        add = dot_nn(expo[pl.ds(start, ROWS), :], scaled[pl.ds(at, width), :])
        acc = add if acc is None else acc + add
        at += width
    for k in range(ROWS // LANES):
        here = line + start // LANES + k
        value = total[pl.ds(start + k * LANES, LANES), :] * columns[:, here : here + 1]
        write(start + k * LANES, value + acc[k * LANES : (k + 1) * LANES, :])


def send_kernel(n_z, logit, place, sums, part, partner, total, ours, *refs):
    n_exp = 3
    expos = refs[:n_exp]
    blocks = refs[n_exp : n_exp + n_z + 1]
    low, high, scaled, across, loss = refs[n_exp + n_z + 1 : n_exp + n_z + 6]
    lines, whole = refs[n_exp + n_z + 6 :]
    z, role = place[1], place[2]
    column = sums[0]
    for k in range(1, n_z):
        column = column + sums[k]
    whole[...] = column
    mine = part[:4, :] + partner[4:, :]
    theirs = part[4:, :] + partner[:4, :]
    lines[...] = jnp.ones((LANES, LANES), F32)
    for k, shift in enumerate(ring_order(n_z)):
        lines[4 * k : 4 * k + 4, :] = 1.0 / whole[lax.rem(z + shift, n_z)]
    lines[4 * n_z : 4 * n_z + 4, :] = 1.0 / mine
    lines[4 * n_z + 4 : 4 * n_z + 8, :] = 1.0 / theirs
    columns = lines[...].T
    across[...] = columns

    at = 0
    for block in blocks:
        for start in range(0, block.shape[0], LANES):
            line = at // LANES
            t = block[pl.ds(start, LANES), :].astype(F32)
            scaled[pl.ds(at, LANES), :] = (t * columns[:, line : line + 1]).astype(BF)
            at += LANES

    def write(start, value):
        target = low if start < CHIP + ROWS else high
        target[pl.ds(start % ROWS, LANES), :] = value.astype(BF)

    for start in range(CHIP, 2 * CHIP, ROWS):
        mix_rows(expos, scaled, total, columns, 4 * n_z, start, write)

    logs = jnp.log(mine) + jnp.log(whole[z])
    logs = jnp.where(role == 0, logs[:2], logs[2:])
    at = pl.multiple_of(role * ROWS, ROWS)
    both = ours[pl.ds(at, ROWS), :].astype(F32) * blocks[0][pl.ds(at, ROWS), :].astype(F32)
    both = both[:, :LANES] + both[:, LANES:]
    for k in range(2):
        positive = logit * to_lanes(both[k * LANES : (k + 1) * LANES, :])
        loss[:, k * LANES : (k + 1) * LANES] = 0.5 * logs[k : k + 1, :] - positive


def own_kernel(n_z, total, scaled, across, *refs):
    expos, own = refs[:-1], refs[-1]
    columns = across[...]

    def write(start, value):
        own[pl.ds(start, LANES), :] = value

    for start in range(0, CHIP, ROWS):
        mix_rows(expos, scaled, total, columns, 4 * n_z, start, write)


def unit_order(tall):
    unit = lax.broadcasted_iota(jnp.int32, (tall, tall), 1)
    origin = (unit // 4 % 8) * 32 + unit // 64 * 8 + (unit // 32 % 2) * 4 + unit % 4
    line = lax.broadcasted_iota(jnp.int32, (tall, tall), 0)
    return jnp.where(line == origin, 1.0, 0.0).astype(BF)


def turned(order, values):
    return lax.dot_general(
        order, values, (((0,), (1,)), ((), ())), preferred_element_type=F32
    ).astype(BF)


def slope_kernel(normed, slope, hidden):
    order = unit_order(TALL)
    for start in range(0, CHIP, ROWS):
        rows = pl.ds(start, ROWS)
        for at in range(0, HID, TALL):
            v = normed[rows, at : at + TALL]
            gate = sigmoid(v)
            h = v * gate
            slope[rows, at : at + TALL] = gate * (1.0 + v - h)
            hidden[at : at + TALL, start : start + ROWS] = turned(order, h.astype(BF))


def slopes(normed):
    cost = pl.CostEstimate(
        flops=2 * CHIP * HID * TALL, bytes_accessed=10 * CHIP * HID, transcendentals=CHIP * HID
    )
    outs = [shape((CHIP, HID), F32), shape((HID, CHIP), BF)]
    return call(slope_kernel, outs, [VMEM], cost=cost)(normed)


def row_kernel(
    coef, start, place, own, recv, other, embed, inv, n1, f1, s1, n2, f2, s2,
    sa_mid, sa_out, goal_mid, goal_out,
    ge_s, p1_s, p2_s,
    w_mid, w_out, sems,
):
    role = place[2]
    pairs = [((sa_out, goal_out), w_out), ((sa_mid, goal_mid), w_mid)]
    by_role(role, pairs, sems)
    rows = pl.ds(start, ROWS)
    grad = coef * (
        own[rows, :] + recv[...].astype(F32) - 2.0 * other[rows, :].astype(F32)
    )
    e = embed[rows, :]
    scale = inv[rows, :]
    along = jnp.mean(grad * e, axis=-1, keepdims=True)
    ge = (EMB ** (-0.5) * scale * (grad - e * (scale * scale * along))).astype(BF)
    ge_s[...] = ge

    def step(back, normed, factor, slope, out):
        v = normed[rows, :]
        back = back * slope[rows, :]
        mean = jnp.mean(back, axis=-1, keepdims=True)
        tilt = jnp.mean(back * v, axis=-1, keepdims=True)
        pre = (factor[rows, :] * (back - mean - v * tilt)).astype(BF)
        out[...] = pre
        return pre

    wait_role(role, pairs[:1], sems, 0)
    p2 = step(dot_nt(ge, w_out[...]), n2, f2, s2, p2_s)
    wait_role(role, pairs[1:], sems, 1)
    step(dot_nt(p2, w_mid[...]), n1, f1, s1, p1_s)

def product_kernel(place, h1, h2, x, ge_a, p1_a, p2_a, ge_b, p1_b, p2_b, grads):
    role = place[2]

    def times(units, pair):
        return dot_nn(units[:, :ROWS], pair[0][...]) + dot_nn(units[:, ROWS:], pair[1][...])

    tall = TALL
    order = unit_order(tall)

    def slot(y, x_at):
        return jnp.where(role == 0, y, x_at), jnp.where(role == 0, x_at, y)

    row = lax.broadcasted_iota(jnp.int32, (tall, LANES), 0)
    lane = lax.broadcasted_iota(jnp.int32, (tall, LANES), 1)
    wanted = lane // 16 == (row // 32 % 2) * 4 + row % 4
    pack_row = lax.broadcasted_iota(jnp.int32, (32, tall), 0)
    pack_col = lax.broadcasted_iota(jnp.int32, (32, tall), 1)
    pack = (pack_col // 64 == pack_row // 8) & (pack_col // 4 % 8 == pack_row % 8)
    pack = jnp.where(pack, 1.0, 0.0).astype(BF)
    packed = []
    for xh in range(2):
        start = xh * CHIP
        for left, right, tile in ((h1, (p2_a, p2_b), 0), (h2, (ge_a, ge_b), 8), (None, None, 10)):
            if left is None:
                spans = [slice(start + half * tall, start + (half + 1) * tall) for half in range(2)]
                units = [
                    jnp.concatenate([turned(order, p1[:, span]) for span in spans], axis=0)
                    for p1 in (p1_a, p1_b)
                ]
                units = jnp.concatenate(units, axis=1)
                value = dot_nn(units, x[:, :EMB])
            else:
                value = times(left[start : start + CHIP, :], right)
            for part in range(8):
                first, second = slot(part // 2, xh * 2 + part % 2)
                for z in range(8):
                    line = z // 4 * tall + part * 32 + z % 4 * 8
                    base = second * (4 * TILES * 8) + z // 2 * TILES * 8
                    for k in range(0, value.shape[1] // LANES, 2):
                        two = [
                            value[line : line + 8, at * LANES : (at + 1) * LANES] for at in (k, k + 1)
                        ]
                        at = pl.multiple_of(base + (tile + k) * 8, 16)
                        piece = jnp.concatenate(two, axis=0).astype(BF)
                        grads[first * 2 + z % 2, pl.ds(at, 16), :] = piece
            if tile == 10:
                value = dot_nn(units, x[:, EMB:])
                for half in range(2):
                    mine = jnp.where(wanted, value[half * tall : (half + 1) * tall], 0.0)
                    packed.append(dot_nn(pack, mine.astype(BF)))
    halves = {}
    for y in range(4):
        for xh in range(2):
            pieces = [packed[2 * xh + half][y * 8 : y * 8 + 8] for half in range(2)]
            for parity in range(2):
                rows = [p[z * 4 + parity * 2 :][:2] for p in pieces for z in range(2)]
                for xl in range(2):
                    halves[y, xh * 2 + xl, parity] = jnp.concatenate(rows, axis=0)
    low = 16 * TILES * 8
    for first in range(4):
        for parity in range(2):
            for pair in (0, 2):
                rows = [
                    jnp.where(role == 0, halves[first, at, parity], halves[at, first, parity])
                    for at in (pair, pair + 1)
                ]
                piece = jnp.concatenate(rows, axis=0).astype(BF)
                grads[first * 2 + parity, low + pair * 8 : low + pair * 8 + 16, :] = piece


def plus(parts, rows):
    value = parts[0, rows, :].astype(F32)
    for k in range(1, parts.shape[0]):
        value = value + parts[k, rows, :].astype(F32)
    return value


def sum_kernel(parts, out):
    height = TILES * 8
    for part in range(16):
        extra = pl.ds(16 * height + part // 8 * 16, 16)
        out[part, :height, :] = plus(parts, pl.ds(part * height, height)).astype(BF)
        out[part, height:, :] = plus(parts, extra).astype(BF)


def split_kernel(place, parts, keep, send, extra):
    role = place[2]
    value = plus(parts, slice(None))
    extra[...] = value[TILES * 8 :]
    for k in range(TILES):
        low, high = value[k * 8 : k * 8 + 4], value[k * 8 + 4 : k * 8 + 8]
        keep[k * 4 : k * 4 + 4, :] = jnp.where(role == 0, low, high)
        send[k * 4 : k * 4 + 4, :] = jnp.where(role == 0, high, low)
    blank = jnp.zeros((8, LANES), F32)
    part = (place[0] * 2 + place[3]) % 2 * 4 + place[1] // 2
    for out, side in ((keep, role), (send, 1 - role)):
        out[TILES * 4 :, :] = blank + extra[pl.ds(part * 2 + side, 1), :]


def last_kernel(place, keep, recv, obs_a, act_a, mid_a, out_a, obs_b, mid_b, out_b):
    role, xl = place[2], place[3]
    sa = jnp.where(role == 0, keep[...], recv[...])
    goal = jnp.where(role == 0, recv[...], keep[...])
    for value, mid, out, obs in ((sa, mid_a, out_a, obs_a), (goal, mid_b, out_b, obs_b)):
        for k in range(TILES):
            target, at = (mid, k) if k < 8 else (out, k - 8) if k < 10 else (obs, k - 10)
            target[:, at * LANES : (at + 1) * LANES] = value[k * 4 : k * 4 + 4]
    line = sa[TILES * 4 : TILES * 4 + 1]
    line = jnp.where(xl == 0, line[:, :64], line[:, 64:])
    for r in range(4):
        act_a[r : r + 1, :] = line[:, r * 16 : r * 16 + 16]


def shifted(value, axis, shift):
    count = lax.axis_size(axis)
    return lax.ppermute(value, axis, [(k, (k + shift) % count) for k in range(count)])


def body(
    observations,
    actions,
    replay_index,
    future_offset,
    sa_obs,
    sa_act,
    sa_mid,
    sa_out,
    goal_obs,
    goal_mid,
    goal_out,
):
    n_z = lax.axis_size("z")
    weights = (sa_obs, sa_act, sa_mid, sa_out, goal_obs, goal_mid, goal_out)
    sa_obs, sa_act, sa_mid, sa_out, goal_obs, goal_mid, goal_out = (
        pltpu.with_memory_space_constraint(weight, pltpu.HBM) for weight in weights
    )
    slabs = (replay_index, future_offset, observations[0], actions[0].T)
    slabs = [pltpu.with_memory_space_constraint(slab, pltpu.HBM) for slab in slabs]
    logit = 3.0 * math.sqrt(EMB)
    coef = logit / (2.0 * lax.axis_size("y") * lax.axis_size("xl"))
    place = jnp.stack([lax.axis_index(axis) for axis in ("xh", "z", "c", "xl")]).astype(jnp.int32)

    acts = actions.shape[2]
    tall = observations.shape[1]
    keep, send = call(
        pick_kernel,
        [shape((ROWS, WIDE), BF)] * 2,
        [SMEM] + [HBM] * 4,
        scratch=[
            pltpu.VMEM((1, ROWS), jnp.int32),
            pltpu.VMEM((1, ROWS), jnp.int32),
            pltpu.VMEM((tall, EMB), BF),
            pltpu.VMEM((acts, tall), BF),
            pltpu.SemaphoreType.DMA((4,)),
        ],
    )(place, *slabs)
    recv = shifted(send, "c", 1)
    x, n1, f1, n2, f2, embed, inv, unit = call(
        forward_kernel,
        [
            shape((CHIP, WIDE), BF),
            shape((CHIP, HID), F32),
            shape((CHIP, 1), F32),
            shape((CHIP, HID), F32),
            shape((CHIP, 1), F32),
            shape((CHIP, EMB), F32),
            shape((CHIP, 1), F32),
            shape((CHIP, EMB), BF),
        ],
        [SMEM, VMEM, VMEM] + [HBM] * 7,
        scratch=[
            pltpu.VMEM((WIDE, HID), BF),
            pltpu.VMEM((HID, HID), BF),
            pltpu.VMEM((HID, EMB), BF),
            pltpu.SemaphoreType.DMA((4,)),
        ],
    )(place, keep, recv, sa_obs, sa_act, sa_mid, sa_out, goal_obs, goal_mid, goal_out)

    def crossed(value, shift):
        hop = [((k + shift) % n_z * 2 + 1 - c) for k in range(n_z) for c in range(2)]
        return lax.ppermute(value, ("z", "c"), list(enumerate(hop)))

    ahead, back = crossed(unit, 1), crossed(unit, -1)
    s1, h1 = slopes(n1)
    s2, h2 = slopes(n2)
    back, ahead, s1, h1, s2, h2, late = lax.optimization_barrier((back, ahead, s1, h1, s2, h2, unit))
    steps = [[ahead, back]]
    for k in range(2, n_z // 2 - 1):
        ahead, back = shifted(ahead, "z", 1), shifted(back, "z", -1)
        steps.append([ahead, back])
    other, theirs = shifted(late, "c", 1), shifted(late, "xh", 1)
    early = [other] + [block for step in steps for block in step]
    ahead, back = shifted(ahead, "z", 1), shifted(back, "z", -1)
    factor = logit * math.log2(math.e)
    expo, part, total, columns = scores(place, unit, theirs, early, None, None, factor)
    held = [columns]
    ahead, back, part, total = lax.optimization_barrier((ahead, back, part, total))
    last = [shifted(back[:ROWS], "z", -1), shifted(ahead[ROWS:], "z", 1)]
    expos = [expo]
    expo, part, total, columns = scores(place, unit, theirs, [ahead, back], (part, total), None, factor)
    expos.append(expo)
    held.append(columns)
    expo, part, total, columns = scores(place, unit, theirs, last, (part, total), held, factor)
    expos.append(expo)
    blocks = early + [ahead, back] + last
    partner = shifted(part, "xh", 1)
    partner, columns = lax.optimization_barrier((partner, columns))
    sums = lax.all_to_all(jnp.broadcast_to(columns[None], (n_z, n_z, 4, LANES)), "z", 0, 0)
    low, high, scaled, across, loss = call(
        functools.partial(send_kernel, n_z, logit),
        [
            shape((ROWS, EMB), BF),
            shape((ROWS, EMB), BF),
            shape((n_z * CHIP, EMB), BF),
            shape((LANES, LANES), F32),
            shape((1, ROWS), F32),
        ],
        [SMEM] + [VMEM] * (5 + len(expos) + len(blocks)),
        scratch=[pltpu.VMEM((LANES, LANES), F32), pltpu.VMEM((n_z, 4, LANES), F32)],
    )(place, sums, part, partner, total, unit, *expos, *blocks)
    added = [shifted(low, "xh", 1), shifted(high, "xh", 1)]
    own = call(
        functools.partial(own_kernel, n_z),
        [shape((CHIP, EMB), F32)],
        [VMEM] * (3 + len(expos)),
        cost=pl.CostEstimate(
            flops=2 * CHIP * n_z * CHIP * EMB,
            bytes_accessed=2 * n_z * CHIP * (CHIP + EMB),
            transcendentals=0,
        ),
    )(total, scaled, across, *expos)[0]
    halves = []
    for half, recv in enumerate(added):
        halves += call(
            functools.partial(row_kernel, coef, half * ROWS),
            [shape((ROWS, EMB), BF), shape((ROWS, HID), BF), shape((ROWS, HID), BF)],
            [SMEM] + [VMEM] * 11 + [HBM] * 4,
            scratch=[
                pltpu.VMEM((HID, HID), BF),
                pltpu.VMEM((HID, EMB), BF),
                pltpu.SemaphoreType.DMA((2,)),
            ],
            cost=pl.CostEstimate(
                flops=2 * ROWS * HID * (HID + EMB), bytes_accessed=8 * HID * HID, transcendentals=0
            ),
        )(
            place, own, recv, other, embed, inv, n1, f1, s1, n2, f2, s2,
            sa_mid, sa_out, goal_mid, goal_out,
        )
    grads = call(
        product_kernel,
        [shape((8, 16 * TILES * 8 + 32, LANES), BF)],
        [SMEM] + [VMEM] * 9,
    )(place, h1, h2, x, *halves)[0]

    def member(c, first, second, z):
        y, x_at = (first, second) if c == 0 else (second, first)
        return ((c * 4 + y) * 4 + x_at) * n_z + z % n_z

    half = n_z // 2
    near = [
        [member(c, a, b, 2 * q + p if c == 0 or p else 2 * q + 2) for a in range(4) for p in range(2)]
        for c in range(2)
        for b in range(4)
        for q in range(half)
    ]
    far = [
        [member(c, a, b, 2 * q + p) for b in range(4) for q in range(half)]
        for c in range(2)
        for a in range(4)
        for p in range(2)
    ]
    axes = ("c", "y", "xh", "xl", "z")
    grads = lax.all_to_all(grads, axes, 0, 0, axis_index_groups=near)
    grads = call(sum_kernel, [shape((16, TILES * 8 + 16, LANES), BF)], [VMEM])(grads)[0]
    grads = lax.all_to_all(grads, axes, 0, 0, axis_index_groups=far)
    keep, send = call(
        split_kernel,
        [shape((TILES * 4 + 8, LANES), F32)] * 2,
        [SMEM, VMEM],
        scratch=[pltpu.VMEM((16, LANES), F32)],
    )(place, grads)
    recv = shifted(send, "c", 1)
    obs_a, act_a, mid_a, out_a, obs_b, mid_b, out_b = call(
        last_kernel,
        [
            shape((4, EMB), F32),
            shape((4, acts), F32),
            shape((4, HID), F32),
            shape((4, EMB), F32),
            shape((4, EMB), F32),
            shape((4, HID), F32),
            shape((4, EMB), F32),
        ],
        [SMEM] + [VMEM] * 2,
    )(place, keep, recv)
    return (loss, obs_a.T, act_a.T, mid_a, out_a, obs_b.T, mid_b, out_b)


def solution(mesh):
    fine = Mesh(mesh.devices.reshape(2, -1, 2, mesh.shape["dp"] // 2, 2), ("xh", "z", "c", "y", "xl"))
    neg = ("xh", "z", "c")
    dp = ("y", "xl")
    return jax.shard_map(
        body,
        mesh=fine,
        in_specs=(
            P(dp, neg, None),
            P(dp, neg, None),
            P(dp, neg),
            P(dp, neg),
            P(),
            P(),
            P(),
            P(),
            P(),
            P(),
            P(),
        ),
        out_specs=(
            P(dp, neg),
            P(None, neg + dp),
            P(None, neg + dp),
            P(neg + dp, None),
            P(neg + dp, None),
            P(None, neg + dp),
            P(neg + dp, None),
            P(neg + dp, None),
        ),
        check_vma=False,
    )
```

```python
import functools
import math

import jax
import jax.numpy as jnp
from jax import lax
from jax.experimental import pallas as pl
from jax.experimental.pallas import tpu as pltpu
from jax.sharding import Mesh
from jax.sharding import PartitionSpec as P

NORM_EPS = 1e-05
UNIT_EPS = 1e-06
ROWS = 256
CHIP = 512
HID = 1024
EMB = 256
WIDE = 384
TALL = 256
TILES = (HID + 2 * EMB) // 128
LANES = 128
BF = jnp.bfloat16
F32 = jnp.float32
VMEM = pl.BlockSpec(memory_space=pltpu.VMEM)
SMEM = pl.BlockSpec(memory_space=pltpu.SMEM)
HBM = pl.BlockSpec(memory_space=pltpu.HBM)
PARAMS = pltpu.CompilerParams(vmem_limit_bytes=20 * 1024 * 1024)


def shape(dims, dtype):
    return jax.ShapeDtypeStruct(dims, dtype)


def dot_nn(a, b):
    return lax.dot_general(a, b, (((1,), (0,)), ((), ())), preferred_element_type=F32)


def dot_nt(a, b):
    return lax.dot_general(a, b, (((1,), (1,)), ((), ())), preferred_element_type=F32)


def dot_tn(a, b):
    return lax.dot_general(a, b, (((0,), (0,)), ((), ())), preferred_element_type=F32)


def sigmoid(v):
    return 0.5 + 0.5 * jnp.tanh(0.5 * v)


def call(kernel, outs, in_specs, scratch=(), cost=None):
    specs = [VMEM] * len(outs)
    return pl.pallas_call(
        kernel,
        out_shape=outs,
        in_specs=in_specs,
        out_specs=specs,
        scratch_shapes=list(scratch),
        compiler_params=PARAMS,
        cost_estimate=cost,
    )


def pick_kernel(place, replay, offset, obs, act, keep, send, replay_s, offset_s, obs_s, act_s, sems):
    copies = [
        pltpu.make_async_copy(source, target, sems.at[n])
        for n, (source, target) in enumerate(
            ((replay, replay_s), (offset, offset_s), (obs, obs_s), (act, act_s))
        )
    ]
    for copy in copies:
        copy.start()
    for copy in copies:
        copy.wait()
    role = place[2]
    index = replay_s[...]
    ahead = index + offset_s[...]
    spot = lax.broadcasted_iota(jnp.int32, (obs_s.shape[0], ROWS), 0)
    for out, rows in (
        (keep, jnp.where(role == 0, index, ahead)),
        (send, jnp.where(role == 0, ahead, index)),
    ):
        hot = jnp.where(spot == rows, 1.0, 0.0).astype(BF)
        out[:, :EMB] = dot_tn(hot, obs_s[...]).astype(BF)
        extra = dot_nn(act_s[...], hot)
        copies = LANES // extra.shape[0]
        out[:, EMB:] = jnp.concatenate([extra] * copies, axis=0).T.astype(BF)


def by_role(role, pairs, sems):
    for k in range(2):

        @pl.when(role == k)
        def _():
            for n, (sources, target) in enumerate(pairs):
                if sources[k] is not None:
                    pltpu.make_async_copy(sources[k], target, sems.at[n]).start()


def wait_role(role, pairs, sems, first):
    for k in range(2):

        @pl.when(role == k)
        def _():
            for n, (sources, target) in enumerate(pairs):
                if sources[k] is not None:
                    pltpu.make_async_copy(sources[k], target, sems.at[first + n]).wait()


def forward_kernel(
    place, keep, recv, sa_obs, sa_act, sa_mid, sa_out, goal_obs, goal_mid, goal_out,
    x, n1, f1, n2, f2, embed, inv, unit,
    w_first, w_mid, w_out, sems,
):
    role = place[2]
    acts = sa_act.shape[0]
    w_first[EMB:, :] = jnp.zeros((WIDE - EMB, HID), BF)
    pairs = [
        ((sa_obs, goal_obs), w_first.at[pl.ds(0, EMB)]),
        ((sa_act, None), w_first.at[pl.ds(EMB, acts)]),
        ((sa_mid, goal_mid), w_mid),
        ((sa_out, goal_out), w_out),
    ]
    by_role(role, pairs, sems)
    own = pl.multiple_of(role * ROWS, ROWS)
    other = pl.multiple_of((1 - role) * ROWS, ROWS)
    x[pl.ds(own, ROWS), :] = keep[...]
    x[pl.ds(other, ROWS), :] = recv[...]
    for start in range(0, CHIP, CHIP):
        rows = pl.ds(start, CHIP)

        def norm(values, normed, factor):
            center = values - jnp.mean(values, axis=-1, keepdims=True)
            scale = lax.rsqrt(jnp.mean(center * center, axis=-1, keepdims=True) + NORM_EPS)
            v = center * scale
            normed[rows, :] = v
            factor[rows, :] = scale
            return (v * sigmoid(v)).astype(BF)

        if start == 0:
            wait_role(role, pairs[:2], sems, 0)
        h1 = norm(dot_nn(x[rows, :], w_first[...]), n1, f1)
        if start == 0:
            wait_role(role, pairs[2:], sems, 2)
        h2 = norm(dot_nn(h1, w_mid[...]), n2, f2)
        e = dot_nn(h2, w_out[...])
        scale = lax.rsqrt(jnp.mean(e * e, axis=-1, keepdims=True) + UNIT_EPS)
        embed[rows, :] = e
        inv[rows, :] = scale
        unit[rows, :] = (e * scale * EMB ** (-0.5)).astype(BF)


def to_lanes(values):
    return jnp.sum(values.T, axis=0, keepdims=True)


def ring_order(place, n_z):
    order = [0]
    for k in range(1, n_z // 2):
        order += [k, n_z - k]
    order.append(n_z // 2)
    z, role = place[1], place[2]
    return [lax.rem(z + jnp.where(role == 0, n_z - shift, shift), n_z) for shift in order]


def score_kernel(n_blocks, first, last, factor, place, *refs):
    refs = list(refs)
    ours, theirs = refs[:2]
    blocks = refs[2 : 2 + n_blocks]
    refs = refs[2 + n_blocks :]
    if not first:
        old_sum, old_total = refs[:2]
        refs = refs[2:]
    if last:
        old_columns = refs[:-4]
        refs = refs[-4:]
    expo, part, total, columns = refs
    down = [None] * n_blocks
    for start in range(0, 2 * CHIP, ROWS):
        source = ours if start < CHIP else theirs
        q = source[pl.ds(start % CHIP, ROWS), :]
        rows = pl.ds(start, ROWS)
        acc = None if first else old_total[rows, :]
        sums = None if first else old_sum[rows, :]
        at = 0
        for n, block in enumerate(blocks):
            t = block[...]
            width = t.shape[0]
            e = jnp.exp2(dot_nt(q, t) * factor)
            for lane in range(0, width, LANES):
                piece = e[:, lane : lane + LANES]
                sums = piece if sums is None else sums + piece
            fold = jnp.sum(e.reshape(ROWS // 8, 8, width), axis=0)
            down[n] = fold if down[n] is None else down[n] + fold
            e16 = e.astype(BF)
            expo[rows, at : at + width] = e16
            add = dot_nn(e16, t)
            acc = add if acc is None else acc + add
            at += width
        total[rows, :] = acc
        if last:
            for k in range(ROWS // LANES):
                line = start // LANES + k
                part[line : line + 1, :] = to_lanes(sums[k * LANES : (k + 1) * LANES, :])
        else:
            part[rows, :] = sums
    lines = []
    for fold in down:
        whole = jnp.sum(fold, axis=0, keepdims=True)
        lines += [whole[:, k : k + LANES] for k in range(0, whole.shape[1], LANES)]
    if last:
        n_z = columns.shape[0]
        held = [ref[k : k + 4, :] for ref in old_columns for k in range(0, ref.shape[0], 4)]
        held.append(jnp.concatenate(lines, axis=0))
        for origin, value in zip(ring_order(place, n_z), held):
            columns[origin] = value
    else:
        for k, line in enumerate(lines):
            columns[k : k + 1, :] = line


def scores(place, ours, theirs, blocks, prev, held, factor):
    width = sum(b.shape[0] for b in blocks)
    last = held is not None
    lines = (2 * sum(c.shape[0] for c in held) + 2 * width // LANES) // 8 if last else width // LANES
    outs = [
        shape((2 * CHIP, width), BF),
        shape((8, LANES) if last else (2 * CHIP, LANES), F32),
        shape((2 * CHIP, EMB), F32),
        shape((lines, 4, LANES) if last else (lines, LANES), F32),
    ]
    args = [place, ours, theirs, *blocks] + list(prev or ()) + list(held or ())
    kernel = functools.partial(score_kernel, len(blocks), prev is None, last, factor)
    cost = pl.CostEstimate(
        flops=4 * 2 * CHIP * width * EMB,
        bytes_accessed=2 * 2 * CHIP * width + 4 * 2 * CHIP * EMB,
        transcendentals=2 * CHIP * width,
    )
    return call(kernel, outs, [SMEM] + [VMEM] * (len(args) - 1), cost=cost)(*args)


def mix_rows(expos, scaled, total, columns, line, start, write):
    acc = None
    at = 0
    for expo in expos:
        width = expo.shape[1]
        add = dot_nn(expo[pl.ds(start, ROWS), :], scaled[pl.ds(at, width), :])
        acc = add if acc is None else acc + add
        at += width
    for k in range(ROWS // LANES):
        here = line + start // LANES + k
        value = total[pl.ds(start + k * LANES, LANES), :] * columns[:, here : here + 1]
        write(start + k * LANES, value + acc[k * LANES : (k + 1) * LANES, :])


def send_kernel(n_z, logit, place, sums, part, partner, total, ours, *refs):
    n_exp = 3
    expos = refs[:n_exp]
    blocks = refs[n_exp : n_exp + n_z + 1]
    send, scaled, across, loss = refs[n_exp + n_z + 1 : n_exp + n_z + 5]
    lines, whole = refs[n_exp + n_z + 5 :]
    z, role = place[1], place[2]
    column = sums[0]
    for k in range(1, n_z):
        column = column + sums[k]
    whole[...] = column
    mine = part[:4, :] + partner[4:, :]
    theirs = part[4:, :] + partner[:4, :]
    lines[...] = jnp.ones((LANES, LANES), F32)
    for k, origin in enumerate(ring_order(place, n_z)):
        lines[4 * k : 4 * k + 4, :] = 1.0 / whole[origin]
    lines[4 * n_z : 4 * n_z + 4, :] = 1.0 / mine
    lines[4 * n_z + 4 : 4 * n_z + 8, :] = 1.0 / theirs
    columns = lines[...].T
    across[...] = columns

    at = 0
    for block in blocks:
        for start in range(0, block.shape[0], LANES):
            line = at // LANES
            t = block[pl.ds(start, LANES), :].astype(F32)
            scaled[pl.ds(at, LANES), :] = (t * columns[:, line : line + 1]).astype(BF)
            at += LANES

    def write(start, value):
        send[pl.ds(start - CHIP, LANES), :] = value.astype(BF)

    for start in range(CHIP, 2 * CHIP, ROWS):
        mix_rows(expos, scaled, total, columns, 4 * n_z, start, write)

    logs = jnp.log(mine) + jnp.log(whole[z])
    logs = jnp.where(role == 0, logs[:2], logs[2:])
    at = pl.multiple_of(role * ROWS, ROWS)
    both = ours[pl.ds(at, ROWS), :].astype(F32) * blocks[0][pl.ds(at, ROWS), :].astype(F32)
    both = both[:, :LANES] + both[:, LANES:]
    for k in range(2):
        positive = logit * to_lanes(both[k * LANES : (k + 1) * LANES, :])
        loss[:, k * LANES : (k + 1) * LANES] = 0.5 * logs[k : k + 1, :] - positive


def own_kernel(n_z, total, scaled, across, *refs):
    expos, own = refs[:-1], refs[-1]
    columns = across[...]

    def write(start, value):
        own[pl.ds(start, LANES), :] = value

    for start in range(0, CHIP, ROWS):
        mix_rows(expos, scaled, total, columns, 4 * n_z, start, write)


def unit_order(tall):
    unit = lax.broadcasted_iota(jnp.int32, (tall, tall), 1)
    origin = (unit // 4 % 8) * 32 + unit // 64 * 8 + (unit // 32 % 2) * 4 + unit % 4
    line = lax.broadcasted_iota(jnp.int32, (tall, tall), 0)
    return jnp.where(line == origin, 1.0, 0.0).astype(BF)


def turned(order, values):
    return lax.dot_general(
        order, values, (((0,), (1,)), ((), ())), preferred_element_type=F32
    ).astype(BF)


def slope_kernel(normed, slope, hidden):
    order = unit_order(TALL)
    for start in range(0, CHIP, ROWS):
        rows = pl.ds(start, ROWS)
        for at in range(0, HID, TALL):
            v = normed[rows, at : at + TALL]
            gate = sigmoid(v)
            h = v * gate
            slope[rows, at : at + TALL] = gate * (1.0 + v - h)
            hidden[at : at + TALL, start : start + ROWS] = turned(order, h.astype(BF))


def slopes(normed):
    cost = pl.CostEstimate(
        flops=2 * CHIP * HID * TALL, bytes_accessed=10 * CHIP * HID, transcendentals=CHIP * HID
    )
    outs = [shape((CHIP, HID), F32), shape((HID, CHIP), BF)]
    return call(slope_kernel, outs, [VMEM], cost=cost)(normed)


def backward_kernel(
    coef, place, own, recv, other, embed, inv, n1, f1, s1, h1, n2, f2, s2, h2, x,
    sa_mid, sa_out, goal_mid, goal_out,
    grads,
    w_mid, w_out, ge_s, p1_s, p2_s, sems,
):
    role = place[2]
    pairs = [((sa_out, goal_out), w_out), ((sa_mid, goal_mid), w_mid)]
    by_role(role, pairs, sems)
    for start in range(0, CHIP, CHIP):
        rows = pl.ds(start, CHIP)
        grad = coef * (
            own[rows, :] + recv[rows, :].astype(F32) - 2.0 * other[rows, :].astype(F32)
        )
        e = embed[rows, :]
        scale = inv[rows, :]
        along = jnp.mean(grad * e, axis=-1, keepdims=True)
        ge = (EMB ** (-0.5) * scale * (grad - e * (scale * scale * along))).astype(BF)
        ge_s[rows, :] = ge

        def step(back, normed, factor, slope, out):
            v = normed[rows, :]
            back = back * slope[rows, :]
            mean = jnp.mean(back, axis=-1, keepdims=True)
            tilt = jnp.mean(back * v, axis=-1, keepdims=True)
            pre = (factor[rows, :] * (back - mean - v * tilt)).astype(BF)
            out[rows, :] = pre
            return pre

        if start == 0:
            wait_role(role, pairs[:1], sems, 0)
        p2 = step(dot_nt(ge, w_out[...]), n2, f2, s2, p2_s)
        if start == 0:
            wait_role(role, pairs[1:], sems, 1)
        step(dot_nt(p2, w_mid[...]), n1, f1, s1, p1_s)
    tall = TALL
    order = unit_order(tall)

    def slot(y, x_at):
        return jnp.where(role == 0, y, x_at), jnp.where(role == 0, x_at, y)

    row = lax.broadcasted_iota(jnp.int32, (tall, LANES), 0)
    lane = lax.broadcasted_iota(jnp.int32, (tall, LANES), 1)
    wanted = lane // 16 == (row // 32 % 2) * 4 + row % 4
    pack_row = lax.broadcasted_iota(jnp.int32, (32, tall), 0)
    pack_col = lax.broadcasted_iota(jnp.int32, (32, tall), 1)
    pack = (pack_col // 64 == pack_row // 8) & (pack_col // 4 % 8 == pack_row % 8)
    pack = jnp.where(pack, 1.0, 0.0).astype(BF)
    packed = []
    for xh in range(2):
        start = xh * CHIP
        for left, right, tile in ((h1, p2_s, 0), (h2, ge_s, 8), (None, x, 10)):
            if left is None:
                spans = [slice(start + half * tall, start + (half + 1) * tall) for half in range(2)]
                units = jnp.concatenate([turned(order, p1_s[:, span]) for span in spans], axis=0)
            else:
                units = left[start : start + CHIP, :]
            value = dot_nn(units, right[:, : right.shape[1] // EMB * EMB])
            for part in range(8):
                first, second = slot(part // 2, xh * 2 + part % 2)
                for z in range(8):
                    line = z // 4 * tall + part * 32 + z % 4 * 8
                    base = second * (4 * TILES * 8) + z // 2 * TILES * 8
                    for k in range(0, value.shape[1] // LANES, 2):
                        two = [
                            value[line : line + 8, at * LANES : (at + 1) * LANES] for at in (k, k + 1)
                        ]
                        at = pl.multiple_of(base + (tile + k) * 8, 16)
                        piece = jnp.concatenate(two, axis=0).astype(BF)
                        grads[first * 2 + z % 2, pl.ds(at, 16), :] = piece
            if tile == 10:
                value = dot_nn(units, x[:, EMB:])
                for half in range(2):
                    mine = jnp.where(wanted, value[half * tall : (half + 1) * tall], 0.0)
                    packed.append(dot_nn(pack, mine.astype(BF)))
    halves = {}
    for y in range(4):
        for xh in range(2):
            pieces = [packed[2 * xh + half][y * 8 : y * 8 + 8] for half in range(2)]
            for parity in range(2):
                rows = [p[z * 4 + parity * 2 :][:2] for p in pieces for z in range(2)]
                for xl in range(2):
                    halves[y, xh * 2 + xl, parity] = jnp.concatenate(rows, axis=0)
    low = 16 * TILES * 8
    for first in range(4):
        for parity in range(2):
            for pair in (0, 2):
                rows = [
                    jnp.where(role == 0, halves[first, at, parity], halves[at, first, parity])
                    for at in (pair, pair + 1)
                ]
                piece = jnp.concatenate(rows, axis=0).astype(BF)
                grads[first * 2 + parity, low + pair * 8 : low + pair * 8 + 16, :] = piece


def plus(parts, rows):
    value = parts[0, rows, :].astype(F32)
    for k in range(1, parts.shape[0]):
        value = value + parts[k, rows, :].astype(F32)
    return value


def sum_kernel(parts, out):
    height = TILES * 8
    for part in range(16):
        extra = pl.ds(16 * height + part // 8 * 16, 16)
        out[part, :height, :] = plus(parts, pl.ds(part * height, height)).astype(BF)
        out[part, height:, :] = plus(parts, extra).astype(BF)


def split_kernel(place, parts, keep, send, extra):
    role = place[2]
    value = plus(parts, slice(None))
    extra[...] = value[TILES * 8 :]
    for k in range(TILES):
        low, high = value[k * 8 : k * 8 + 4], value[k * 8 + 4 : k * 8 + 8]
        keep[k * 4 : k * 4 + 4, :] = jnp.where(role == 0, low, high)
        send[k * 4 : k * 4 + 4, :] = jnp.where(role == 0, high, low)
    blank = jnp.zeros((8, LANES), F32)
    part = (place[0] * 2 + place[3]) % 2 * 4 + place[1] // 2
    for out, side in ((keep, role), (send, 1 - role)):
        out[TILES * 4 :, :] = blank + extra[pl.ds(part * 2 + side, 1), :]


def last_kernel(place, keep, recv, obs_a, act_a, mid_a, out_a, obs_b, mid_b, out_b):
    role, xl = place[2], place[3]
    sa = jnp.where(role == 0, keep[...], recv[...])
    goal = jnp.where(role == 0, recv[...], keep[...])
    for value, mid, out, obs in ((sa, mid_a, out_a, obs_a), (goal, mid_b, out_b, obs_b)):
        for k in range(TILES):
            target, at = (mid, k) if k < 8 else (out, k - 8) if k < 10 else (obs, k - 10)
            target[:, at * LANES : (at + 1) * LANES] = value[k * 4 : k * 4 + 4]
    line = sa[TILES * 4 : TILES * 4 + 1]
    line = jnp.where(xl == 0, line[:, :64], line[:, 64:])
    for r in range(4):
        act_a[r : r + 1, :] = line[:, r * 16 : r * 16 + 16]


def shifted(value, axis, shift):
    count = lax.axis_size(axis)
    return lax.ppermute(value, axis, [(k, (k + shift) % count) for k in range(count)])


def body(
    observations,
    actions,
    replay_index,
    future_offset,
    sa_obs,
    sa_act,
    sa_mid,
    sa_out,
    goal_obs,
    goal_mid,
    goal_out,
):
    n_z = lax.axis_size("z")
    weights = (sa_obs, sa_act, sa_mid, sa_out, goal_obs, goal_mid, goal_out)
    sa_obs, sa_act, sa_mid, sa_out, goal_obs, goal_mid, goal_out = (
        pltpu.with_memory_space_constraint(weight, pltpu.HBM) for weight in weights
    )
    slabs = (replay_index, future_offset, observations[0], actions[0].T)
    slabs = [pltpu.with_memory_space_constraint(slab, pltpu.HBM) for slab in slabs]
    logit = 3.0 * math.sqrt(EMB)
    coef = logit / (2.0 * lax.axis_size("y") * lax.axis_size("xl"))
    place = jnp.stack([lax.axis_index(axis) for axis in ("xh", "z", "c", "xl")]).astype(jnp.int32)

    acts = actions.shape[2]
    tall = observations.shape[1]
    keep, send = call(
        pick_kernel,
        [shape((ROWS, WIDE), BF)] * 2,
        [SMEM] + [HBM] * 4,
        scratch=[
            pltpu.VMEM((1, ROWS), jnp.int32),
            pltpu.VMEM((1, ROWS), jnp.int32),
            pltpu.VMEM((tall, EMB), BF),
            pltpu.VMEM((acts, tall), BF),
            pltpu.SemaphoreType.DMA((4,)),
        ],
    )(place, *slabs)
    recv = shifted(send, "c", 1)
    x, n1, f1, n2, f2, embed, inv, unit = call(
        forward_kernel,
        [
            shape((CHIP, WIDE), BF),
            shape((CHIP, HID), F32),
            shape((CHIP, 1), F32),
            shape((CHIP, HID), F32),
            shape((CHIP, 1), F32),
            shape((CHIP, EMB), F32),
            shape((CHIP, 1), F32),
            shape((CHIP, EMB), BF),
        ],
        [SMEM, VMEM, VMEM] + [HBM] * 7,
        scratch=[
            pltpu.VMEM((WIDE, HID), BF),
            pltpu.VMEM((HID, HID), BF),
            pltpu.VMEM((HID, EMB), BF),
            pltpu.SemaphoreType.DMA((4,)),
        ],
    )(place, keep, recv, sa_obs, sa_act, sa_mid, sa_out, goal_obs, goal_mid, goal_out)

    def hop(value, way, cross=0):
        pairs = []
        for k in range(n_z):
            for c in range(2):
                to = c ^ cross
                pairs.append((k * 2 + c, (k + (-way if to else way)) % n_z * 2 + to))
        return lax.ppermute(value, ("z", "c"), pairs)

    ahead, back = hop(unit, 1, 1), hop(unit, -1, 1)
    s1, h1 = slopes(n1)
    s2, h2 = slopes(n2)
    ahead, back, s1, h1, s2, h2, late = lax.optimization_barrier((ahead, back, s1, h1, s2, h2, unit))
    steps = [[ahead, back]]
    for k in range(2, n_z // 2 - 1):
        ahead, back = hop(ahead, 1), hop(back, -1)
        steps.append([ahead, back])
    other, theirs = shifted(late, "c", 1), shifted(late, "xh", 1)
    early = [other] + [block for step in steps for block in step]
    ahead, back = hop(ahead, 1), hop(back, -1)
    factor = logit * math.log2(math.e)
    expo, part, total, columns = scores(place, unit, theirs, early, None, None, factor)
    held = [columns]
    ahead, back, part, total = lax.optimization_barrier((ahead, back, part, total))
    last = [hop(back[:ROWS], -1), hop(ahead[ROWS:], 1)]
    expos = [expo]
    expo, part, total, columns = scores(place, unit, theirs, [ahead, back], (part, total), None, factor)
    expos.append(expo)
    held.append(columns)
    expo, part, total, columns = scores(place, unit, theirs, last, (part, total), held, factor)
    expos.append(expo)
    blocks = early + [ahead, back] + last
    partner = shifted(part, "xh", 1)
    partner, columns = lax.optimization_barrier((partner, columns))
    sums = lax.all_to_all(jnp.broadcast_to(columns[None], (n_z, n_z, 4, LANES)), "z", 0, 0)
    partial, scaled, across, loss = call(
        functools.partial(send_kernel, n_z, logit),
        [
            shape((CHIP, EMB), BF),
            shape((n_z * CHIP, EMB), BF),
            shape((LANES, LANES), F32),
            shape((1, ROWS), F32),
        ],
        [SMEM] + [VMEM] * (5 + len(expos) + len(blocks)),
        scratch=[pltpu.VMEM((LANES, LANES), F32), pltpu.VMEM((n_z, 4, LANES), F32)],
    )(place, sums, part, partner, total, unit, *expos, *blocks)
    added = shifted(partial, "xh", 1)
    own = call(
        functools.partial(own_kernel, n_z),
        [shape((CHIP, EMB), F32)],
        [VMEM] * (3 + len(expos)),
        cost=pl.CostEstimate(
            flops=2 * CHIP * n_z * CHIP * EMB,
            bytes_accessed=2 * n_z * CHIP * (CHIP + EMB),
            transcendentals=0,
        ),
    )(total, scaled, across, *expos)[0]
    grads = call(
        functools.partial(backward_kernel, coef),
        [shape((8, 16 * TILES * 8 + 32, LANES), BF)],
        [SMEM] + [VMEM] * 14 + [HBM] * 4,
        scratch=[
            pltpu.VMEM((HID, HID), BF),
            pltpu.VMEM((HID, EMB), BF),
            pltpu.VMEM((CHIP, EMB), BF),
            pltpu.VMEM((CHIP, HID), BF),
            pltpu.VMEM((CHIP, HID), BF),
            pltpu.SemaphoreType.DMA((2,)),
        ],
    )(
        place, own, added, other, embed, inv, n1, f1, s1, h1, n2, f2, s2, h2, x,
        sa_mid, sa_out, goal_mid, goal_out,
    )[0]

    def member(c, first, second, z):
        y, x_at = (first, second) if c == 0 else (second, first)
        return ((c * 4 + y) * 4 + x_at) * n_z + z % n_z

    half = n_z // 2
    near = [
        [member(c, a, b, 2 * q + p if c == 0 or p else 2 * q + 2) for a in range(4) for p in range(2)]
        for c in range(2)
        for b in range(4)
        for q in range(half)
    ]
    far = [
        [member(c, a, b, 2 * q + p) for b in range(4) for q in range(half)]
        for c in range(2)
        for a in range(4)
        for p in range(2)
    ]
    axes = ("c", "y", "xh", "xl", "z")
    grads = lax.all_to_all(grads, axes, 0, 0, axis_index_groups=near)
    grads = call(sum_kernel, [shape((16, TILES * 8 + 16, LANES), BF)], [VMEM])(grads)[0]
    grads = lax.all_to_all(grads, axes, 0, 0, axis_index_groups=far)
    keep, send = call(
        split_kernel,
        [shape((TILES * 4 + 8, LANES), F32)] * 2,
        [SMEM, VMEM],
        scratch=[pltpu.VMEM((16, LANES), F32)],
    )(place, grads)
    recv = shifted(send, "c", 1)
    obs_a, act_a, mid_a, out_a, obs_b, mid_b, out_b = call(
        last_kernel,
        [
            shape((4, EMB), F32),
            shape((4, acts), F32),
            shape((4, HID), F32),
            shape((4, EMB), F32),
            shape((4, EMB), F32),
            shape((4, HID), F32),
            shape((4, EMB), F32),
        ],
        [SMEM] + [VMEM] * 2,
    )(place, keep, recv)
    return (loss, obs_a.T, act_a.T, mid_a, out_a, obs_b.T, mid_b, out_b)


def solution(mesh):
    fine = Mesh(mesh.devices.reshape(2, -1, 2, mesh.shape["dp"] // 2, 2), ("xh", "z", "c", "y", "xl"))
    neg = ("xh", "z", "c")
    dp = ("y", "xl")
    return jax.shard_map(
        body,
        mesh=fine,
        in_specs=(
            P(dp, neg, None),
            P(dp, neg, None),
            P(dp, neg),
            P(dp, neg),
            P(),
            P(),
            P(),
            P(),
            P(),
            P(),
            P(),
        ),
        out_specs=(
            P(dp, neg),
            P(None, neg + dp),
            P(None, neg + dp),
            P(neg + dp, None),
            P(neg + dp, None),
            P(None, neg + dp),
            P(neg + dp, None),
            P(neg + dp, None),
        ),
        check_vma=False,
    )
```
